32 devices in a mesh: dp: 16 (over z, y, x), hidden: 2 (over core).
Axes of the slice: x: 2, y: 2, z: 4, core: 2. Of those that a mesh axis runs over, the one named last changes fastest.
Arguments:
- tokens: float32 [50176, 320], P(('dp', 'hidden')), may hold values from -6 to 6
- block_kind: int32 [256], replicated, may hold values from 0 to 1
- first_gain: float32 [320], replicated, may hold values from 0.25 to 1.75
- first_bias: float32 [320], replicated, may hold values from -1.5 to 1.5
- query_weight: float32 [320, 320], replicated, may hold values from -0.3125 to 0.3125
- query_bias: float32 [320], replicated, may hold values from -1.5 to 1.5
- reduce_weight: float32 [1280, 320], replicated, may hold values from -0.15625 to 0.15625
- reduce_bias: float32 [320], replicated, may hold values from -1.5 to 1.5
- reduce_gain: float32 [320], replicated, may hold values from 0.25 to 1.75
- reduce_shift: float32 [320], replicated, may hold values from -1.5 to 1.5
- keyval_weight: float32 [320, 640], replicated, may hold values from -0.3125 to 0.3125
- value_bias: float32 [320], replicated, may hold values from -1.5 to 1.5
- output_weight: float32 [320, 320], replicated, may hold values from -0.625 to 0.625
- output_bias: float32 [320], replicated, may hold values from -1.5 to 1.5
- second_gain: float32 [320], replicated, may hold values from 0.25 to 1.75
- second_shift: float32 [320], replicated, may hold values from -1.5 to 1.5
- expand_weight: float32 [320, 1280], P(None, 'hidden'), may hold values from -0.3125 to 0.3125
- expand_bias: float32 [1280], P('hidden'), may hold values from -1.5 to 1.5
- depth_weight: float32 [9, 1280], P(None, 'hidden'), may hold values from -2 to 2
- depth_bias: float32 [1280], P('hidden'), may hold values from -1.5 to 1.5
- shrink_weight: float32 [1280, 320], P('hidden'), may hold values from -0.25 to 0.25
- shrink_bias: float32 [320], replicated, may hold values from -1.5 to 1.5
- cotangent: float32 [50176, 320], P(('dp', 'hidden')), may hold values from -6 to 6
Outputs:
- result: float32 [50176, 320], P(('dp', 'hidden'))
- tokens_grad: float32 [50176, 320], P(('dp', 'hidden'))
- grad_first_gain: float32 [320], replicated
- grad_first_bias: float32 [320], replicated
- grad_query_weight: float32 [320, 320], replicated
- grad_query_bias: float32 [320], replicated
- grad_reduce_weight: float32 [1280, 320], replicated
- grad_reduce_bias: float32 [320], replicated
- grad_reduce_gain: float32 [320], replicated
- grad_reduce_shift: float32 [320], replicated
- grad_keyval_weight: float32 [320, 640], replicated
- grad_value_bias: float32 [320], replicated
- grad_output_weight: float32 [320, 320], replicated
- grad_output_bias: float32 [320], replicated
- grad_second_gain: float32 [320], replicated
- grad_second_shift: float32 [320], replicated
- grad_expand_weight: float32 [320, 1280], P(None, 'hidden')
- grad_expand_bias: float32 [1280], P('hidden')
- grad_depth_weight: float32 [9, 1280], P(None, 'hidden')
- grad_depth_bias: float32 [1280], P('hidden')
- grad_shrink_weight: float32 [1280, 320], P('hidden')
- grad_shrink_bias: float32 [320], replicated
The draws below stay inside these ranges and needn't reach their ends.
Inputs may be any that keep to these rules, and one draw needn't show every extreme that they name: `block_kind`: 0: one 224 crop as a 14 x 14 grid; 1: 5 96 crops of 6 x 6 rows each, then empty rows.
All inputs are finite; a program needn't handle non-finite values.
Results may differ from the reference program's by a relative error of at most 0.0003.
Values sent between devices are 32-bit elements; how exact they have to be, the bound alone decides.
A program may use at most 384 MiB of HBM per device.

```python
from functools import partial
import jax
import jax.numpy as jnp
from jax import lax

D = 320
HEADS = 5
HEAD = 64
FF = 1280
BLOCK = 196
GRID = 14
SMALL = 6
SMALL_IMGS = 5
KVB = 49
BLOCKS = 256
TOKENS = 50176


def place_ends(drawn, own_key, least, top_value):
    dims = drawn.shape
    spot = [jax.random.randint(jax.random.fold_in(own_key, axis), (), 0, dims[axis]) for axis in range(len(dims))]
    drawn = drawn.at[tuple(spot)].set(least)
    longest = dims.index(max(dims))
    spot[longest] = (spot[longest] + 1) % dims[longest]
    return drawn.at[tuple(spot)].set(top_value)


def levels(own_key, extent, cuts, low, top_value):
    loudness, own = 1.0, jax.random.fold_in(own_key, 6)
    for dim, blocks in cuts:
        steps = jnp.exp(jax.random.uniform(jax.random.fold_in(own, dim), (blocks,), jnp.float32, low / len(cuts), top_value / len(cuts)))
        loudness = loudness * jnp.repeat(steps, extent[dim] // blocks).reshape([-1 if axis == dim else 1 for axis in range(len(extent))])
    return loudness


def centred(own_key, dims, scale, limit, shards=(), kind=jnp.bfloat16):
    gain = levels(own_key, dims, shards, -0.22, 0.18) if shards else 1.0
    drawn = jax.random.normal(own_key, dims, jnp.float32) * scale * gain
    return jnp.minimum(jnp.maximum(drawn, -limit), limit).astype(kind)


def setup_inputs(seed: int = 0) -> dict:
    keys = jax.random.split(jax.random.key(seed), 24)
    return {
        "tokens": centred(keys[0], (TOKENS, D), 1.0, 6.0, ((0, 32),), jnp.float32),
        "block_kind": place_ends(jax.random.randint(keys[1], (BLOCKS,), 0, 2), jax.random.fold_in(keys[1], 1), 0, 1).astype(jnp.int32),
        "first_gain": jnp.clip(1.0 + 0.15 * jax.random.normal(keys[2], (D,), jnp.float32), 0.25, 1.75),
        "first_bias": centred(keys[3], (D,), 0.3, 1.5, (), jnp.float32),
        "query_weight": centred(keys[4], (D, D), D ** -0.5, 0.3125, (), jnp.float32),
        "query_bias": centred(keys[5], (D,), 0.3, 1.5, (), jnp.float32),
        "reduce_weight": centred(keys[6], (4 * D, D), (4 * D) ** -0.5, 0.15625, (), jnp.float32),
        "reduce_bias": centred(keys[7], (D,), 0.3, 1.5, (), jnp.float32),
        "reduce_gain": jnp.clip(1.0 + 0.15 * jax.random.normal(keys[8], (D,), jnp.float32), 0.25, 1.75),
        "reduce_shift": centred(keys[9], (D,), 0.3, 1.5, (), jnp.float32),
        "keyval_weight": centred(keys[10], (D, 2 * D), D ** -0.5, 0.3125, (), jnp.float32),
        "value_bias": centred(keys[11], (D,), 0.3, 1.5, (), jnp.float32),
        "output_weight": centred(keys[12], (D, D), (D // 4) ** -0.5, 0.625, (), jnp.float32),
        "output_bias": centred(keys[13], (D,), 0.3, 1.5, (), jnp.float32),
        "second_gain": jnp.clip(1.0 + 0.15 * jax.random.normal(keys[14], (D,), jnp.float32), 0.25, 1.75),
        "second_shift": centred(keys[15], (D,), 0.3, 1.5, (), jnp.float32),
        "expand_weight": centred(keys[16], (D, FF), D ** -0.5, 0.3125, ((1, 2),), jnp.float32),
        "expand_bias": centred(keys[17], (FF,), 0.3, 1.5, ((0, 2),), jnp.float32),
        "depth_weight": centred(keys[18], (9, FF), 0.33, 2.0, ((1, 2),), jnp.float32),
        "depth_bias": centred(keys[19], (FF,), 0.3, 1.5, ((0, 2),), jnp.float32),
        "shrink_weight": centred(keys[20], (FF, D), (FF // 2) ** -0.5, 0.25, ((0, 2),), jnp.float32),
        "shrink_bias": centred(keys[21], (D,), 0.3, 1.5, (), jnp.float32),
        "cotangent": centred(keys[22], (TOKENS, D), 1.0, 6.0, ((0, 32),), jnp.float32),
    }


@jax.custom_vjp
def low(v):
    return lax.optimization_barrier(v.astype(jnp.bfloat16)).astype(jnp.float32)

@jax.custom_vjp
def low_back(v):
    return v

def low_keep(v):
    return (low(v), None)

def low_pass(kept, grad):
    return (grad,)

def back_keep(v):
    return (v, None)

def back_low(kept, grad):
    return (low(grad),)
low.defvjp(low_keep, low_pass)
low_back.defvjp(back_keep, back_low)

def layer_norm(values, norm_gain, norm_shift):
    center = lax.optimization_barrier(jnp.mean(values, -1, keepdims=True))
    centered = values - center
    spread = lax.optimization_barrier(jnp.mean(centered * centered, -1, keepdims=True))
    return centered * lax.rsqrt(spread + 1e-06) * norm_gain + norm_shift

def linear(values, weight):
    return jnp.einsum('bnc,cd->bnd', values, weight, precision=lax.Precision.HIGHEST)

def pick_rows(values, row_index):
    return jnp.take_along_axis(values, row_index[:, :, None], axis=1)

def block_tables(block_kinds):
    row_ids = jnp.arange(BLOCK, dtype=jnp.int32)
    single = (block_kinds == 0)[:, None]
    small_area = SMALL * SMALL
    image_ids = jnp.minimum(row_ids // small_area, SMALL_IMGS - 1)
    local_ids = row_ids - image_ids * small_area
    grid_side = jnp.where(single, jnp.int32(GRID), jnp.int32(SMALL))
    grid_base = jnp.where(single, jnp.int32(0), image_ids[None, :] * small_area)
    pos_row = jnp.where(single, row_ids[None, :] // GRID, local_ids[None, :] // SMALL)
    pos_col = jnp.where(single, row_ids[None, :] % GRID, local_ids[None, :] % SMALL)
    row_valid = pos_row < grid_side
    neigh_index = []
    neigh_valid = []
    for shift_row in (-1, 0, 1):
        for shift_col in (-1, 0, 1):
            near_row = pos_row + shift_row
            near_col = pos_col + shift_col
            inside = row_valid & (near_row >= 0) & (near_row < grid_side) & (near_col >= 0) & (near_col < grid_side)
            neigh_index.append(jnp.where(inside, grid_base + near_row * grid_side + near_col, row_ids[None, :]).astype(jnp.int32))
            neigh_valid.append(inside.astype(jnp.float32))
    key_ids = jnp.arange(KVB, dtype=jnp.int32)
    small_side = SMALL // 2
    small_keys = small_side * small_side
    key_image = jnp.minimum(key_ids // small_keys, SMALL_IMGS - 1)
    key_local = key_ids - key_image * small_keys
    key_live = jnp.where(single, True, (key_ids < SMALL_IMGS * small_keys)[None, :])
    key_row = jnp.where(single, key_ids[None, :] // (GRID // 2), key_local[None, :] // small_side)
    key_col = jnp.where(single, key_ids[None, :] % (GRID // 2), key_local[None, :] % small_side)
    key_base = jnp.where(single, jnp.int32(0), key_image[None, :] * small_area)
    patch_index = []
    for sub_row in (0, 1):
        for sub_col in (0, 1):
            spot = key_base + (2 * key_row + sub_row) * grid_side + 2 * key_col + sub_col
            patch_index.append(jnp.where(key_live, spot, jnp.int32(0)).astype(jnp.int32))
    same_image = (image_ids[:, None] == key_image[None, :])[None]
    allowed = jnp.where(single[:, :, None], True, same_image & key_live[:, None, :])
    row_live = row_valid.astype(jnp.float32)[:, :, None]
    return (jnp.stack(neigh_index, -1), jnp.stack(neigh_valid, -1), patch_index, allowed, row_live)

def attention_branch(tables, tokens, first_gain, first_bias, query_weight, query_bias, reduce_weight, reduce_bias, reduce_gain, reduce_shift, keyval_weight, value_bias, output_weight, output_bias):
    patch_index, allowed, row_live = tables
    normed = layer_norm(tokens, first_gain, first_bias)
    query = linear(normed, query_weight) + query_bias
    patches = jnp.concatenate([pick_rows(normed, spots) for spots in patch_index], -1)
    reduced = layer_norm(linear(patches, reduce_weight) + reduce_bias, reduce_gain, reduce_shift)
    keyval = linear(reduced, keyval_weight)
    model_width = query.shape[-1]
    blocks = query.shape[0]
    key_heads = keyval[..., :model_width].reshape(blocks, KVB, HEADS, HEAD)
    value_heads = (keyval[..., model_width:] + value_bias).reshape(blocks, KVB, HEADS, HEAD)
    query_heads = query.reshape(blocks, BLOCK, HEADS, HEAD)
    scores = jnp.einsum('bqhd,bkhd->bhqk', query_heads, key_heads, precision=lax.Precision.HIGHEST) * HEAD ** (-0.5)
    scores = jnp.where(allowed[:, None], scores, -1e+30)
    weights = jax.nn.softmax(scores, axis=-1)
    mixed_heads = jnp.einsum('bhqk,bkhd->bqhd', weights, value_heads, precision=lax.Precision.HIGHEST).reshape(blocks, BLOCK, model_width)
    return tokens + row_live * (linear(mixed_heads, output_weight) + output_bias)

def feed_forward(tables, normed, expand_weight, expand_bias, depth_weight, depth_bias, shrink_weight):
    neigh_index, neigh_valid = tables
    hidden = linear(normed, expand_weight) + expand_bias
    summed = depth_bias + jnp.zeros_like(hidden)
    for tap in range(9):
        summed = summed + pick_rows(hidden, neigh_index[:, :, tap]) * neigh_valid[:, :, tap, None] * depth_weight[tap]
    active = jax.nn.gelu(summed, approximate=False)
    return linear(active, shrink_weight)

def whole_layer(block_kinds, tokens, first_gain, first_bias, query_weight, query_bias, reduce_weight, reduce_bias, reduce_gain, reduce_shift, keyval_weight, value_bias, output_weight, output_bias, second_gain, second_shift, expand_weight, expand_bias, depth_weight, depth_bias, shrink_weight, shrink_bias):
    neigh_index, neigh_valid, patch_index, allowed, row_live = block_tables(block_kinds)
    after_attn = attention_branch((patch_index, allowed, row_live), tokens, first_gain, first_bias, query_weight, query_bias, reduce_weight, reduce_bias, reduce_gain, reduce_shift, keyval_weight, value_bias, output_weight, output_bias)
    second = layer_norm(after_attn, second_gain, second_shift)
    branch = feed_forward((neigh_index, neigh_valid), second, expand_weight, expand_bias, depth_weight, depth_bias, shrink_weight)
    return after_attn + row_live * (branch + shrink_bias)

def reference(tokens, block_kind, first_gain, first_bias, query_weight, query_bias, reduce_weight, reduce_bias, reduce_gain, reduce_shift, keyval_weight, value_bias, output_weight, output_bias, second_gain, second_shift, expand_weight, expand_bias, depth_weight, depth_bias, shrink_weight, shrink_bias, cotangent):
    block_count = block_kind.shape[0]
    layer_fn = partial(whole_layer, block_kind)
    result, layer_back = jax.vjp(layer_fn, tokens.reshape(block_count, BLOCK, tokens.shape[1]), first_gain, first_bias, query_weight, query_bias, reduce_weight, reduce_bias, reduce_gain, reduce_shift, keyval_weight, value_bias, output_weight, output_bias, second_gain, second_shift, expand_weight, expand_bias, depth_weight, depth_bias, shrink_weight, shrink_bias)
    gradients = layer_back(cotangent.reshape(result.shape))
    return (result.reshape(tokens.shape), gradients[0].reshape(tokens.shape), gradients[1], gradients[2], gradients[3], gradients[4], gradients[5], gradients[6], gradients[7], gradients[8], gradients[9], gradients[10], gradients[11], gradients[12], gradients[13], gradients[14], gradients[15], gradients[16], gradients[17], gradients[18], gradients[19], gradients[20])
```

```python
from functools import partial

import jax
import jax.numpy as jnp
import numpy as np
from jax import lax
from jax.experimental import pallas as pl
from jax.experimental.pallas import tpu as pltpu
from jax.sharding import PartitionSpec as P

HEADS = 5
HEAD = 64
BLOCK = 196
GRID = 14
SMALL = 6
SMALL_IMGS = 5
KVB = 49
D = 320
FF = 1280
KPAD = 56
WIN = 208
ODD = 184
CHUNK = 256
CHUNKS = FF // CHUNK
SLAB = 224
HALF = 112
PAD = 16
MIB = 1024 * 1024

f32 = jnp.float32
bf16 = jnp.bfloat16
MESH = pl.DeviceIdType.MESH


def gather_table():
    out = np.zeros((2, 2, 4 * KPAD, WIN), np.float32)
    for kind in range(2):
        for parity in range(2):
            off = 12 * parity
            for a in range(2):
                for b in range(2):
                    for key in range(KVB):
                        if kind == 0:
                            i, j = divmod(key, GRID // 2)
                            spot = (2 * i + a) * GRID + 2 * j + b
                        else:
                            if key >= 45:
                                continue
                            image, rest = divmod(key, 9)
                            i, j = divmod(rest, 3)
                            spot = image * 36 + (2 * i + a) * SMALL + 2 * j + b
                        out[kind, parity, (2 * a + b) * KPAD + key, off + spot] = 1.0
    return out.reshape(4, 4 * KPAD, WIN)


def score_table():
    out = np.full((2, 2, WIN, 256), -1e30, np.float32)
    for kind in range(2):
        for parity in range(2):
            off = 12 * parity
            for row in range(WIN):
                local = row - off
                for key in range(KVB):
                    if kind == 0 or local < 0 or local >= BLOCK:
                        good = True
                    else:
                        good = key < 45 and key // 9 == min(local // 36, 4)
                    if good:
                        for head in range(HEADS):
                            out[kind, parity, row, head * KVB + key] = 0.0
    return out.reshape(4, WIN, 256)


def row_table():
    out = np.zeros((2, 2, WIN, 128), np.float32)
    for parity in range(2):
        off = 12 * parity
        for row in range(BLOCK):
            i, j = divmod(row, GRID)
            out[0, parity, off + row, :7] = (1, j > 0, j < 13, i > 0, 0, i < 13, 0)
            if row < 180:
                i, j = divmod(row % 36, SMALL)
                out[1, parity, off + row, :7] = (1, j > 0, j < 5, 0, i > 0, 0, i < 5)
    return out.reshape(4, WIN, 128)


def split(x):
    high = x.astype(bf16)
    return high, (x - high.astype(f32)).astype(bf16)


def pack_left(x):
    high = x.astype(bf16).astype(f32)
    low = x - high
    tail = jnp.concatenate([high[:, 256:], low[:, 256:]], 1).astype(bf16)
    high, low = high[:, :256].astype(bf16), low[:, :256].astype(bf16)
    return jnp.concatenate([high, low, high, tail, tail], 1)


def pack_short(x):
    high = x.astype(bf16).astype(f32)
    low = x - high
    tail = jnp.concatenate([high[:, 256:], low[:, 256:]], 1).astype(bf16)
    return jnp.concatenate([high[:, :256].astype(bf16), low[:, :256].astype(bf16), tail], 1)


def pack_lane(w):
    high = w.astype(bf16).astype(f32)
    low = w - high
    tail_high = jnp.concatenate([high[:, 256:], high[:, 256:]], 1).astype(bf16)
    tail_low = jnp.concatenate([low[:, 256:], low[:, 256:]], 1).astype(bf16)
    high, low = high[:, :256].astype(bf16), low[:, :256].astype(bf16)
    return jnp.concatenate([high, high, low, tail_high, tail_low], 1)


def pack_down(w):
    high, low = split(w)
    return jnp.concatenate(
        [high[:256], high[:256], low[:256], high[256:], high[256:], low[256:], low[256:]], 0
    )


def triple_left(x):
    high, low = split(x)
    return jnp.concatenate([high, low, high], 1)


def triple_down(w):
    high, low = split(w)
    return jnp.concatenate([high, high, low], 0)


def triple_lane(w):
    high, low = split(w)
    return jnp.concatenate([high, high, low], 1)


def mm(a, b):
    return jnp.dot(a, b, preferred_element_type=f32)


def mm_lane(a, b):
    return lax.dot_general(a, b, (((1,), (1,)), ((), ())), preferred_element_type=f32)


def mm_rows(a, b):
    left_high, left_low = split(a.T)
    high, low = split(b)
    return mm(left_high, high) + mm(left_low, high) + mm(left_high, low)


def norm_rows(x):
    center = jnp.sum(x, -1, keepdims=True) * (1.0 / D)
    centered = x - center
    spread = jnp.sum(centered * centered, -1, keepdims=True) * (1.0 / D)
    scale = lax.rsqrt(spread + 1e-06)
    return centered * scale, scale


def norm_back(h, n, scale):
    mean_h = jnp.sum(h, -1, keepdims=True) * (1.0 / D)
    mean_hn = jnp.sum(h * n, -1, keepdims=True) * (1.0 / D)
    return scale * (h - mean_h - n * mean_hn)


def fold(x):
    return jnp.sum(x.reshape(x.shape[0] // 8, 8, x.shape[1]), 0)


def window(block):
    return pl.multiple_of((block // 2) * (2 * BLOCK) + (block % 2) * ODD, 8)


def slab(w):
    return pl.ds(pl.multiple_of(w * SLAB, SLAB), SLAB)


def place_window(ref, block, value):
    start = window(block)

    @pl.when(block % 2 == 0)
    def _():
        ref[pl.ds(start, WIN), :] = value

    @pl.when(block % 2 == 1)
    def _():
        edge = ref[pl.ds(start + 8, 8), :]
        rows = lax.broadcasted_iota(jnp.int32, edge.shape, 0)
        ref[pl.ds(start + 8, 8), :] = jnp.where(rows < 4, edge, value[8:16])
        ref[pl.ds(start + 16, WIN - 16), :] = value[16:]


def head_block(rows_ref, block, out_ref):
    start = pl.multiple_of(block * KPAD, 8)
    for head in range(HEADS):
        tile = head // 2
        if tile < 2:
            value = rows_ref[pl.ds(start, KPAD), tile * 128 : tile * 128 + 128]
            lane = lax.broadcasted_iota(jnp.int32, value.shape, 1)
            value = jnp.where((lane >= 64) == (head % 2 == 1), value, 0.0)
        else:
            half = rows_ref[pl.ds(start, KPAD), 256:320]
            value = jnp.concatenate([half, half], 1)
        out_ref[tile, head * KVB : head * KVB + KVB, :] = value[:KVB]


def head_rows(ref):
    return jnp.concatenate([ref[0], ref[1], ref[2][:, :64]], 1)


def head_unblock(ref, value):
    ref[0] = value[:, :128]
    ref[1] = value[:, 128:256]
    ref[2] = jnp.concatenate([value[:, 256:], value[:, 256:]], 1)
    lane = lax.broadcasted_iota(jnp.int32, (KPAD, 128), 1)
    row = lax.broadcasted_iota(jnp.int32, (KPAD, 128), 0)
    tiles = []
    for tile in range(3):
        first = ref[tile, 2 * tile * KVB : 2 * tile * KVB + KPAD, :]
        if tile < 2:
            second = ref[tile, (2 * tile + 1) * KVB : (2 * tile + 1) * KVB + KPAD, :]
            first = jnp.where(lane < 64, first, second)
        tiles.append(jnp.where(row < KVB, first, 0.0))
    return jnp.concatenate([tiles[0], tiles[1], tiles[2][:, :64]], 1)


def head_lane(ref):
    parts = []
    for tile in range(3):
        high = ref[tile].astype(bf16)
        parts.append((high, (ref[tile] - high.astype(f32)).astype(bf16)))
    return jnp.concatenate(
        [parts[0][0], parts[1][0], parts[0][0], parts[1][0], parts[0][1], parts[1][1], parts[2][0], parts[2][1]], 1
    )


def head_of_lane(shape):
    lane = lax.broadcasted_iota(jnp.int32, shape, 1)
    return [lane < (head + 1) * KVB for head in range(HEADS - 1)]


def by_head(below, values):
    out = values[HEADS - 1]
    for head in range(HEADS - 2, -1, -1):
        out = jnp.where(below[head], values[head], out)
    return out


def per_head(below, x, empty, reduce):
    out = []
    for head in range(HEADS):
        here = x
        if head < HEADS - 1:
            here = jnp.where(below[head], here, empty)
        if head > 0:
            here = jnp.where(below[head - 1], empty, here)
        out.append(reduce(here, axis=1, keepdims=True))
    return by_head(below, [jnp.broadcast_to(v, x.shape) for v in out])


def line(ref):
    return ref[...].reshape(1, -1)


def own_first(blocks):
    return (lax.axis_index("dp") * lax.axis_size("hidden") + lax.axis_index("hidden")) * blocks


def attention_kernel(
    kinds,
    tokens_t,
    table,
    scores_mask,
    row_marks,
    first_gain,
    first_bias,
    query_bias,
    reduce_bias,
    reduce_gain,
    reduce_shift,
    value_bias,
    output_bias,
    wq,
    wr,
    wkv,
    wo,
    after,
    marks,
    first_n,
    query,
    attended,
    probs,
    keys,
    values,
    red_n,
    patches,
    wq_s,
    wo_s,
    wk_s,
    wv_s,
    wr_s,
    tokens,
    normed,
    kb,
    vb,
):
    blocks = probs.shape[0]
    slabs = tokens.shape[0] // SLAB
    first = own_first(blocks)
    g1, b1, bq, br = line(first_gain), line(first_bias), line(query_bias), line(reduce_bias)
    gr, sr, bv, bo = line(reduce_gain), line(reduce_shift), line(value_bias), line(output_bias)
    wq_s[...] = pack_down(wq[...])
    wo_s[...] = pack_down(wo[...])
    wk_s[...] = pack_down(wkv[:, :D])
    wv_s[...] = pack_down(wkv[:, D:])
    for sub in range(4):
        wr_s[sub] = pack_lane(wr[:, sub * D : sub * D + D])
    kb[...] = jnp.zeros_like(kb)
    vb[...] = jnp.zeros_like(vb)
    tokens[...] = tokens_t[...].T

    @pl.loop(0, slabs)
    def _(w):
        n, scale = norm_rows(tokens[slab(w), :])
        first_n[slab(w), :] = jnp.concatenate([n, jnp.broadcast_to(scale, (SLAB, 64))], 1)
        n = n * g1 + b1
        normed[slab(w), :] = n
        query[slab(w), :] = mm(pack_left(n), wq_s[...]) + bq

    @pl.loop(0, blocks)
    def _(b):
        which = kinds[first + b] * 2 + b % 2
        place_window(marks, b, row_marks[which])
        part = normed[pl.ds(window(b), WIN), :]
        high, low = split(part)
        pick = table[which]
        got = mm(pick, high) + mm(pick, low)
        rows = pl.ds(pl.multiple_of(b * KPAD, 8), KPAD)
        for sub in range(4):
            patches[sub, rows, :] = got[sub * KPAD : sub * KPAD + KPAD]

    @pl.loop(0, blocks * KPAD // SLAB)
    def _(w):
        acc = br + mm_lane(pack_left(patches[0, slab(w), :]), wr_s[0])
        for sub in range(1, 4):
            acc = acc + mm_lane(pack_left(patches[sub, slab(w), :]), wr_s[sub])
        n, scale = norm_rows(acc)
        red_n[slab(w), :] = jnp.concatenate([n, jnp.broadcast_to(scale, (SLAB, 64))], 1)
        packed = pack_left(n * gr + sr)
        keys[slab(w), :] = mm(packed, wk_s[...])
        values[slab(w), :] = mm(packed, wv_s[...]) + bv

    @pl.loop(0, blocks)
    def _(b):
        which = kinds[first + b] * 2 + b % 2
        head_block(keys, b, kb)
        head_block(values, b, vb)
        q = query[pl.ds(window(b), WIN), :]
        s = mm_lane(pack_left(q), head_lane(kb)) * (HEAD**-0.5) + scores_mask[which]
        below = head_of_lane(s.shape)
        e = jnp.exp(s - per_head(below, s, -3e38, jnp.max))
        p = e / per_head(below, e, 0.0, jnp.sum)
        probs[b] = p
        out = mm(triple_left(p), triple_down(head_rows(vb)))
        place_window(attended, b, out)

    @pl.loop(0, slabs)
    def _(w):
        branch = mm(pack_left(attended[slab(w), :]), wo_s[...]) + bo
        after[slab(w), :] = tokens[slab(w), :] + marks[slab(w), 0:1] * branch


def attention_forward(kinds, tokens_t, vecs, wq, wr, wkv, wo):
    rows = tokens_t.shape[1]
    blocks = rows // BLOCK
    krows = blocks * KPAD
    vm = pl.BlockSpec(memory_space=pltpu.VMEM)

    def shape(*dims):
        return jax.ShapeDtypeStruct(dims, f32)

    return pl.pallas_call(
        attention_kernel,
        out_shape=(
            shape(rows, D),
            shape(rows, 128),
            shape(rows, D + 64),
            shape(rows, D),
            shape(rows, D),
            shape(blocks, WIN, 256),
            shape(krows, D),
            shape(krows, D),
            shape(krows, D + 64),
            shape(4, krows, D),
        ),
        in_specs=[pl.BlockSpec(memory_space=pltpu.SMEM)] + [vm] * 16,
        out_specs=(vm,) * 10,
        scratch_shapes=[
            pltpu.VMEM((1024, D), bf16),
            pltpu.VMEM((1024, D), bf16),
            pltpu.VMEM((1024, D), bf16),
            pltpu.VMEM((1024, D), bf16),
            pltpu.VMEM((4, D, 1024), bf16),
            pltpu.VMEM((rows, D), f32),
            pltpu.VMEM((rows, D), f32),
            pltpu.VMEM((3, 256, 128), f32),
            pltpu.VMEM((3, 256, 128), f32),
        ],
        compiler_params=pltpu.CompilerParams(vmem_limit_bytes=60 * MIB),
        name="attention",
    )(
        kinds,
        tokens_t,
        jnp.asarray(gather_table(), bf16),
        jnp.asarray(score_table()),
        jnp.asarray(row_table()),
        *vecs,
        wq,
        wr,
        wkv,
        wo,
    )


ERF_P = 0.3275911
ERF = (0.254829592, -0.284496736, 1.421413741, -1.453152027, 1.061405429)


def gelu_pair(x):
    size = jnp.abs(x)
    d = 1.0 + (ERF_P * 0.7071067811865476) * size
    t = pl.reciprocal(d, approx=True)
    t = t * (2.0 - d * t)
    e = jnp.exp(-0.5 * (x * x))
    poly = t * (ERF[0] + t * (ERF[1] + t * (ERF[2] + t * (ERF[3] + t * ERF[4]))))
    tail = 0.5 * (poly * e)
    phi = jnp.where(x < 0.0, tail, 1.0 - tail)
    return x * phi, phi + x * (0.3989422804014327 * e)


TOP = 64
STEP = 16


def forward_kernel(
    after,
    cot_t,
    marks,
    second_gain,
    second_shift,
    shrink_bias,
    own_we,
    own_ws,
    own_taps,
    result_t,
    g_after,
    pack,
    sums,
    we_s,
    we_l,
    ws_s,
    ws_l,
    result,
    g_second,
    masks,
    taps,
    second,
    branch,
    second_t,
    branch_t,
    xs0,
    xs1,
    ga0,
    ga1,
    y0,
    ym,
    yp,
    act0,
    act1,
    gx0,
    gx1,
    dwe,
    dws,
    dw,
    sem,
):
    rows = after.shape[0]
    part = rows // 2
    ends = xs0.shape[1]
    per = FF // 128 // own_we.shape[0]
    xs, ga, act, gx = (xs0, xs1), (ga0, ga1), (act0, act1), (gx0, gx1)

    g2, s2, bs = line(second_gain), line(second_shift), line(shrink_bias)
    loads = []
    for tile in range(FF // 128):
        lanes = pl.ds((tile % per) * 128, 128)
        for i, (source, low, size) in enumerate(((own_we, 0, D), (own_ws, D, D), (own_taps, 2 * D, 16))):
            loads.append(
                pltpu.make_async_copy(
                    source.at[tile // per, :, lanes], pack.at[tile, pl.ds(low, size)], sem.at[3 * tile + i]
                )
            )
    for load in loads:
        load.start()

    for ref in (xs0, xs1, ga0, ga1, y0, ym, yp, masks.at[0], masks.at[1]):
        for t in range(ref.shape[0]):
            ref[t, 0:TOP, :] = jnp.zeros((TOP, 128), f32)
            ref[t, TOP + part : ends, :] = jnp.zeros((ends - TOP - part, 128), f32)
    act1[...] = jnp.zeros_like(act1)
    gx1[...] = jnp.zeros_like(gx1)
    sums[...] = jnp.zeros_like(sums)
    g_after[...] = cot_t[...].T

    for h in range(2):

        @pl.loop(0, part // HALF)
        def _(w):
            here = pl.ds(pl.multiple_of(h * part + w * HALF, 16), HALF)
            lower = pl.ds(pl.multiple_of(TOP + w * HALF, 16), HALF)
            n, _ = norm_rows(after[here, :])
            value = n * g2 + s2
            for k in range(1, 7):
                masks[h, k - 1, lower, :] = jnp.broadcast_to(marks[here, k : k + 1], (HALF, 128))
            grad = marks[here, 0:1] * g_after[here, :]
            sums[2] += fold(grad)
            second[here, :] = pack_short(value)
            branch[here, :] = pack_short(grad)
            g_second[here, :] = value
            result[here, :] = grad

        for source, turned in ((g_second, second_t), (result, branch_t)):
            high, low = split(source[h * part : (h + 1) * part, :].T)
            turned[h] = jnp.concatenate([high, low, high], 1)
    result[...] = jnp.zeros_like(result)
    g_second[...] = jnp.zeros_like(g_second)

    for load in loads:
        load.wait()
    for c in range(CHUNKS):
        for which, (down, lane) in enumerate(((we_s, we_l), (ws_s, ws_l))):
            value = jnp.concatenate([pack[2 * c + t, which * D : which * D + D, :] for t in range(2)], 1)
            high, low = split(value)
            down[c] = jnp.concatenate([high, low], 0)
            lane[c] = jnp.concatenate([high, low], 1)
        for t in range(2):
            for k in range(11):
                taps[c, t, k] = jnp.broadcast_to(pack[2 * c + t, 2 * D + k : 2 * D + k + 1, :], (8, 128))

    inner = slice(TOP, TOP + part)

    def own(h):
        return slice(h * part, (h + 1) * part)

    def left(ref, h):
        x = ref[own(h), :]
        return jnp.concatenate([x[:, :512], x[:, :256], x[:, 512:], x[:, 512:]], 1)

    def deep(ref, c):
        x = ref[c]
        return jnp.concatenate(
            [x[:256], x[:256], x[D : D + 256], x[256:D], x[256:D], x[D + 256 :], x[D + 256 :]], 0
        )

    def expand_task(c, h):
        e = mm(left(second, h), deep(we_s, c))
        for t in range(2):
            xs[h][t, inner, :] = e[:, 128 * t : 128 * t + 128] + taps[c, t, 9][0:1]

    def active_grad_task(c, h):
        g = mm(left(branch, h), deep(ws_s, c))
        for t in range(2):
            ga[h][t, inner, :] = g[:, 128 * t : 128 * t + 128]

    def out_task(c, h, source, lane, out):
        x = source[h][inner, :]
        weight = lane[c]
        out[own(h), :] += mm_lane(
            jnp.concatenate([x, x[:, :256]], 1), jnp.concatenate([weight[:, :256], weight], 1)
        )

    def weight_task(c, h, source, turned, total, row):
        x = source[h][inner, :]
        high, low = x[:, :256], x[:, 256:]
        value = mm(turned[h], jnp.concatenate([high, high, low], 0))
        if h == 0:
            total[...] = value
        else:
            value = value + total[...]
            for t in range(2):
                pack[2 * c + t, row : row + D, :] = value[:, 128 * t : 128 * t + 128]

    def early_tasks(c, h):
        return [partial(expand_task, c, h), partial(active_grad_task, c, h)]

    def late_tasks(c, h):
        return [
            partial(out_task, c, h, act, ws_l, result),
            partial(weight_task, c, h, act, branch_t, dws, D),
            partial(out_task, c, h, gx, we_l, g_second),
            partial(weight_task, c, h, gx, second_t, dwe, 0),
        ]

    def near(ref, t, base, shift=0):
        at = base + TOP + shift
        return ref[t, at : at + STEP, :].reshape(STEP // 8, 8, 128)

    def put(ref, t, base, value):
        ref[t, base + TOP : base + TOP + STEP, :] = value.reshape(STEP, 128)

    def put_split(ref, t, base, value):
        high, low = split(value.reshape(STEP, 128))
        here = slice(base + TOP, base + TOP + STEP)
        ref[here, 128 * t : 128 * t + 128] = high
        ref[here, 256 + 128 * t : 384 + 128 * t] = low

    def item(c, h, tasks):
        m = masks.at[h]
        x, g = xs[h], ga[h]

        def columns(t, base):
            return (
                near(m, 0, base) * near(x, t, base, -1),
                near(x, t, base),
                near(m, 1, base) * near(x, t, base, 1),
            )

        def mix(t, values, ks):
            a, b, d = (v * taps[c, t, k] for v, k in zip(values, ks))
            return a + b + d

        def rows_step(t, base):
            cols = columns(t, base)
            put(ym, t, base, mix(t, cols, (0, 1, 2)))
            put(y0, t, base, mix(t, cols, (3, 4, 5)) + taps[c, t, 10])
            put(yp, t, base, mix(t, cols, (6, 7, 8)))

        def gelu_step(t, base):
            conv = (
                near(y0, t, base)
                + near(m, 2, base) * near(ym, t, base, -14)
                + near(m, 3, base) * near(ym, t, base, -6)
                + near(m, 4, base) * near(yp, t, base, 14)
                + near(m, 5, base) * near(yp, t, base, 6)
            )
            active, slope = gelu_pair(conv)
            put_split(act[h], t, base, active)
            put(g, t, base, near(g, t, base) * slope)

        def back_step(t, base, totals):
            down = near(m, 2, base) * near(g, t, base, -14) + near(m, 3, base) * near(g, t, base, -6)
            same = near(g, t, base)
            up = near(m, 4, base) * near(g, t, base, 14) + near(m, 5, base) * near(g, t, base, 6)
            cols = columns(t, base)
            moved = (up, same, down)
            totals[10] = totals[10] + jnp.sum(same, 0)
            for p in range(3):
                for q in range(3):
                    totals[3 * p + q] = totals[3 * p + q] + jnp.sum(moved[p] * cols[q], 0)
            put(ym, t, base, mix(t, moved, (0, 3, 6)))
            put(y0, t, base, mix(t, moved, (1, 4, 7)))
            put(yp, t, base, mix(t, moved, (2, 5, 8)))

        def last_step(t, base, totals):
            value = (
                near(y0, t, base) + near(m, 0, base) * near(yp, t, base, -1) + near(m, 1, base) * near(ym, t, base, 1)
            )
            put_split(gx[h], t, base, value)
            totals[9] = totals[9] + jnp.sum(value, 0)

        steps = part // STEP
        slots = {round((i + 0.5) * 2 * steps / max(len(tasks), 1)): task for i, task in enumerate(tasks)}
        for t in range(2):
            totals = [jnp.zeros((8, 128), f32)] * 11
            for k in range(steps + 3):
                base = k * STEP
                if k < steps:
                    rows_step(t, base)
                if 1 <= k < steps + 1:
                    gelu_step(t, base - STEP)
                if 2 <= k < steps + 2:
                    back_step(t, base - 2 * STEP, totals)
                if 3 <= k:
                    last_step(t, base - 3 * STEP, totals)
                if k < steps and t * steps + k in slots:
                    slots[t * steps + k]()
            for k in range(11):
                if h == 0:
                    dw[t, k] = totals[k]
                else:
                    pack[2 * c + t, 2 * D + k : 2 * D + k + 1, :] = jnp.sum(dw[t, k] + totals[k], 0, keepdims=True)

    for task in early_tasks(0, 0):
        task()

    @pl.loop(0, CHUNKS)
    def _(c):
        item(c, 0, early_tasks(c, 1) + late_tasks(jnp.maximum(c - 1, 0), 1))
        item(c, 1, early_tasks(jnp.minimum(c + 1, CHUNKS - 1), 0) + late_tasks(c, 0))

    for task in late_tasks(CHUNKS - 1, 1):
        task()
    for c in range(CHUNKS):
        for t in range(2):
            pack[2 * c + t, 2 * D + 11 : 2 * D + 16, :] = jnp.zeros((5, 128), f32)

    @pl.loop(0, rows // SLAB)
    def _(w):
        a = after[slab(w), :]
        live = marks[slab(w), 0:1]
        result[slab(w), :] = a + live * (result[slab(w), :] + bs)
        n, scale = norm_rows(a)
        g = g_second[slab(w), :]
        sums[0] += fold(g * n)
        sums[1] += fold(g)
        g_after[slab(w), :] = g_after[slab(w), :] + norm_back(g * g2, n, scale)

    result_t[...] = result[...].T


def feed_forward(after, cot_t, marks, vecs, weights):
    rows = after.shape[0]
    vm = pl.BlockSpec(memory_space=pltpu.VMEM)
    part = rows // 2
    ends = 2 * TOP + part
    padded = pltpu.VMEM((2, ends, 128), f32)
    half = pltpu.VMEM((ends, 2 * CHUNK), bf16)
    return pl.pallas_call(
        forward_kernel,
        out_shape=(
            jax.ShapeDtypeStruct((D, rows), f32),
            jax.ShapeDtypeStruct((rows, D), f32),
            jax.ShapeDtypeStruct((2 * CHUNKS, 2 * D + 16, 128), f32),
            jax.ShapeDtypeStruct((3, 8, D), f32),
        ),
        in_specs=[vm] * 6 + [pl.BlockSpec(memory_space=pl.ANY)] * 3,
        out_specs=(vm,) * 4,
        scratch_shapes=[
            pltpu.VMEM((CHUNKS, 2 * D, CHUNK), bf16),
            pltpu.VMEM((CHUNKS, D, 2 * CHUNK), bf16),
            pltpu.VMEM((CHUNKS, 2 * D, CHUNK), bf16),
            pltpu.VMEM((CHUNKS, D, 2 * CHUNK), bf16),
            pltpu.VMEM((rows, D), f32),
            pltpu.VMEM((rows, D), f32),
            pltpu.VMEM((2, 6, ends, 128), f32),
            pltpu.VMEM((CHUNKS, 2, 11, 8, 128), f32),
            pltpu.VMEM((rows, 640), bf16),
            pltpu.VMEM((rows, 640), bf16),
            pltpu.VMEM((2, D, 3 * part), bf16),
            pltpu.VMEM((2, D, 3 * part), bf16),
            padded,
            padded,
            padded,
            padded,
            padded,
            padded,
            padded,
            half,
            half,
            half,
            half,
            pltpu.VMEM((D, CHUNK), f32),
            pltpu.VMEM((D, CHUNK), f32),
            pltpu.VMEM((2, 11, 8, 128), f32),
            pltpu.SemaphoreType.DMA((6 * CHUNKS,)),
        ],
        compiler_params=pltpu.CompilerParams(vmem_limit_bytes=63 * MIB),
        name="feed_forward",
    )(after, cot_t, marks, *vecs, *weights)


class Wires:
    def __init__(self, pairs, cores, send, recv):
        self.bits = pairs.bit_length() - 1
        self.cores = cores
        self.me, self.core = lax.axis_index("dp"), lax.axis_index("hidden")
        self.other = cores - 1 - self.core
        self.send, self.recv, self.used = send, recv, 0

    def groups(self):
        rest = list(range(2, self.bits))
        return [(k,) for k in range(min(2, self.bits))] + [tuple(rest[i : i + 2]) for i in range(0, len(rest), 2)]

    def bit(self, k):
        return (self.me // (1 << k)) % 2

    def peer(self, group, j):
        flips = [(1 - 2 * self.bit(k)) * (1 << k) for i, k in enumerate(group) if (j >> i) & 1]
        return (sum(flips, self.me), self.core)

    def place(self, group, j):
        bits = [(1 - self.bit(k) if (j >> i) & 1 else self.bit(k)) * (1 << i) for i, k in enumerate(group)]
        return sum(bits[1:], bits[0])

    def greet(self):
        peers = [self.peer(group, j) for group in self.groups() for j in range(1, 1 << len(group))]
        if self.cores > 1:
            peers.append((self.me, self.other))
        if not peers:
            return
        barrier = pltpu.get_barrier_semaphore()
        for target in peers:
            pl.semaphore_signal(barrier, inc=1, device_id=target, device_id_type=MESH)
        pl.semaphore_wait(barrier, len(peers))

    def copy(self, src, dst, target):
        slot = self.used
        self.used += 1
        return pltpu.make_async_remote_copy(
            src_ref=src,
            dst_ref=dst,
            send_sem=self.send.at[slot],
            recv_sem=self.recv.at[slot],
            device_id=target,
            device_id_type=MESH,
        )

    def local(self, src, dst):
        slot = self.used
        self.used += 1
        return pltpu.make_async_copy(src, dst, self.send.at[slot])

    def sibling(self, src, dst):
        return self.copy(src, dst, (self.me, self.other))


def rows_of(start, size):
    return pl.ds(pl.multiple_of(start, 8), size)


class Chain:
    def __init__(self, wires, acc, near, got, full, base, rows, order, opening, closing, wait=0):
        self.stages, self.next = [], -wait
        whole = pl.ds(base, rows)

        def meet():
            if near is not None:
                acc[whole, :] = acc[whole, :] + near[whole, :]

        start, size, spot = base + 0 * wires.me, rows, base
        pending, action = opening, meet
        self.stages.append(([], None, opening))
        held = []
        for group in order:
            many = 1 << len(group)
            size //= many
            keep = start + wires.place(group, 0) * size
            copies, lands = [], []
            for j in range(1, many):
                land = pl.ds(spot, size)
                spot += size
                give = start + wires.place(group, j) * size
                copies.append(wires.copy(acc.at[rows_of(give, size)], got.at[land], wires.peer(group, j)))
                lands.append(land)
            self.stages.append((pending, action, copies))

            def add(keep=keep, lands=lands, size=size):
                value = acc[rows_of(keep, size), :]
                for land in lands:
                    value = value + got[land, :]
                acc[rows_of(keep, size), :] = value

            pending, action = copies, add
            held.append((group, start))
            start = keep
        last, last_start, last_size = action, start, size

        def settle():
            last()
            full[rows_of(last_start, last_size), :] = acc[rows_of(last_start, last_size), :]

        action = settle
        for group, before in reversed(held):
            mine = rows_of(start, size)
            many = 1 << len(group)
            copies = [wires.copy(full.at[mine], full.at[mine], wires.peer(group, j)) for j in range(1, many)]
            self.stages.append((pending, action, copies))
            pending, action = copies, None
            start, size = before, size * many
        if closing:
            self.stages.append((pending, action, closing))
            pending, action = closing, None
        self.stages.append((pending, action, []))

    def run(self, stage):
        if stage < 0 or stage >= len(self.stages):
            return
        waits, action, starts = self.stages[stage]
        for c in waits:
            c.wait()
        if action is not None:
            action()
        for c in starts:
            c.start()

    def step(self):
        self.run(self.next)
        self.next += 1
        return self.next < len(self.stages)


def step_all(chains):
    return [c.step() for c in chains]


def drain(chains):
    while any(step_all(chains)):
        pass


def axis_orders(groups):
    return groups, groups[1::-1] + groups[2:], groups[2:] + groups[:2]


def cut(total, unit, parts):
    units = total // unit
    marks = sorted({0, units} | {round(units * x) for x in parts})
    return [(a * unit, b * unit) for a, b in zip(marks, marks[1:])]


def round_up(x, unit):
    return -(-x // unit) * unit


def sum_rows(pairs, cores):
    unit = 8 * pairs
    ff = round_up(2 * CHUNKS // cores * (2 * D + 16), unit)
    rest = round_up(20 * (D // cores), unit)
    return ff, rest


def backward_kernel(
    pairs,
    cores,
    kinds,
    first_n,
    g_after,
    marks,
    table,
    first_gain,
    first_bias,
    reduce_gain,
    reduce_shift,
    wq,
    wr,
    wkv,
    wo,
    query,
    attended,
    probs,
    keys,
    values,
    red_n,
    patches,
    sums,
    ff_pack,
    grad,
    ff_full,
    full,
    small,
    wq_l,
    wo_l,
    wk_l,
    wv_l,
    wr_l,
    g_att,
    g_query,
    g_keys,
    g_values,
    g_patch,
    g_scores,
    kb,
    vb,
    tmp,
    acc,
    ff_acc,
    ff_near,
    ff_got,
    big,
    near,
    got,
    small_sum,
    small_got,
    send,
    recv,
):
    blocks = probs.shape[0]
    rows = g_after.shape[0]
    slabs = rows // SLAB
    krows = blocks * KPAD
    first = own_first(blocks)
    part = D // cores
    g1, b1, gr, sr = line(first_gain), line(first_bias), line(reduce_gain), line(reduce_shift)

    wires = Wires(pairs, cores, send, recv)
    core = wires.core
    orders = axis_orders(wires.groups())
    unit = 8 * pairs
    ff_real = ff_pack.shape[0] // cores
    ff_total, total = ff_acc.shape[0], big.shape[1]
    if ff_total > ff_real:
        ff_acc[ff_real:, :] = jnp.zeros((ff_total - ff_real, 128), f32)
        ff_near[ff_real:, :] = jnp.zeros((ff_total - ff_real, 128), f32)
    if total > 20 * part:
        for h in range(cores):
            big[h, 20 * part :, :] = jnp.zeros((total - 20 * part, 128), f32)
    wires.greet()
    ff_chains = []
    for i, (low, high) in enumerate(cut(ff_total, unit, (11 / 26, 22 / 26))):
        size = min(high, ff_real) - low
        here = pl.ds(low, size)
        opening = [wires.local(ff_pack.at[rows_of(core * ff_real + low, size)], ff_acc.at[here])]
        if cores > 1:
            opening.append(wires.sibling(ff_pack.at[rows_of(wires.other * ff_real + low, size)], ff_near.at[here]))
        ff_chains.append(
            Chain(
                wires,
                ff_acc,
                ff_near if cores > 1 else None,
                ff_got,
                ff_full,
                low,
                high - low,
                orders[i],
                opening,
                [],
            )
        )
    bounds = [2 * part, 12 * part, 17 * part]
    chains = []
    cuts = cut(total, unit, (2 / 25, 8 / 25, 13 / 25, 15 / 25, 18 / 25, 21 / 25, 23 / 25))
    for i, (low, high) in enumerate(cuts):
        here = pl.ds(low, high - low)
        opening, closing = [], []
        if cores > 1:
            opening = [wires.sibling(big.at[wires.other, here], near.at[here])]
            closing = [wires.sibling(full.at[core, here], full.at[core, here])]
        chain = Chain(
            wires,
            big.at[core],
            near if cores > 1 else None,
            got,
            full.at[core],
            low,
            high - low,
            orders[(0, 0, 1, 2, 0, 1, 0, 1)[i]],
            opening,
            closing,
        )
        chain.ready = sum(high > x for x in bounds)
        chains.append(chain)
    going = list(ff_chains)

    def ready(level):
        going.extend(c for c in chains if c.ready == level)
        step_all(going)

    def tick():
        step_all(going)

    def ticks_at(index, spots):
        for i, spot in enumerate(spots):

            @pl.when(index == spot)
            def _():
                for c in going:
                    c.run(c.next + i)

    def skip(count):
        for c in going:
            c.next += count

    def store(tile, value):
        for t in range(value.shape[1] // 128):
            for h in range(cores):
                big[h, (tile + t) * part : (tile + t + 1) * part, :] = value[
                    h * part : (h + 1) * part, 128 * t : 128 * t + 128
                ]

    tick()
    wo_l[...] = pack_lane(wo[...])
    wk_l[...] = pack_lane(wkv[:, :D])
    wv_l[...] = pack_lane(wkv[:, D:])
    kb[...] = jnp.zeros_like(kb)
    vb[...] = jnp.zeros_like(vb)
    acc[...] = jnp.zeros_like(acc)

    @pl.loop(0, slabs)
    def _(w):
        g = marks[slab(w), 0:1] * g_after[slab(w), :]
        grad[slab(w), :] = g
        acc[0] += fold(g)
        g_att[slab(w), :] = mm_lane(pack_left(g), wo_l[...])

    tick()
    d_wo = mm_rows(attended[...], grad[...])
    store(0, d_wo[:, :256])
    going.extend(c for c in chains if c.ready == 0)

    @pl.loop(0, blocks)
    def _(b):
        head_block(values, b, vb)
        here = pl.ds(window(b), WIN)
        first_row = 12 * (b % 2)
        row = lax.broadcasted_iota(jnp.int32, (WIN, D), 0)
        inside = (row >= first_row) & (row < first_row + BLOCK)
        ga = jnp.where(inside, g_att[here, :], 0.0)
        p = probs[b]
        gp = mm_lane(pack_left(ga), head_lane(vb))
        below = head_of_lane(p.shape)
        gs = p * (gp - per_head(below, gp * p, 0.0, jnp.sum)) * (HEAD**-0.5)
        g_scores[b] = gs
        here_k = pl.ds(pl.multiple_of(b * KPAD, 8), KPAD)
        g_values[here_k, :] = head_unblock(tmp, mm_rows(p, ga))
        g_keys[here_k, :] = head_unblock(tmp, mm_rows(gs, query[here, :]))
        ticks_at(b, range(1, blocks, 2))

    skip(len(range(1, blocks, 2)))

    @pl.loop(0, krows // SLAB)
    def _(w):
        gk, gv = g_keys[slab(w), :], g_values[slab(w), :]
        acc[1] += fold(gv)
        g = mm_lane(pack_left(gk), wk_l[...]) + mm_lane(pack_left(gv), wv_l[...])
        n = red_n[slab(w), :D]
        acc[2] += fold(g * n)
        acc[3] += fold(g)
        g = norm_back(g * gr, n, red_n[slab(w), D : D + 1])
        acc[4] += fold(g)
        grad[slab(w), :] = g

    g_red = grad[0:krows, :]
    for pair in range(2):
        d_wr = jnp.concatenate([mm_rows(g_red, patches[2 * pair]), mm_rows(g_red, patches[2 * pair + 1])], 1)
        store(2 + 5 * pair, d_wr)
    ready(1)
    reduced = red_n[:, :D] * gr + sr
    d_wk = mm_rows(reduced, g_keys[...])
    d_wv = mm_rows(reduced, g_values[...])
    store(12, jnp.concatenate([d_wk, d_wv], 1))
    ready(2)
    for sub in range(4):
        wr_l[sub] = pack_down(wr[:, sub * D : sub * D + D])

    @pl.loop(0, krows // SLAB)
    def _(w):
        packed = pack_left(grad[slab(w), :])
        for sub in range(4):
            g_patch[sub, slab(w), :] = mm(packed, wr_l[sub])

    @pl.loop(0, blocks)
    def _(b):
        head_block(keys, b, kb)
        place_window(g_query, b, mm(triple_left(g_scores[b]), triple_down(head_rows(kb))))
        ticks_at(b, range(1, blocks, 4))

    skip(len(range(1, blocks, 4)))
    wq_l[...] = pack_lane(wq[...])

    @pl.loop(0, slabs)
    def _(w):
        acc[5] += fold(g_query[slab(w), :])
        grad[slab(w), :] = first_n[slab(w), :D] * g1 + b1

    d_wq = mm_rows(grad[...], g_query[...])
    store(17, jnp.concatenate([d_wo[:, 256:], d_wq], 1))
    ready(3)

    @pl.loop(0, slabs)
    def _(w):
        g_att[slab(w), :] = mm_lane(pack_left(g_query[slab(w), :]), wq_l[...])
        ticks_at(w, range(3, slabs, 4))

    skip(len(range(3, slabs, 4)))

    @pl.loop(0, blocks)
    def _(b):
        which = kinds[first + b] * 2 + b % 2
        here_k = pl.ds(pl.multiple_of(b * KPAD, 8), KPAD)
        high, low = split(jnp.concatenate([g_patch[sub, here_k, :] for sub in range(4)], 0))
        pick = table[which]
        dims = (((0,), (0,)), ((), ()))
        moved = lax.dot_general(pick, high, dims, preferred_element_type=f32)
        moved = moved + lax.dot_general(pick, low, dims, preferred_element_type=f32)
        g_att[pl.ds(window(b), WIN), :] += moved
        ticks_at(b, range(3, blocks, 8))

    skip(len(range(3, blocks, 8)))

    @pl.loop(0, slabs)
    def _(w):
        n, scale = first_n[slab(w), :D], first_n[slab(w), D : D + 1]
        g = g_att[slab(w), :]
        acc[6] += fold(g * n)
        acc[7] += fold(g)
        grad[slab(w), :] = g_after[slab(w), :] + norm_back(g * g1, n, scale)
        ticks_at(w, range(3, slabs, 4))

    skip(len(range(3, slabs, 4)))
    order = (acc[6], acc[7], acc[5], acc[4], acc[2], acc[3], acc[1], acc[0], sums[0], sums[1], sums[2])
    value = jnp.concatenate([jnp.sum(x, 0, keepdims=True) for x in order] + [jnp.zeros((5, D), f32)], 0)
    value = jnp.concatenate([value, value[:, 256:]], 1)
    for t in range(3):
        small_sum[0, 16 * t : 16 * t + 16, :] = value[:, 128 * t : 128 * t + 128]
    partners = [wires.peer((k,), 1) for k in range(wires.bits)]
    if cores > 1:
        partners.insert(0, (wires.me, wires.other))
    for i, target in enumerate(partners):
        c = wires.copy(small_sum.at[i], small_got.at[i], target)
        c.start()
        tick()
        c.wait()
        small_sum[i + 1] = small_sum[i] + small_got[i]
    for t in range(3):
        small[:, 128 * t : 128 * t + 128] = small_sum[len(partners), 16 * t : 16 * t + 16, :]
    drain(going)


def attention_backward(pairs, cores, kinds, g_after, marks, vecs, wq, wr, wkv, wo, saved, sums, ff_pack):
    rows = g_after.shape[0]
    blocks = rows // BLOCK
    krows = blocks * KPAD
    bits = pairs.bit_length() - 1
    ff_total, total = sum_rows(pairs, cores)
    slots = 15 * (3 + 3 * bits)
    vm = pl.BlockSpec(memory_space=pltpu.VMEM)
    first_n, *saved = saved
    return pl.pallas_call(
        partial(backward_kernel, pairs, cores),
        out_shape=(
            jax.ShapeDtypeStruct((rows, D), f32),
            jax.ShapeDtypeStruct((ff_total, 128), f32),
            jax.ShapeDtypeStruct((cores, total, 128), f32),
            jax.ShapeDtypeStruct((16, 3 * 128), f32),
        ),
        in_specs=[pl.BlockSpec(memory_space=pltpu.SMEM)] + [vm] * 20 + [pl.BlockSpec(memory_space=pl.ANY)],
        out_specs=(vm,) * 4,
        scratch_shapes=[
            pltpu.VMEM((D, 1024), bf16),
            pltpu.VMEM((D, 1024), bf16),
            pltpu.VMEM((D, 1024), bf16),
            pltpu.VMEM((D, 1024), bf16),
            pltpu.VMEM((4, 1024, D), bf16),
            pltpu.VMEM((rows, D), f32),
            pltpu.VMEM((rows, D), f32),
            pltpu.VMEM((krows, D), f32),
            pltpu.VMEM((krows, D), f32),
            pltpu.VMEM((4, krows, D), f32),
            pltpu.VMEM((blocks, WIN, 256), f32),
            pltpu.VMEM((3, 256, 128), f32),
            pltpu.VMEM((3, 256, 128), f32),
            pltpu.VMEM((3, 256, 128), f32),
            pltpu.VMEM((8, 8, D), f32),
            pltpu.VMEM((ff_total, 128), f32),
            pltpu.VMEM((ff_total, 128), f32),
            pltpu.VMEM((ff_total, 128), f32),
            pltpu.VMEM((cores, total, 128), f32),
            pltpu.VMEM((total, 128), f32),
            pltpu.VMEM((total, 128), f32),
            pltpu.VMEM((bits + cores, 48, 128), f32),
            pltpu.VMEM((bits + cores, 48, 128), f32),
            pltpu.SemaphoreType.DMA((slots,)),
            pltpu.SemaphoreType.DMA((slots,)),
        ],
        compiler_params=pltpu.CompilerParams(
            collective_id=0 if pairs * cores > 1 else None, has_side_effects=True, vmem_limit_bytes=63 * MIB
        ),
        name="attention_back",
    )(
        kinds,
        first_n,
        g_after,
        marks,
        jnp.asarray(gather_table(), bf16),
        vecs[0],
        vecs[1],
        vecs[4],
        vecs[5],
        wq,
        wr,
        wkv,
        wo,
        *saved,
        sums,
        ff_pack,
    )


def unpack_kernel(grad, ff, rest, small, grad_t, d_we, d_ws, d_dw, d_be, d_bd, d_wr, d_wkv, d_wq, d_wo, *lines):
    cores = rest.shape[0]
    part = D // cores
    grad_t[...] = grad[...].T
    span = 2 * D + 16
    for t in range(d_we.shape[1] // 128):
        lanes = slice(128 * t, 128 * t + 128)
        d_we[:, lanes] = ff[t * span : t * span + D, :]
        d_ws[:, lanes] = ff[t * span + D : t * span + 2 * D, :]
        d_dw[:, lanes] = ff[t * span + 2 * D : t * span + 2 * D + 9, :]
    for row, ref in ((9, d_be), (10, d_bd)):
        at = 2 * D + row
        parts = [ff[t * span + at : t * span + at + 1, :] for t in range(d_we.shape[1] // 128)]
        ref[...] = jnp.concatenate(parts, 1).reshape(-1)
    for i, ref in enumerate(lines):
        ref[...] = small[i : i + 1, :D].reshape(-1)

    def tile(k):
        return jnp.concatenate([rest[h, k * part : k * part + part, :] for h in range(cores)], 0)

    for t in range(10):
        d_wr[:, 128 * t : 128 * t + 128] = tile(2 + t)
    for t in range(5):
        d_wkv[:, 128 * t : 128 * t + 128] = tile(12 + t)
    mixed = jnp.concatenate([tile(17 + t) for t in range(3)], 1)
    d_wo[...] = jnp.concatenate([tile(0), tile(1), mixed[:, :64]], 1)
    d_wq[...] = mixed[:, 64:]


def unpack(grad, ff, rest, small):
    cores = rest.shape[0]
    rows = grad.shape[0]
    chans = FF // cores
    vm = pl.BlockSpec(memory_space=pltpu.VMEM)
    shapes = [(D, rows), (D, chans), (D, chans), (9, chans), (chans,), (chans,)]
    shapes += [(D, 4 * D), (D, 2 * D), (D, D), (D, D)] + [(D,)] * 11
    return pl.pallas_call(
        unpack_kernel,
        out_shape=tuple(jax.ShapeDtypeStruct(x, f32) for x in shapes),
        in_specs=[vm] * 4,
        out_specs=(vm,) * len(shapes),
        compiler_params=pltpu.CompilerParams(vmem_limit_bytes=60 * MIB),
        name="unpack",
    )(grad, ff, rest, small)


def body(
    pairs,
    cores,
    tokens,
    block_kind,
    first_gain,
    first_bias,
    query_weight,
    query_bias,
    reduce_weight,
    reduce_bias,
    reduce_gain,
    reduce_shift,
    keyval_weight,
    value_bias,
    output_weight,
    output_bias,
    second_gain,
    second_shift,
    expand_weight,
    expand_bias,
    depth_weight,
    depth_bias,
    shrink_weight,
    shrink_bias,
    cotangent,
):
    own_taps = jnp.concatenate(
        [depth_weight, expand_bias[None], depth_bias[None], jnp.zeros((5, expand_bias.shape[0]), f32)], 0
    )
    hidden = [lax.all_gather(x, "hidden", axis=0) for x in (expand_weight, shrink_weight.T, own_taps)]
    vecs = (
        first_gain,
        first_bias,
        query_bias,
        reduce_bias,
        reduce_gain,
        reduce_shift,
        value_bias,
        output_bias,
    )
    late = (second_gain, second_shift, shrink_bias)
    weights = (query_weight, reduce_weight.T, keyval_weight, output_weight)
    after, marks, *saved = attention_forward(block_kind, tokens.T, vecs, *weights)
    result_t, g_after, ff_pack, sums = feed_forward(after, cotangent.T, marks, late, hidden)
    grad, ff_sum, rest, small = attention_backward(
        pairs, cores, block_kind, g_after, marks, vecs, *weights, saved, sums, ff_pack.reshape(-1, 128)
    )
    outs = unpack(grad, ff_sum, rest, small)
    grad_t, d_we, d_ws, d_dw, d_be, d_bd, d_wr, d_wkv, d_wq, d_wo, *small = outs
    return (
        result_t.T,
        grad_t.T,
        small[0],
        small[1],
        d_wq,
        small[2],
        d_wr.T,
        small[3],
        small[4],
        small[5],
        d_wkv,
        small[6],
        d_wo,
        small[7],
        small[8],
        small[9],
        d_we,
        d_be,
        d_dw,
        d_bd,
        d_ws.T,
        small[10],
    )


def solution(mesh):
    both = P(("dp", "hidden"), None)
    cols = P(None, "hidden")
    chan = P("hidden")
    deep = P("hidden", None)
    whole = P()
    return jax.shard_map(
        partial(body, mesh.shape["dp"], mesh.shape["hidden"]),
        mesh=mesh,
        in_specs=(both,) + (whole,) * 15 + (cols, chan, cols, chan, deep, whole, both),
        out_specs=(both, both) + (whole,) * 14 + (cols, chan, cols, chan, deep, whole),
        check_vma=False,
    )
```

```python
from functools import partial

import jax
import jax.numpy as jnp
import numpy as np
from jax import lax
from jax.experimental import pallas as pl
from jax.experimental.pallas import tpu as pltpu
from jax.sharding import PartitionSpec as P

HEADS = 5
HEAD = 64
BLOCK = 196
GRID = 14
SMALL = 6
SMALL_IMGS = 5
KVB = 49
D = 320
FF = 1280
KPAD = 56
WIN = 208
ODD = 184
CHUNK = 256
CHUNKS = FF // CHUNK
SLAB = 224
HALF = 112
PAD = 16
MIB = 1024 * 1024

f32 = jnp.float32
bf16 = jnp.bfloat16
MESH = pl.DeviceIdType.MESH


def gather_table():
    out = np.zeros((2, 2, 4 * KPAD, WIN), np.float32)
    for kind in range(2):
        for parity in range(2):
            off = 12 * parity
            for a in range(2):
                for b in range(2):
                    for key in range(KVB):
                        if kind == 0:
                            i, j = divmod(key, GRID // 2)
                            spot = (2 * i + a) * GRID + 2 * j + b
                        else:
                            if key >= 45:
                                continue
                            image, rest = divmod(key, 9)
                            i, j = divmod(rest, 3)
                            spot = image * 36 + (2 * i + a) * SMALL + 2 * j + b
                        out[kind, parity, (2 * a + b) * KPAD + key, off + spot] = 1.0
    return out.reshape(4, 4 * KPAD, WIN)


def score_table():
    out = np.full((2, 2, WIN, 256), -1e30, np.float32)
    for kind in range(2):
        for parity in range(2):
            off = 12 * parity
            for row in range(WIN):
                local = row - off
                for key in range(KVB):
                    if kind == 0 or local < 0 or local >= BLOCK:
                        good = True
                    else:
                        good = key < 45 and key // 9 == min(local // 36, 4)
                    if good:
                        for head in range(HEADS):
                            out[kind, parity, row, head * KVB + key] = 0.0
    return out.reshape(4, WIN, 256)


def row_table():
    out = np.zeros((2, 2, WIN, 128), np.float32)
    for parity in range(2):
        off = 12 * parity
        for row in range(BLOCK):
            i, j = divmod(row, GRID)
            out[0, parity, off + row, :7] = (1, j > 0, j < 13, i > 0, 0, i < 13, 0)
            if row < 180:
                i, j = divmod(row % 36, SMALL)
                out[1, parity, off + row, :7] = (1, j > 0, j < 5, 0, i > 0, 0, i < 5)
    return out.reshape(4, WIN, 128)


def split(x):
    high = x.astype(bf16)
    return high, (x - high.astype(f32)).astype(bf16)


def pack_left(x):
    high = x.astype(bf16).astype(f32)
    low = x - high
    tail = jnp.concatenate([high[:, 256:], low[:, 256:]], 1).astype(bf16)
    high, low = high[:, :256].astype(bf16), low[:, :256].astype(bf16)
    return jnp.concatenate([high, low, high, tail, tail], 1)


def pack_short(x):
    high = x.astype(bf16).astype(f32)
    low = x - high
    tail = jnp.concatenate([high[:, 256:], low[:, 256:]], 1).astype(bf16)
    return jnp.concatenate([high[:, :256].astype(bf16), low[:, :256].astype(bf16), tail], 1)


def pack_lane(w):
    high = w.astype(bf16).astype(f32)
    low = w - high
    tail_high = jnp.concatenate([high[:, 256:], high[:, 256:]], 1).astype(bf16)
    tail_low = jnp.concatenate([low[:, 256:], low[:, 256:]], 1).astype(bf16)
    high, low = high[:, :256].astype(bf16), low[:, :256].astype(bf16)
    return jnp.concatenate([high, high, low, tail_high, tail_low], 1)


def pack_down(w):
    high, low = split(w)
    return jnp.concatenate(
        [high[:256], high[:256], low[:256], high[256:], high[256:], low[256:], low[256:]], 0
    )


def triple_left(x):
    high, low = split(x)
    return jnp.concatenate([high, low, high], 1)


def triple_down(w):
    high, low = split(w)
    return jnp.concatenate([high, high, low], 0)


def triple_lane(w):
    high, low = split(w)
    return jnp.concatenate([high, high, low], 1)


def mm(a, b):
    return jnp.dot(a, b, preferred_element_type=f32)


def mm_lane(a, b):
    return lax.dot_general(a, b, (((1,), (1,)), ((), ())), preferred_element_type=f32)


def mm_rows(a, b):
    left_high, left_low = split(a.T)
    high, low = split(b)
    return mm(left_high, high) + mm(left_low, high) + mm(left_high, low)


def norm_rows(x):
    center = jnp.sum(x, -1, keepdims=True) * (1.0 / D)
    centered = x - center
    spread = jnp.sum(centered * centered, -1, keepdims=True) * (1.0 / D)
    scale = lax.rsqrt(spread + 1e-06)
    return centered * scale, scale


def norm_back(h, n, scale):
    mean_h = jnp.sum(h, -1, keepdims=True) * (1.0 / D)
    mean_hn = jnp.sum(h * n, -1, keepdims=True) * (1.0 / D)
    return scale * (h - mean_h - n * mean_hn)


def fold(x):
    return jnp.sum(x.reshape(x.shape[0] // 8, 8, x.shape[1]), 0)


def window(block):
    return pl.multiple_of((block // 2) * (2 * BLOCK) + (block % 2) * ODD, 8)


def slab(w):
    return pl.ds(pl.multiple_of(w * SLAB, SLAB), SLAB)


def place_window(ref, block, value):
    start = window(block)

    @pl.when(block % 2 == 0)
    def _():
        ref[pl.ds(start, WIN), :] = value

    @pl.when(block % 2 == 1)
    def _():
        edge = ref[pl.ds(start + 8, 8), :]
        rows = lax.broadcasted_iota(jnp.int32, edge.shape, 0)
        ref[pl.ds(start + 8, 8), :] = jnp.where(rows < 4, edge, value[8:16])
        ref[pl.ds(start + 16, WIN - 16), :] = value[16:]


def head_block(rows_ref, block, out_ref):
    start = pl.multiple_of(block * KPAD, 8)
    for head in range(HEADS):
        tile = head // 2
        if tile < 2:
            value = rows_ref[pl.ds(start, KPAD), tile * 128 : tile * 128 + 128]
            lane = lax.broadcasted_iota(jnp.int32, value.shape, 1)
            value = jnp.where((lane >= 64) == (head % 2 == 1), value, 0.0)
        else:
            half = rows_ref[pl.ds(start, KPAD), 256:320]
            value = jnp.concatenate([half, half], 1)
        out_ref[tile, head * KVB : head * KVB + KVB, :] = value[:KVB]


def head_rows(ref):
    return jnp.concatenate([ref[0], ref[1], ref[2][:, :64]], 1)


def head_unblock(ref, value):
    ref[0] = value[:, :128]
    ref[1] = value[:, 128:256]
    ref[2] = jnp.concatenate([value[:, 256:], value[:, 256:]], 1)
    lane = lax.broadcasted_iota(jnp.int32, (KPAD, 128), 1)
    row = lax.broadcasted_iota(jnp.int32, (KPAD, 128), 0)
    tiles = []
    for tile in range(3):
        first = ref[tile, 2 * tile * KVB : 2 * tile * KVB + KPAD, :]
        if tile < 2:
            second = ref[tile, (2 * tile + 1) * KVB : (2 * tile + 1) * KVB + KPAD, :]
            first = jnp.where(lane < 64, first, second)
        tiles.append(jnp.where(row < KVB, first, 0.0))
    return jnp.concatenate([tiles[0], tiles[1], tiles[2][:, :64]], 1)


def head_lane(ref):
    parts = []
    for tile in range(3):
        high = ref[tile].astype(bf16)
        parts.append((high, (ref[tile] - high.astype(f32)).astype(bf16)))
    return jnp.concatenate(
        [parts[0][0], parts[1][0], parts[0][0], parts[1][0], parts[0][1], parts[1][1], parts[2][0], parts[2][1]], 1
    )


def head_of_lane(shape):
    lane = lax.broadcasted_iota(jnp.int32, shape, 1)
    return [lane < (head + 1) * KVB for head in range(HEADS - 1)]


def by_head(below, values):
    out = values[HEADS - 1]
    for head in range(HEADS - 2, -1, -1):
        out = jnp.where(below[head], values[head], out)
    return out


def per_head(below, x, empty, reduce):
    out = []
    for head in range(HEADS):
        here = x
        if head < HEADS - 1:
            here = jnp.where(below[head], here, empty)
        if head > 0:
            here = jnp.where(below[head - 1], empty, here)
        out.append(reduce(here, axis=1, keepdims=True))
    return by_head(below, [jnp.broadcast_to(v, x.shape) for v in out])


def line(ref):
    return ref[...].reshape(1, -1)


def own_first(blocks):
    return (lax.axis_index("dp") * lax.axis_size("hidden") + lax.axis_index("hidden")) * blocks


def attention_kernel(
    kinds,
    tokens_t,
    table,
    scores_mask,
    row_marks,
    first_gain,
    first_bias,
    query_bias,
    reduce_bias,
    reduce_gain,
    reduce_shift,
    value_bias,
    output_bias,
    wq,
    wr,
    wkv,
    wo,
    after,
    marks,
    first_n,
    query,
    attended,
    probs,
    keys,
    values,
    red_n,
    patches,
    wq_s,
    wo_s,
    wk_s,
    wv_s,
    wr_s,
    tokens,
    normed,
    kb,
    vb,
):
    blocks = probs.shape[0]
    slabs = tokens.shape[0] // SLAB
    first = own_first(blocks)
    g1, b1, bq, br = line(first_gain), line(first_bias), line(query_bias), line(reduce_bias)
    gr, sr, bv, bo = line(reduce_gain), line(reduce_shift), line(value_bias), line(output_bias)
    wq_s[...] = pack_down(wq[...])
    wo_s[...] = pack_down(wo[...])
    wk_s[...] = pack_down(wkv[:, :D])
    wv_s[...] = pack_down(wkv[:, D:])
    for sub in range(4):
        wr_s[sub] = pack_lane(wr[:, sub * D : sub * D + D])
    kb[...] = jnp.zeros_like(kb)
    vb[...] = jnp.zeros_like(vb)
    tokens[...] = tokens_t[...].T

    @pl.loop(0, slabs)
    def _(w):
        n, scale = norm_rows(tokens[slab(w), :])
        first_n[slab(w), :] = jnp.concatenate([n, jnp.broadcast_to(scale, (SLAB, 64))], 1)
        n = n * g1 + b1
        normed[slab(w), :] = n
        query[slab(w), :] = mm(pack_left(n), wq_s[...]) + bq

    @pl.loop(0, blocks)
    def _(b):
        which = kinds[first + b] * 2 + b % 2
        place_window(marks, b, row_marks[which])
        part = normed[pl.ds(window(b), WIN), :]
        high, low = split(part)
        pick = table[which]
        got = mm(pick, high) + mm(pick, low)
        rows = pl.ds(pl.multiple_of(b * KPAD, 8), KPAD)
        for sub in range(4):
            patches[sub, rows, :] = got[sub * KPAD : sub * KPAD + KPAD]

    @pl.loop(0, blocks * KPAD // SLAB)
    def _(w):
        acc = br + mm_lane(pack_left(patches[0, slab(w), :]), wr_s[0])
        for sub in range(1, 4):
            acc = acc + mm_lane(pack_left(patches[sub, slab(w), :]), wr_s[sub])
        n, scale = norm_rows(acc)
        red_n[slab(w), :] = jnp.concatenate([n, jnp.broadcast_to(scale, (SLAB, 64))], 1)
        packed = pack_left(n * gr + sr)
        keys[slab(w), :] = mm(packed, wk_s[...])
        values[slab(w), :] = mm(packed, wv_s[...]) + bv

    @pl.loop(0, blocks)
    def _(b):
        which = kinds[first + b] * 2 + b % 2
        head_block(keys, b, kb)
        head_block(values, b, vb)
        q = query[pl.ds(window(b), WIN), :]
        s = mm_lane(pack_left(q), head_lane(kb)) * (HEAD**-0.5) + scores_mask[which]
        below = head_of_lane(s.shape)
        e = jnp.exp(s - per_head(below, s, -3e38, jnp.max))
        p = e / per_head(below, e, 0.0, jnp.sum)
        probs[b] = p
        out = mm(triple_left(p), triple_down(head_rows(vb)))
        place_window(attended, b, out)

    @pl.loop(0, slabs)
    def _(w):
        branch = mm(pack_left(attended[slab(w), :]), wo_s[...]) + bo
        after[slab(w), :] = tokens[slab(w), :] + marks[slab(w), 0:1] * branch


def attention_forward(kinds, tokens_t, vecs, wq, wr, wkv, wo):
    rows = tokens_t.shape[1]
    blocks = rows // BLOCK
    krows = blocks * KPAD
    vm = pl.BlockSpec(memory_space=pltpu.VMEM)

    def shape(*dims):
        return jax.ShapeDtypeStruct(dims, f32)

    return pl.pallas_call(
        attention_kernel,
        out_shape=(
            shape(rows, D),
            shape(rows, 128),
            shape(rows, D + 64),
            shape(rows, D),
            shape(rows, D),
            shape(blocks, WIN, 256),
            shape(krows, D),
            shape(krows, D),
            shape(krows, D + 64),
            shape(4, krows, D),
        ),
        in_specs=[pl.BlockSpec(memory_space=pltpu.SMEM)] + [vm] * 16,
        out_specs=(vm,) * 10,
        scratch_shapes=[
            pltpu.VMEM((1024, D), bf16),
            pltpu.VMEM((1024, D), bf16),
            pltpu.VMEM((1024, D), bf16),
            pltpu.VMEM((1024, D), bf16),
            pltpu.VMEM((4, D, 1024), bf16),
            pltpu.VMEM((rows, D), f32),
            pltpu.VMEM((rows, D), f32),
            pltpu.VMEM((3, 256, 128), f32),
            pltpu.VMEM((3, 256, 128), f32),
        ],
        compiler_params=pltpu.CompilerParams(vmem_limit_bytes=60 * MIB),
        name="attention",
    )(
        kinds,
        tokens_t,
        jnp.asarray(gather_table(), bf16),
        jnp.asarray(score_table()),
        jnp.asarray(row_table()),
        *vecs,
        wq,
        wr,
        wkv,
        wo,
    )


ERF_P = 0.3275911
ERF = (0.254829592, -0.284496736, 1.421413741, -1.453152027, 1.061405429)


def gelu_pair(x):
    size = jnp.abs(x)
    d = 1.0 + (ERF_P * 0.7071067811865476) * size
    t = pl.reciprocal(d, approx=True)
    t = t * (2.0 - d * t)
    e = jnp.exp(-0.5 * (x * x))
    poly = t * (ERF[0] + t * (ERF[1] + t * (ERF[2] + t * (ERF[3] + t * ERF[4]))))
    tail = 0.5 * (poly * e)
    phi = jnp.where(x < 0.0, tail, 1.0 - tail)
    return x * phi, phi + x * (0.3989422804014327 * e)


TOP = 64
STEP = 16


def forward_kernel(
    after,
    cot_t,
    marks,
    second_gain,
    second_shift,
    shrink_bias,
    own_we,
    own_ws,
    own_taps,
    result_t,
    g_after,
    pack,
    sums,
    we_s,
    we_l,
    ws_s,
    ws_l,
    result,
    g_second,
    masks,
    taps,
    second,
    branch,
    second_t,
    branch_t,
    xs0,
    xs1,
    ga0,
    ga1,
    y0,
    ym,
    yp,
    act0,
    act1,
    gx0,
    gx1,
    dwe,
    dws,
    dw,
    sem,
):
    rows = after.shape[0]
    part = rows // 2
    ends = xs0.shape[1]
    per = FF // 128 // own_we.shape[0]
    xs, ga, act, gx = (xs0, xs1), (ga0, ga1), (act0, act1), (gx0, gx1)

    g2, s2, bs = line(second_gain), line(second_shift), line(shrink_bias)
    loads = []
    for tile in range(FF // 128):
        lanes = pl.ds((tile % per) * 128, 128)
        for i, (source, low, size) in enumerate(((own_we, 0, D), (own_ws, D, D), (own_taps, 2 * D, 16))):
            loads.append(
                pltpu.make_async_copy(
                    source.at[tile // per, :, lanes], pack.at[tile, pl.ds(low, size)], sem.at[3 * tile + i]
                )
            )
    for load in loads:
        load.start()

    for ref in (xs0, xs1, ga0, ga1, y0, ym, yp, masks.at[0], masks.at[1]):
        for t in range(ref.shape[0]):
            ref[t, 0:TOP, :] = jnp.zeros((TOP, 128), f32)
            ref[t, TOP + part : ends, :] = jnp.zeros((ends - TOP - part, 128), f32)
    act1[...] = jnp.zeros_like(act1)
    gx1[...] = jnp.zeros_like(gx1)
    sums[...] = jnp.zeros_like(sums)
    g_after[...] = cot_t[...].T

    for h in range(2):

        @pl.loop(0, part // HALF)
        def _(w):
            here = pl.ds(pl.multiple_of(h * part + w * HALF, 16), HALF)
            lower = pl.ds(pl.multiple_of(TOP + w * HALF, 16), HALF)
            n, _ = norm_rows(after[here, :])
            value = n * g2 + s2
            for k in range(1, 7):
                masks[h, k - 1, lower, :] = jnp.broadcast_to(marks[here, k : k + 1], (HALF, 128))
            grad = marks[here, 0:1] * g_after[here, :]
            sums[2] += fold(grad)
            second[here, :] = pack_short(value)
            branch[here, :] = pack_short(grad)
            g_second[here, :] = value
            result[here, :] = grad

        for source, turned in ((g_second, second_t), (result, branch_t)):
            high, low = split(source[h * part : (h + 1) * part, :].T)
            turned[h] = jnp.concatenate([high, low, high], 1)
    result[...] = jnp.zeros_like(result)
    g_second[...] = jnp.zeros_like(g_second)

    for load in loads:
        load.wait()
    for c in range(CHUNKS):
        for which, (down, lane) in enumerate(((we_s, we_l), (ws_s, ws_l))):
            value = jnp.concatenate([pack[2 * c + t, which * D : which * D + D, :] for t in range(2)], 1)
            high, low = split(value)
            down[c] = jnp.concatenate([high, low], 0)
            lane[c] = jnp.concatenate([high, low], 1)
        for t in range(2):
            for k in range(11):
                taps[c, t, k] = jnp.broadcast_to(pack[2 * c + t, 2 * D + k : 2 * D + k + 1, :], (8, 128))

    inner = slice(TOP, TOP + part)

    def own(h):
        return slice(h * part, (h + 1) * part)

    def left(ref, h):
        x = ref[own(h), :]
        return jnp.concatenate([x[:, :512], x[:, :256], x[:, 512:], x[:, 512:]], 1)

    def deep(ref, c):
        x = ref[c]
        return jnp.concatenate(
            [x[:256], x[:256], x[D : D + 256], x[256:D], x[256:D], x[D + 256 :], x[D + 256 :]], 0
        )

    def expand_task(c, h):
        e = mm(left(second, h), deep(we_s, c))
        for t in range(2):
            xs[h][t, inner, :] = e[:, 128 * t : 128 * t + 128] + taps[c, t, 9][0:1]

    def active_grad_task(c, h):
        g = mm(left(branch, h), deep(ws_s, c))
        for t in range(2):
            ga[h][t, inner, :] = g[:, 128 * t : 128 * t + 128]

    def out_task(c, h, source, lane, out):
        x = source[h][inner, :]
        weight = lane[c]
        out[own(h), :] += mm_lane(
            jnp.concatenate([x, x[:, :256]], 1), jnp.concatenate([weight[:, :256], weight], 1)
        )

    def weight_task(c, h, source, turned, total, row):
        x = source[h][inner, :]
        high, low = x[:, :256], x[:, 256:]
        value = mm(turned[h], jnp.concatenate([high, high, low], 0))
        if h == 0:
            total[...] = value
        else:
            value = value + total[...]
            for t in range(2):
                pack[2 * c + t, row : row + D, :] = value[:, 128 * t : 128 * t + 128]

    def early_tasks(c, h):
        return [partial(expand_task, c, h), partial(active_grad_task, c, h)]

    def late_tasks(c, h):
        return [
            partial(out_task, c, h, act, ws_l, result),
            partial(weight_task, c, h, act, branch_t, dws, D),
            partial(out_task, c, h, gx, we_l, g_second),
            partial(weight_task, c, h, gx, second_t, dwe, 0),
        ]

    def near(ref, t, base, shift=0):
        at = base + TOP + shift
        return ref[t, at : at + STEP, :].reshape(STEP // 8, 8, 128)

    def put(ref, t, base, value):
        ref[t, base + TOP : base + TOP + STEP, :] = value.reshape(STEP, 128)

    def put_split(ref, t, base, value):
        high, low = split(value.reshape(STEP, 128))
        here = slice(base + TOP, base + TOP + STEP)
        ref[here, 128 * t : 128 * t + 128] = high
        ref[here, 256 + 128 * t : 384 + 128 * t] = low

    def item(c, h, tasks):
        m = masks.at[h]
        x, g = xs[h], ga[h]

        def columns(t, base):
            return (
                near(m, 0, base) * near(x, t, base, -1),
                near(x, t, base),
                near(m, 1, base) * near(x, t, base, 1),
            )

        def mix(t, values, ks):
            a, b, d = (v * taps[c, t, k] for v, k in zip(values, ks))
            return a + b + d

        def rows_step(t, base):
            cols = columns(t, base)
            put(ym, t, base, mix(t, cols, (0, 1, 2)))
            put(y0, t, base, mix(t, cols, (3, 4, 5)) + taps[c, t, 10])
            put(yp, t, base, mix(t, cols, (6, 7, 8)))

        def gelu_step(t, base):
            conv = (
                near(y0, t, base)
                + near(m, 2, base) * near(ym, t, base, -14)
                + near(m, 3, base) * near(ym, t, base, -6)
                + near(m, 4, base) * near(yp, t, base, 14)
                + near(m, 5, base) * near(yp, t, base, 6)
            )
            active, slope = gelu_pair(conv)
            put_split(act[h], t, base, active)
            put(g, t, base, near(g, t, base) * slope)

        def back_step(t, base, totals):
            down = near(m, 2, base) * near(g, t, base, -14) + near(m, 3, base) * near(g, t, base, -6)
            same = near(g, t, base)
            up = near(m, 4, base) * near(g, t, base, 14) + near(m, 5, base) * near(g, t, base, 6)
            cols = columns(t, base)
            moved = (up, same, down)
            totals[10] = totals[10] + jnp.sum(same, 0)
            for p in range(3):
                for q in range(3):
                    totals[3 * p + q] = totals[3 * p + q] + jnp.sum(moved[p] * cols[q], 0)
            put(ym, t, base, mix(t, moved, (0, 3, 6)))
            put(y0, t, base, mix(t, moved, (1, 4, 7)))
            put(yp, t, base, mix(t, moved, (2, 5, 8)))

        def last_step(t, base, totals):
            value = (
                near(y0, t, base) + near(m, 0, base) * near(yp, t, base, -1) + near(m, 1, base) * near(ym, t, base, 1)
            )
            put_split(gx[h], t, base, value)
            totals[9] = totals[9] + jnp.sum(value, 0)

        steps = part // STEP
        slots = {round((i + 0.5) * 2 * steps / max(len(tasks), 1)): task for i, task in enumerate(tasks)}
        for t in range(2):
            totals = [jnp.zeros((8, 128), f32)] * 11
            for k in range(steps + 3):
                base = k * STEP
                if k < steps:
                    rows_step(t, base)
                if 1 <= k < steps + 1:
                    gelu_step(t, base - STEP)
                if 2 <= k < steps + 2:
                    back_step(t, base - 2 * STEP, totals)
                if 3 <= k:
                    last_step(t, base - 3 * STEP, totals)
                if k < steps and t * steps + k in slots:
                    slots[t * steps + k]()
            for k in range(11):
                if h == 0:
                    dw[t, k] = totals[k]
                else:
                    pack[2 * c + t, 2 * D + k : 2 * D + k + 1, :] = jnp.sum(dw[t, k] + totals[k], 0, keepdims=True)

    for task in early_tasks(0, 0):
        task()

    @pl.loop(0, CHUNKS)
    def _(c):
        item(c, 0, early_tasks(c, 1) + late_tasks(jnp.maximum(c - 1, 0), 1))
        item(c, 1, early_tasks(jnp.minimum(c + 1, CHUNKS - 1), 0) + late_tasks(c, 0))

    for task in late_tasks(CHUNKS - 1, 1):
        task()
    for c in range(CHUNKS):
        for t in range(2):
            pack[2 * c + t, 2 * D + 11 : 2 * D + 16, :] = jnp.zeros((5, 128), f32)

    @pl.loop(0, rows // SLAB)
    def _(w):
        a = after[slab(w), :]
        live = marks[slab(w), 0:1]
        result[slab(w), :] = a + live * (result[slab(w), :] + bs)
        n, scale = norm_rows(a)
        g = g_second[slab(w), :]
        sums[0] += fold(g * n)
        sums[1] += fold(g)
        g_after[slab(w), :] = g_after[slab(w), :] + norm_back(g * g2, n, scale)

    result_t[...] = result[...].T


def feed_forward(after, cot_t, marks, vecs, weights):
    rows = after.shape[0]
    vm = pl.BlockSpec(memory_space=pltpu.VMEM)
    part = rows // 2
    ends = 2 * TOP + part
    padded = pltpu.VMEM((2, ends, 128), f32)
    half = pltpu.VMEM((ends, 2 * CHUNK), bf16)
    return pl.pallas_call(
        forward_kernel,
        out_shape=(
            jax.ShapeDtypeStruct((D, rows), f32),
            jax.ShapeDtypeStruct((rows, D), f32),
            jax.ShapeDtypeStruct((2 * CHUNKS, 2 * D + 16, 128), f32),
            jax.ShapeDtypeStruct((3, 8, D), f32),
        ),
        in_specs=[vm] * 6 + [pl.BlockSpec(memory_space=pl.ANY)] * 3,
        out_specs=(vm,) * 4,
        scratch_shapes=[
            pltpu.VMEM((CHUNKS, 2 * D, CHUNK), bf16),
            pltpu.VMEM((CHUNKS, D, 2 * CHUNK), bf16),
            pltpu.VMEM((CHUNKS, 2 * D, CHUNK), bf16),
            pltpu.VMEM((CHUNKS, D, 2 * CHUNK), bf16),
            pltpu.VMEM((rows, D), f32),
            pltpu.VMEM((rows, D), f32),
            pltpu.VMEM((2, 6, ends, 128), f32),
            pltpu.VMEM((CHUNKS, 2, 11, 8, 128), f32),
            pltpu.VMEM((rows, 640), bf16),
            pltpu.VMEM((rows, 640), bf16),
            pltpu.VMEM((2, D, 3 * part), bf16),
            pltpu.VMEM((2, D, 3 * part), bf16),
            padded,
            padded,
            padded,
            padded,
            padded,
            padded,
            padded,
            half,
            half,
            half,
            half,
            pltpu.VMEM((D, CHUNK), f32),
            pltpu.VMEM((D, CHUNK), f32),
            pltpu.VMEM((2, 11, 8, 128), f32),
            pltpu.SemaphoreType.DMA((6 * CHUNKS,)),
        ],
        compiler_params=pltpu.CompilerParams(vmem_limit_bytes=63 * MIB),
        name="feed_forward",
    )(after, cot_t, marks, *vecs, *weights)


class Wires:
    def __init__(self, pairs, cores, send, recv):
        self.bits = pairs.bit_length() - 1
        self.cores = cores
        self.me, self.core = lax.axis_index("dp"), lax.axis_index("hidden")
        self.other = cores - 1 - self.core
        self.send, self.recv, self.used = send, recv, 0

    def groups(self):
        rest = list(range(2, self.bits))
        return [(k,) for k in range(min(2, self.bits))] + [tuple(rest[i : i + 2]) for i in range(0, len(rest), 2)]

    def bit(self, k):
        return (self.me // (1 << k)) % 2

    def peer(self, group, j):
        flips = [(1 - 2 * self.bit(k)) * (1 << k) for i, k in enumerate(group) if (j >> i) & 1]
        return (sum(flips, self.me), self.core)

    def place(self, group, j):
        bits = [(1 - self.bit(k) if (j >> i) & 1 else self.bit(k)) * (1 << i) for i, k in enumerate(group)]
        return sum(bits[1:], bits[0])

    def greet(self):
        peers = [self.peer(group, j) for group in self.groups() for j in range(1, 1 << len(group))]
        if self.cores > 1:
            peers.append((self.me, self.other))
        if not peers:
            return
        barrier = pltpu.get_barrier_semaphore()
        for target in peers:
            pl.semaphore_signal(barrier, inc=1, device_id=target, device_id_type=MESH)
        pl.semaphore_wait(barrier, len(peers))

    def copy(self, src, dst, target):
        slot = self.used
        self.used += 1
        return pltpu.make_async_remote_copy(
            src_ref=src,
            dst_ref=dst,
            send_sem=self.send.at[slot],
            recv_sem=self.recv.at[slot],
            device_id=target,
            device_id_type=MESH,
        )

    def local(self, src, dst):
        slot = self.used
        self.used += 1
        return pltpu.make_async_copy(src, dst, self.send.at[slot])

    def sibling(self, src, dst):
        return self.copy(src, dst, (self.me, self.other))


def rows_of(start, size):
    return pl.ds(pl.multiple_of(start, 8), size)


class Chain:
    def __init__(self, wires, acc, near, got, full, base, rows, order, opening, closing):
        self.stages, self.costs = [], []
        whole = pl.ds(base, rows)
        scale = 512 * wires.cores / LINK

        def meet():
            if near is not None:
                acc[whole, :] = acc[whole, :] + near[whole, :]

        start, size, spot = base + 0 * wires.me, rows, base
        pending, action = opening, meet
        self.stages.append(([], None, opening))
        self.costs.append(("core", rows * 512 / CORE_LINK))
        held = []
        for group in order:
            many = 1 << len(group)
            size //= many
            keep = start + wires.place(group, 0) * size
            copies, lands = [], []
            for j in range(1, many):
                land = pl.ds(spot, size)
                spot += size
                give = start + wires.place(group, j) * size
                copies.append(wires.copy(acc.at[rows_of(give, size)], got.at[land], wires.peer(group, j)))
                lands.append(land)
            self.stages.append((pending, action, copies))
            self.costs.append((group, scale * size * (1 if many == 2 else many)))

            def add(keep=keep, lands=lands, size=size):
                value = acc[rows_of(keep, size), :]
                for land in lands:
                    value = value + got[land, :]
                acc[rows_of(keep, size), :] = value

            pending, action = copies, add
            held.append((group, start))
            start = keep
        last, last_start, last_size = action, start, size

        def settle():
            last()
            full[rows_of(last_start, last_size), :] = acc[rows_of(last_start, last_size), :]

        action = settle
        for group, before in reversed(held):
            mine = rows_of(start, size)
            many = 1 << len(group)
            copies = [wires.copy(full.at[mine], full.at[mine], wires.peer(group, j)) for j in range(1, many)]
            self.stages.append((pending, action, copies))
            self.costs.append((group, scale * size * (1 if many == 2 else many)))
            pending, action = copies, None
            start, size = before, size * many
        if closing:
            self.stages.append((pending, action, closing))
            self.costs.append(("core", rows * 512 / CORE_LINK))
            pending, action = closing, None
        self.stages.append((pending, action, []))
        self.costs.append((None, 0.0))

    def run(self, stage):
        waits, action, starts = self.stages[stage]
        for c in waits:
            c.wait()
        if action is not None:
            action()
        for c in starts:
            c.start()


class Exchange(Chain):
    def __init__(self, wires, sums, got):
        partners = [((k,), wires.peer((k,), 1)) for k in range(wires.bits)]
        if wires.cores > 1:
            partners.insert(0, ("core", (wires.me, wires.other)))
        self.stages, self.costs = [], []
        pending, action = [], None
        for i, (name, target) in enumerate(partners):
            c = wires.copy(sums.at[i], got.at[i], target)
            self.stages.append((pending, action, [c]))
            self.costs.append((name, 0.5))

            def add(i=i):
                sums[i + 1] = sums[i] + got[i]

            pending, action = [c], add
        self.stages.append((pending, action, []))
        self.costs.append((None, 0.0))
        self.last = len(partners)


LINK = 100e3
CORE_LINK = 400e3
DELAY = 1.5
STEP_WORK = 0.1


class Plan:
    def __init__(self):
        self.now, self.free, self.going = 0.0, {}, []

    def add(self, chains):
        self.going += [[self.now, c, 0] for c in chains]

    def after(self, us):
        self.now += us
        due = []
        while True:
            ready = [g for g in self.going if g[0] <= self.now]
            if not ready:
                return due
            due.append(self.take(min(ready, key=lambda g: g[0])))

    def take(self, entry):
        done, chain, stage = entry
        self.now = max(self.now, done) + STEP_WORK
        link, us = chain.costs[stage]
        self.free[link] = max(self.free.get(link, 0.0), self.now) + us
        if stage + 1 == len(chain.stages):
            self.going.remove(entry)
        else:
            entry[0], entry[2] = self.free[link] + DELAY, stage + 1
        return chain, stage

    def rest(self):
        due = []
        while self.going:
            due.append(self.take(min(self.going, key=lambda g: g[0])))
        return due


def run_steps(steps):
    for chain, stage in steps:
        chain.run(stage)


def axis_orders(groups):
    return groups, groups[1::-1] + groups[2:], groups[2:] + groups[:2]


def cut(total, unit, parts):
    units = total // unit
    marks = sorted({0, units} | {round(units * x) for x in parts})
    return [(a * unit, b * unit) for a, b in zip(marks, marks[1:])]


def round_up(x, unit):
    return -(-x // unit) * unit


def sum_rows(pairs, cores):
    unit = 8 * pairs
    ff = round_up(2 * CHUNKS // cores * (2 * D + 16), unit)
    rest = round_up(20 * (D // cores), unit)
    return ff, rest


def backward_kernel(
    pairs,
    cores,
    kinds,
    first_n,
    g_after,
    marks,
    table,
    first_gain,
    first_bias,
    reduce_gain,
    reduce_shift,
    wq,
    wr,
    wkv,
    wo,
    query,
    attended,
    probs,
    keys,
    values,
    red_n,
    patches,
    sums,
    ff_pack,
    grad,
    ff_full,
    full,
    small,
    wq_l,
    wo_l,
    wk_l,
    wv_l,
    wr_l,
    g_att,
    g_query,
    g_keys,
    g_values,
    g_patch,
    g_scores,
    kb,
    vb,
    tmp,
    acc,
    ff_acc,
    ff_near,
    ff_got,
    big,
    near,
    got,
    small_sum,
    small_got,
    send,
    recv,
):
    blocks = probs.shape[0]
    rows = g_after.shape[0]
    slabs = rows // SLAB
    krows = blocks * KPAD
    first = own_first(blocks)
    part = D // cores
    g1, b1, gr, sr = line(first_gain), line(first_bias), line(reduce_gain), line(reduce_shift)

    wires = Wires(pairs, cores, send, recv)
    core = wires.core
    orders = axis_orders(wires.groups())
    unit = 8 * pairs
    ff_real = ff_pack.shape[0] // cores
    ff_total, total = ff_acc.shape[0], big.shape[1]
    if ff_total > ff_real:
        ff_acc[ff_real:, :] = jnp.zeros((ff_total - ff_real, 128), f32)
        ff_near[ff_real:, :] = jnp.zeros((ff_total - ff_real, 128), f32)
    if total > 20 * part:
        for h in range(cores):
            big[h, 20 * part :, :] = jnp.zeros((total - 20 * part, 128), f32)
    wires.greet()
    ff_chains = []
    for i, (low, high) in enumerate(cut(ff_total, unit, (4 / 26, 10 / 26, 16 / 26, 21 / 26))):
        size = min(high, ff_real) - low
        here = pl.ds(low, size)
        opening = [wires.local(ff_pack.at[rows_of(core * ff_real + low, size)], ff_acc.at[here])]
        if cores > 1:
            opening.append(wires.sibling(ff_pack.at[rows_of(wires.other * ff_real + low, size)], ff_near.at[here]))
        ff_chains.append(
            Chain(
                wires,
                ff_acc,
                ff_near if cores > 1 else None,
                ff_got,
                ff_full,
                low,
                high - low,
                orders[(2, 0, 1, 0, 1)[i]],
                opening,
                [],
            )
        )
    bounds = [2 * part, 12 * part, 17 * part]
    chains = []
    cuts = cut(total, unit, (2 / 25, 8 / 25, 13 / 25, 15 / 25, 18 / 25, 21 / 25, 23 / 25))
    for i, (low, high) in enumerate(cuts):
        here = pl.ds(low, high - low)
        opening, closing = [], []
        if cores > 1:
            opening = [wires.sibling(big.at[wires.other, here], near.at[here])]
            closing = [wires.sibling(full.at[core, here], full.at[core, here])]
        chain = Chain(
            wires,
            big.at[core],
            near if cores > 1 else None,
            got,
            full.at[core],
            low,
            high - low,
            orders[(0, 0, 1, 2, 0, 1, 0, 1)[i]],
            opening,
            closing,
        )
        chain.ready = sum(high > x for x in bounds)
        chains.append(chain)
    plan = Plan()
    plan.add(ff_chains)

    def tick(us, level=None):
        run_steps(plan.after(us))
        if level is not None:
            plan.add([c for c in chains if c.ready == level])
            run_steps(plan.after(0.0))

    def ticks(count, us):
        return [plan.after(us) for _ in range(count)]

    def run_at(index, planned):
        for i, steps in enumerate(planned):
            if steps:
                pl.when(index == i)(partial(run_steps, steps))

    def store(tile, value):
        for t in range(value.shape[1] // 128):
            for h in range(cores):
                big[h, (tile + t) * part : (tile + t + 1) * part, :] = value[
                    h * part : (h + 1) * part, 128 * t : 128 * t + 128
                ]

    tick(0.0)
    wo_l[...] = pack_lane(wo[...])
    wk_l[...] = pack_lane(wkv[:, :D])
    wv_l[...] = pack_lane(wkv[:, D:])
    kb[...] = jnp.zeros_like(kb)
    vb[...] = jnp.zeros_like(vb)
    acc[...] = jnp.zeros_like(acc)
    tick(2.0)
    planned_0 = ticks(slabs, 0.6)

    @pl.loop(0, slabs)
    def _(w):
        g = marks[slab(w), 0:1] * g_after[slab(w), :]
        grad[slab(w), :] = g
        acc[0] += fold(g)
        g_att[slab(w), :] = mm_lane(pack_left(g), wo_l[...])
        run_at(w, planned_0)

    d_wo = mm_rows(attended[...], grad[...])
    store(0, d_wo[:, :256])
    tick(3.5, 0)
    planned_1 = ticks(blocks, 1.8)

    @pl.loop(0, blocks)
    def _(b):
        head_block(values, b, vb)
        here = pl.ds(window(b), WIN)
        first_row = 12 * (b % 2)
        row = lax.broadcasted_iota(jnp.int32, (WIN, D), 0)
        inside = (row >= first_row) & (row < first_row + BLOCK)
        ga = jnp.where(inside, g_att[here, :], 0.0)
        p = probs[b]
        gp = mm_lane(pack_left(ga), head_lane(vb))
        below = head_of_lane(p.shape)
        gs = p * (gp - per_head(below, gp * p, 0.0, jnp.sum)) * (HEAD**-0.5)
        g_scores[b] = gs
        here_k = pl.ds(pl.multiple_of(b * KPAD, 8), KPAD)
        g_values[here_k, :] = head_unblock(tmp, mm_rows(p, ga))
        g_keys[here_k, :] = head_unblock(tmp, mm_rows(gs, query[here, :]))
        run_at(b, planned_1)


    @pl.loop(0, krows // SLAB)
    def _(w):
        gk, gv = g_keys[slab(w), :], g_values[slab(w), :]
        acc[1] += fold(gv)
        g = mm_lane(pack_left(gk), wk_l[...]) + mm_lane(pack_left(gv), wv_l[...])
        n = red_n[slab(w), :D]
        acc[2] += fold(g * n)
        acc[3] += fold(g)
        g = norm_back(g * gr, n, red_n[slab(w), D : D + 1])
        acc[4] += fold(g)
        grad[slab(w), :] = g

    tick(2.0)
    g_red = grad[0:krows, :]
    for pair in range(2):
        d_wr = jnp.concatenate([mm_rows(g_red, patches[2 * pair]), mm_rows(g_red, patches[2 * pair + 1])], 1)
        store(2 + 5 * pair, d_wr)
        tick(2.0, 1 if pair else None)
    reduced = red_n[:, :D] * gr + sr
    d_wk = mm_rows(reduced, g_keys[...])
    d_wv = mm_rows(reduced, g_values[...])
    store(12, jnp.concatenate([d_wk, d_wv], 1))
    tick(2.5, 2)
    for sub in range(4):
        wr_l[sub] = pack_down(wr[:, sub * D : sub * D + D])

    @pl.loop(0, krows // SLAB)
    def _(w):
        packed = pack_left(grad[slab(w), :])
        for sub in range(4):
            g_patch[sub, slab(w), :] = mm(packed, wr_l[sub])

    tick(2.0)
    planned_2 = ticks(blocks, 0.6)

    @pl.loop(0, blocks)
    def _(b):
        head_block(keys, b, kb)
        place_window(g_query, b, mm(triple_left(g_scores[b]), triple_down(head_rows(kb))))
        run_at(b, planned_2)

    wq_l[...] = pack_lane(wq[...])

    @pl.loop(0, slabs)
    def _(w):
        acc[5] += fold(g_query[slab(w), :])
        grad[slab(w), :] = first_n[slab(w), :D] * g1 + b1

    d_wq = mm_rows(grad[...], g_query[...])
    store(17, jnp.concatenate([d_wo[:, 256:], d_wq], 1))
    tick(4.0, 3)
    planned_3 = ticks(slabs, 0.45)

    @pl.loop(0, slabs)
    def _(w):
        g_att[slab(w), :] = mm_lane(pack_left(g_query[slab(w), :]), wq_l[...])
        run_at(w, planned_3)

    planned_4 = ticks(blocks, 0.3)

    @pl.loop(0, blocks)
    def _(b):
        which = kinds[first + b] * 2 + b % 2
        here_k = pl.ds(pl.multiple_of(b * KPAD, 8), KPAD)
        high, low = split(jnp.concatenate([g_patch[sub, here_k, :] for sub in range(4)], 0))
        pick = table[which]
        dims = (((0,), (0,)), ((), ()))
        moved = lax.dot_general(pick, high, dims, preferred_element_type=f32)
        moved = moved + lax.dot_general(pick, low, dims, preferred_element_type=f32)
        g_att[pl.ds(window(b), WIN), :] += moved
        run_at(b, planned_4)

    planned_5 = ticks(slabs, 0.3)

    @pl.loop(0, slabs)
    def _(w):
        n, scale = first_n[slab(w), :D], first_n[slab(w), D : D + 1]
        g = g_att[slab(w), :]
        acc[6] += fold(g * n)
        acc[7] += fold(g)
        grad[slab(w), :] = g_after[slab(w), :] + norm_back(g * g1, n, scale)
        run_at(w, planned_5)

    order = (acc[6], acc[7], acc[5], acc[4], acc[2], acc[3], acc[1], acc[0], sums[0], sums[1], sums[2])
    value = jnp.concatenate([jnp.sum(x, 0, keepdims=True) for x in order] + [jnp.zeros((5, D), f32)], 0)
    value = jnp.concatenate([value, value[:, 256:]], 1)
    for t in range(3):
        small_sum[0, 16 * t : 16 * t + 16, :] = value[:, 128 * t : 128 * t + 128]
    exchange = Exchange(wires, small_sum, small_got)
    plan.add([exchange])
    run_steps(plan.rest())
    for t in range(3):
        small[:, 128 * t : 128 * t + 128] = small_sum[exchange.last, 16 * t : 16 * t + 16, :]


def attention_backward(pairs, cores, kinds, g_after, marks, vecs, wq, wr, wkv, wo, saved, sums, ff_pack):
    rows = g_after.shape[0]
    blocks = rows // BLOCK
    krows = blocks * KPAD
    bits = pairs.bit_length() - 1
    ff_total, total = sum_rows(pairs, cores)
    slots = 15 * (3 + 3 * bits)
    vm = pl.BlockSpec(memory_space=pltpu.VMEM)
    first_n, *saved = saved
    return pl.pallas_call(
        partial(backward_kernel, pairs, cores),
        out_shape=(
            jax.ShapeDtypeStruct((rows, D), f32),
            jax.ShapeDtypeStruct((ff_total, 128), f32),
            jax.ShapeDtypeStruct((cores, total, 128), f32),
            jax.ShapeDtypeStruct((16, 3 * 128), f32),
        ),
        in_specs=[pl.BlockSpec(memory_space=pltpu.SMEM)] + [vm] * 20 + [pl.BlockSpec(memory_space=pl.ANY)],
        out_specs=(vm,) * 4,
        scratch_shapes=[
            pltpu.VMEM((D, 1024), bf16),
            pltpu.VMEM((D, 1024), bf16),
            pltpu.VMEM((D, 1024), bf16),
            pltpu.VMEM((D, 1024), bf16),
            pltpu.VMEM((4, 1024, D), bf16),
            pltpu.VMEM((rows, D), f32),
            pltpu.VMEM((rows, D), f32),
            pltpu.VMEM((krows, D), f32),
            pltpu.VMEM((krows, D), f32),
            pltpu.VMEM((4, krows, D), f32),
            pltpu.VMEM((blocks, WIN, 256), f32),
            pltpu.VMEM((3, 256, 128), f32),
            pltpu.VMEM((3, 256, 128), f32),
            pltpu.VMEM((3, 256, 128), f32),
            pltpu.VMEM((8, 8, D), f32),
            pltpu.VMEM((ff_total, 128), f32),
            pltpu.VMEM((ff_total, 128), f32),
            pltpu.VMEM((ff_total, 128), f32),
            pltpu.VMEM((cores, total, 128), f32),
            pltpu.VMEM((total, 128), f32),
            pltpu.VMEM((total, 128), f32),
            pltpu.VMEM((bits + cores, 48, 128), f32),
            pltpu.VMEM((bits + cores, 48, 128), f32),
            pltpu.SemaphoreType.DMA((slots,)),
            pltpu.SemaphoreType.DMA((slots,)),
        ],
        compiler_params=pltpu.CompilerParams(
            collective_id=0 if pairs * cores > 1 else None, has_side_effects=True, vmem_limit_bytes=63 * MIB
        ),
        name="attention_back",
    )(
        kinds,
        first_n,
        g_after,
        marks,
        jnp.asarray(gather_table(), bf16),
        vecs[0],
        vecs[1],
        vecs[4],
        vecs[5],
        wq,
        wr,
        wkv,
        wo,
        *saved,
        sums,
        ff_pack,
    )


def unpack_kernel(grad, ff, rest, small, grad_t, d_we, d_ws, d_dw, d_be, d_bd, d_wr, d_wkv, d_wq, d_wo, *lines):
    cores = rest.shape[0]
    part = D // cores
    grad_t[...] = grad[...].T
    span = 2 * D + 16
    for t in range(d_we.shape[1] // 128):
        lanes = slice(128 * t, 128 * t + 128)
        d_we[:, lanes] = ff[t * span : t * span + D, :]
        d_ws[:, lanes] = ff[t * span + D : t * span + 2 * D, :]
        d_dw[:, lanes] = ff[t * span + 2 * D : t * span + 2 * D + 9, :]
    for row, ref in ((9, d_be), (10, d_bd)):
        at = 2 * D + row
        parts = [ff[t * span + at : t * span + at + 1, :] for t in range(d_we.shape[1] // 128)]
        ref[...] = jnp.concatenate(parts, 1).reshape(-1)
    for i, ref in enumerate(lines):
        ref[...] = small[i : i + 1, :D].reshape(-1)

    def tile(k):
        return jnp.concatenate([rest[h, k * part : k * part + part, :] for h in range(cores)], 0)

    for t in range(10):
        d_wr[:, 128 * t : 128 * t + 128] = tile(2 + t)
    for t in range(5):
        d_wkv[:, 128 * t : 128 * t + 128] = tile(12 + t)
    mixed = jnp.concatenate([tile(17 + t) for t in range(3)], 1)
    d_wo[...] = jnp.concatenate([tile(0), tile(1), mixed[:, :64]], 1)
    d_wq[...] = mixed[:, 64:]


def unpack(grad, ff, rest, small):
    cores = rest.shape[0]
    rows = grad.shape[0]
    chans = FF // cores
    vm = pl.BlockSpec(memory_space=pltpu.VMEM)
    shapes = [(D, rows), (D, chans), (D, chans), (9, chans), (chans,), (chans,)]
    shapes += [(D, 4 * D), (D, 2 * D), (D, D), (D, D)] + [(D,)] * 11
    return pl.pallas_call(
        unpack_kernel,
        out_shape=tuple(jax.ShapeDtypeStruct(x, f32) for x in shapes),
        in_specs=[vm] * 4,
        out_specs=(vm,) * len(shapes),
        compiler_params=pltpu.CompilerParams(vmem_limit_bytes=60 * MIB),
        name="unpack",
    )(grad, ff, rest, small)


def body(
    pairs,
    cores,
    tokens,
    block_kind,
    first_gain,
    first_bias,
    query_weight,
    query_bias,
    reduce_weight,
    reduce_bias,
    reduce_gain,
    reduce_shift,
    keyval_weight,
    value_bias,
    output_weight,
    output_bias,
    second_gain,
    second_shift,
    expand_weight,
    expand_bias,
    depth_weight,
    depth_bias,
    shrink_weight,
    shrink_bias,
    cotangent,
):
    own_taps = jnp.concatenate(
        [depth_weight, expand_bias[None], depth_bias[None], jnp.zeros((5, expand_bias.shape[0]), f32)], 0
    )
    hidden = [lax.all_gather(x, "hidden", axis=0) for x in (expand_weight, shrink_weight.T, own_taps)]
    vecs = (
        first_gain,
        first_bias,
        query_bias,
        reduce_bias,
        reduce_gain,
        reduce_shift,
        value_bias,
        output_bias,
    )
    late = (second_gain, second_shift, shrink_bias)
    weights = (query_weight, reduce_weight.T, keyval_weight, output_weight)
    after, marks, *saved = attention_forward(block_kind, tokens.T, vecs, *weights)
    result_t, g_after, ff_pack, sums = feed_forward(after, cotangent.T, marks, late, hidden)
    grad, ff_sum, rest, small = attention_backward(
        pairs, cores, block_kind, g_after, marks, vecs, *weights, saved, sums, ff_pack.reshape(-1, 128)
    )
    outs = unpack(grad, ff_sum, rest, small)
    grad_t, d_we, d_ws, d_dw, d_be, d_bd, d_wr, d_wkv, d_wq, d_wo, *small = outs
    return (
        result_t.T,
        grad_t.T,
        small[0],
        small[1],
        d_wq,
        small[2],
        d_wr.T,
        small[3],
        small[4],
        small[5],
        d_wkv,
        small[6],
        d_wo,
        small[7],
        small[8],
        small[9],
        d_we,
        d_be,
        d_dw,
        d_bd,
        d_ws.T,
        small[10],
    )


def solution(mesh):
    both = P(("dp", "hidden"), None)
    cols = P(None, "hidden")
    chan = P("hidden")
    deep = P("hidden", None)
    whole = P()
    return jax.shard_map(
        partial(body, mesh.shape["dp"], mesh.shape["hidden"]),
        mesh=mesh,
        in_specs=(both,) + (whole,) * 15 + (cols, chan, cols, chan, deep, whole, both),
        out_specs=(both, both) + (whole,) * 14 + (cols, chan, cols, chan, deep, whole),
        check_vma=False,
    )
```

```python
from functools import partial

import jax
import jax.numpy as jnp
import numpy as np
from jax import lax
from jax.experimental import pallas as pl
from jax.experimental.pallas import tpu as pltpu
from jax.sharding import PartitionSpec as P

HEADS = 5
HEAD = 64
BLOCK = 196
GRID = 14
SMALL = 6
SMALL_IMGS = 5
KVB = 49
D = 320
FF = 1280
KPAD = 56
WIN = 208
ODD = 184
CHUNK = 256
CHUNKS = FF // CHUNK
SLAB = 224
PAD = 16
MIB = 1024 * 1024

f32 = jnp.float32
bf16 = jnp.bfloat16
MESH = pl.DeviceIdType.MESH


def gather_table():
    out = np.zeros((2, 2, 4 * KPAD, WIN), np.float32)
    for kind in range(2):
        for parity in range(2):
            off = 12 * parity
            for a in range(2):
                for b in range(2):
                    for key in range(KVB):
                        if kind == 0:
                            i, j = divmod(key, GRID // 2)
                            spot = (2 * i + a) * GRID + 2 * j + b
                        else:
                            if key >= 45:
                                continue
                            image, rest = divmod(key, 9)
                            i, j = divmod(rest, 3)
                            spot = image * 36 + (2 * i + a) * SMALL + 2 * j + b
                        out[kind, parity, (2 * a + b) * KPAD + key, off + spot] = 1.0
    return out.reshape(4, 4 * KPAD, WIN)


def score_table():
    out = np.full((2, 2, WIN, 256), -1e30, np.float32)
    for kind in range(2):
        for parity in range(2):
            off = 12 * parity
            for row in range(WIN):
                local = row - off
                for key in range(KVB):
                    if kind == 0 or local < 0 or local >= BLOCK:
                        good = True
                    else:
                        good = key < 45 and key // 9 == min(local // 36, 4)
                    if good:
                        for head in range(HEADS):
                            out[kind, parity, row, head * KVB + key] = 0.0
    return out.reshape(4, WIN, 256)


def row_table():
    out = np.zeros((2, 2, WIN, 128), np.float32)
    for parity in range(2):
        off = 12 * parity
        for row in range(BLOCK):
            i, j = divmod(row, GRID)
            out[0, parity, off + row, :7] = (1, j > 0, j < 13, i > 0, 0, i < 13, 0)
            if row < 180:
                i, j = divmod(row % 36, SMALL)
                out[1, parity, off + row, :7] = (1, j > 0, j < 5, 0, i > 0, 0, i < 5)
    return out.reshape(4, WIN, 128)


def split(x):
    high = x.astype(bf16)
    return high, (x - high.astype(f32)).astype(bf16)


def pack_left(x):
    high = x.astype(bf16).astype(f32)
    low = x - high
    tail = jnp.concatenate([high[:, 256:], low[:, 256:]], 1).astype(bf16)
    high, low = high[:, :256].astype(bf16), low[:, :256].astype(bf16)
    return jnp.concatenate([high, low, high, tail, tail], 1)


def pack_short(x):
    high = x.astype(bf16).astype(f32)
    low = x - high
    tail = jnp.concatenate([high[:, 256:], low[:, 256:]], 1).astype(bf16)
    return jnp.concatenate([high[:, :256].astype(bf16), low[:, :256].astype(bf16), tail], 1)


def pack_lane(w):
    high = w.astype(bf16).astype(f32)
    low = w - high
    tail_high = jnp.concatenate([high[:, 256:], high[:, 256:]], 1).astype(bf16)
    tail_low = jnp.concatenate([low[:, 256:], low[:, 256:]], 1).astype(bf16)
    high, low = high[:, :256].astype(bf16), low[:, :256].astype(bf16)
    return jnp.concatenate([high, high, low, tail_high, tail_low], 1)


def pack_down(w):
    high, low = split(w)
    return jnp.concatenate(
        [high[:256], high[:256], low[:256], high[256:], high[256:], low[256:], low[256:]], 0
    )


def triple_left(x):
    high, low = split(x)
    return jnp.concatenate([high, low, high], 1)


def triple_down(w):
    high, low = split(w)
    return jnp.concatenate([high, high, low], 0)


def triple_lane(w):
    high, low = split(w)
    return jnp.concatenate([high, high, low], 1)


def mm(a, b):
    return jnp.dot(a, b, preferred_element_type=f32)


def mm_lane(a, b):
    return lax.dot_general(a, b, (((1,), (1,)), ((), ())), preferred_element_type=f32)


def mm_rows(a, b):
    left_high, left_low = split(a.T)
    high, low = split(b)
    return mm(left_high, high) + mm(left_low, high) + mm(left_high, low)


def norm_rows(x):
    center = jnp.sum(x, -1, keepdims=True) * (1.0 / D)
    centered = x - center
    spread = jnp.sum(centered * centered, -1, keepdims=True) * (1.0 / D)
    scale = lax.rsqrt(spread + 1e-06)
    return centered * scale, scale


def norm_back(h, n, scale):
    mean_h = jnp.sum(h, -1, keepdims=True) * (1.0 / D)
    mean_hn = jnp.sum(h * n, -1, keepdims=True) * (1.0 / D)
    return scale * (h - mean_h - n * mean_hn)


def fold(x):
    return jnp.sum(x.reshape(x.shape[0] // 8, 8, x.shape[1]), 0)


def window(block):
    return pl.multiple_of((block // 2) * (2 * BLOCK) + (block % 2) * ODD, 8)


def slab(w):
    return pl.ds(pl.multiple_of(w * SLAB, SLAB), SLAB)


def place_window(ref, block, value):
    start = window(block)

    @pl.when(block % 2 == 0)
    def _():
        ref[pl.ds(start, WIN), :] = value

    @pl.when(block % 2 == 1)
    def _():
        edge = ref[pl.ds(start + 8, 8), :]
        rows = lax.broadcasted_iota(jnp.int32, edge.shape, 0)
        ref[pl.ds(start + 8, 8), :] = jnp.where(rows < 4, edge, value[8:16])
        ref[pl.ds(start + 16, WIN - 16), :] = value[16:]


def head_block(rows_ref, block, out_ref):
    start = pl.multiple_of(block * KPAD, 8)
    for head in range(HEADS):
        tile = head // 2
        if tile < 2:
            value = rows_ref[pl.ds(start, KPAD), tile * 128 : tile * 128 + 128]
            lane = lax.broadcasted_iota(jnp.int32, value.shape, 1)
            value = jnp.where((lane >= 64) == (head % 2 == 1), value, 0.0)
        else:
            half = rows_ref[pl.ds(start, KPAD), 256:320]
            value = jnp.concatenate([half, half], 1)
        out_ref[tile, head * KVB : head * KVB + KVB, :] = value[:KVB]


def head_rows(ref):
    return jnp.concatenate([ref[0], ref[1], ref[2][:, :64]], 1)


def head_unblock(ref, value):
    ref[0] = value[:, :128]
    ref[1] = value[:, 128:256]
    ref[2] = jnp.concatenate([value[:, 256:], value[:, 256:]], 1)
    lane = lax.broadcasted_iota(jnp.int32, (KPAD, 128), 1)
    row = lax.broadcasted_iota(jnp.int32, (KPAD, 128), 0)
    tiles = []
    for tile in range(3):
        first = ref[tile, 2 * tile * KVB : 2 * tile * KVB + KPAD, :]
        if tile < 2:
            second = ref[tile, (2 * tile + 1) * KVB : (2 * tile + 1) * KVB + KPAD, :]
            first = jnp.where(lane < 64, first, second)
        tiles.append(jnp.where(row < KVB, first, 0.0))
    return jnp.concatenate([tiles[0], tiles[1], tiles[2][:, :64]], 1)


def head_lane(ref):
    parts = []
    for tile in range(3):
        high = ref[tile].astype(bf16)
        parts.append((high, (ref[tile] - high.astype(f32)).astype(bf16)))
    return jnp.concatenate(
        [parts[0][0], parts[1][0], parts[0][0], parts[1][0], parts[0][1], parts[1][1], parts[2][0], parts[2][1]], 1
    )


def head_of_lane(shape):
    lane = lax.broadcasted_iota(jnp.int32, shape, 1)
    return [lane < (head + 1) * KVB for head in range(HEADS - 1)]


def by_head(below, values):
    out = values[HEADS - 1]
    for head in range(HEADS - 2, -1, -1):
        out = jnp.where(below[head], values[head], out)
    return out


def per_head(below, x, empty, reduce):
    out = []
    for head in range(HEADS):
        here = x
        if head < HEADS - 1:
            here = jnp.where(below[head], here, empty)
        if head > 0:
            here = jnp.where(below[head - 1], empty, here)
        out.append(reduce(here, axis=1, keepdims=True))
    return by_head(below, [jnp.broadcast_to(v, x.shape) for v in out])


def line(ref):
    return ref[...].reshape(1, -1)


def own_first(blocks):
    return (lax.axis_index("dp") * lax.axis_size("hidden") + lax.axis_index("hidden")) * blocks


def attention_kernel(
    kinds,
    tokens_t,
    table,
    scores_mask,
    row_marks,
    first_gain,
    first_bias,
    query_bias,
    reduce_bias,
    reduce_gain,
    reduce_shift,
    value_bias,
    output_bias,
    wq,
    wr,
    wkv,
    wo,
    after,
    marks,
    first_n,
    query,
    attended,
    probs,
    keys,
    values,
    red_n,
    patches,
    wq_s,
    wo_s,
    wk_s,
    wv_s,
    wr_s,
    tokens,
    normed,
    kb,
    vb,
):
    blocks = probs.shape[0]
    slabs = tokens.shape[0] // SLAB
    first = own_first(blocks)
    g1, b1, bq, br = line(first_gain), line(first_bias), line(query_bias), line(reduce_bias)
    gr, sr, bv, bo = line(reduce_gain), line(reduce_shift), line(value_bias), line(output_bias)
    wq_s[...] = pack_down(wq[...])
    wo_s[...] = pack_down(wo[...])
    wk_s[...] = pack_down(wkv[:, :D])
    wv_s[...] = pack_down(wkv[:, D:])
    for sub in range(4):
        wr_s[sub] = pack_lane(wr[:, sub * D : sub * D + D])
    kb[...] = jnp.zeros_like(kb)
    vb[...] = jnp.zeros_like(vb)
    tokens[...] = tokens_t[...].T

    @pl.loop(0, slabs)
    def _(w):
        n, scale = norm_rows(tokens[slab(w), :])
        first_n[slab(w), :] = jnp.concatenate([n, jnp.broadcast_to(scale, (SLAB, 64))], 1)
        n = n * g1 + b1
        normed[slab(w), :] = n
        query[slab(w), :] = mm(pack_left(n), wq_s[...]) + bq

    @pl.loop(0, blocks)
    def _(b):
        which = kinds[first + b] * 2 + b % 2
        place_window(marks, b, row_marks[which])
        part = normed[pl.ds(window(b), WIN), :]
        high, low = split(part)
        pick = table[which]
        got = mm(pick, high) + mm(pick, low)
        rows = pl.ds(pl.multiple_of(b * KPAD, 8), KPAD)
        for sub in range(4):
            patches[sub, rows, :] = got[sub * KPAD : sub * KPAD + KPAD]

    @pl.loop(0, blocks * KPAD // SLAB)
    def _(w):
        acc = br + mm_lane(pack_left(patches[0, slab(w), :]), wr_s[0])
        for sub in range(1, 4):
            acc = acc + mm_lane(pack_left(patches[sub, slab(w), :]), wr_s[sub])
        n, scale = norm_rows(acc)
        red_n[slab(w), :] = jnp.concatenate([n, jnp.broadcast_to(scale, (SLAB, 64))], 1)
        packed = pack_left(n * gr + sr)
        keys[slab(w), :] = mm(packed, wk_s[...])
        values[slab(w), :] = mm(packed, wv_s[...]) + bv

    @pl.loop(0, blocks)
    def _(b):
        which = kinds[first + b] * 2 + b % 2
        head_block(keys, b, kb)
        head_block(values, b, vb)
        q = query[pl.ds(window(b), WIN), :]
        s = mm_lane(pack_left(q), head_lane(kb)) * (HEAD**-0.5) + scores_mask[which]
        below = head_of_lane(s.shape)
        e = jnp.exp(s - per_head(below, s, -3e38, jnp.max))
        p = e / per_head(below, e, 0.0, jnp.sum)
        probs[b] = p
        out = mm(triple_left(p), triple_down(head_rows(vb)))
        place_window(attended, b, out)

    @pl.loop(0, slabs)
    def _(w):
        branch = mm(pack_left(attended[slab(w), :]), wo_s[...]) + bo
        after[slab(w), :] = tokens[slab(w), :] + marks[slab(w), 0:1] * branch


def attention_forward(kinds, tokens_t, vecs, wq, wr, wkv, wo):
    rows = tokens_t.shape[1]
    blocks = rows // BLOCK
    krows = blocks * KPAD
    vm = pl.BlockSpec(memory_space=pltpu.VMEM)

    def shape(*dims):
        return jax.ShapeDtypeStruct(dims, f32)

    return pl.pallas_call(
        attention_kernel,
        out_shape=(
            shape(rows, D),
            shape(rows, 128),
            shape(rows, D + 64),
            shape(rows, D),
            shape(rows, D),
            shape(blocks, WIN, 256),
            shape(krows, D),
            shape(krows, D),
            shape(krows, D + 64),
            shape(4, krows, D),
        ),
        in_specs=[pl.BlockSpec(memory_space=pltpu.SMEM)] + [vm] * 16,
        out_specs=(vm,) * 10,
        scratch_shapes=[
            pltpu.VMEM((1024, D), bf16),
            pltpu.VMEM((1024, D), bf16),
            pltpu.VMEM((1024, D), bf16),
            pltpu.VMEM((1024, D), bf16),
            pltpu.VMEM((4, D, 1024), bf16),
            pltpu.VMEM((rows, D), f32),
            pltpu.VMEM((rows, D), f32),
            pltpu.VMEM((3, 256, 128), f32),
            pltpu.VMEM((3, 256, 128), f32),
        ],
        compiler_params=pltpu.CompilerParams(vmem_limit_bytes=60 * MIB),
        name="attention",
    )(
        kinds,
        tokens_t,
        jnp.asarray(gather_table(), bf16),
        jnp.asarray(score_table()),
        jnp.asarray(row_table()),
        *vecs,
        wq,
        wr,
        wkv,
        wo,
    )


ERF_P = 0.3275911
ERF = (0.254829592, -0.284496736, 1.421413741, -1.453152027, 1.061405429)


def gelu_pair(x):
    size = jnp.abs(x)
    d = 1.0 + (ERF_P * 0.7071067811865476) * size
    t = pl.reciprocal(d, approx=True)
    t = t * (2.0 - d * t)
    e = jnp.exp(-0.5 * (x * x))
    poly = t * (ERF[0] + t * (ERF[1] + t * (ERF[2] + t * (ERF[3] + t * ERF[4]))))
    tail = 0.5 * (poly * e)
    phi = jnp.where(x < 0.0, tail, 1.0 - tail)
    return x * phi, phi + x * (0.3989422804014327 * e)


def has_left(r):
    return r % GRID > 0, r < 180 and r % SMALL > 0


def has_right(r):
    return r % GRID < GRID - 1, r < 180 and r % SMALL < SMALL - 1


def has_up(r):
    return r >= GRID, r < 180 and r % 36 >= SMALL


def has_down(r):
    return r < BLOCK - GRID, r < 180 and r % 36 < 30


def total_of(values):
    values = [v for v in values if v is not None]
    out = values[0]
    for v in values[1:]:
        out = out + v
    return out


def forward_kernel(
    kinds,
    after,
    cot_t,
    second_gain,
    second_shift,
    shrink_bias,
    own_we,
    own_ws,
    own_taps,
    result_t,
    g_after,
    pack,
    sums,
    we_s,
    we_l,
    ws_s,
    ws_l,
    result,
    g_second,
    by_block,
    by_place,
    taps,
    second,
    branch,
    second_t,
    branch_t,
    xs0,
    xs1,
    nx1,
    ga0,
    ga1,
    ng1,
    y0,
    yu,
    yd,
    act,
    gx,
    held_act,
    held_gx,
    sem,
):
    rows = after.shape[0]
    part = rows // 2
    per = FF // 128 // own_we.shape[0]
    g2, s2, bs = line(second_gain), line(second_shift), line(shrink_bias)
    first = own_first(8)
    block = lax.broadcasted_iota(jnp.int32, (8, 128), 0)
    kind = jnp.zeros((8, 128), jnp.int32)
    for i in range(8):
        kind = jnp.where(block == i, kinds[first + i], kind)
    zero_kind = kind == 0
    k0 = jnp.where(zero_kind, 1.0, 0.0)
    k1 = 1.0 - k0

    loads = []
    for tile in range(FF // 128):
        lanes = pl.ds((tile % per) * 128, 128)
        for i, (source, low, size) in enumerate(((own_we, 0, D), (own_ws, D, D), (own_taps, 2 * D, 16))):
            loads.append(
                pltpu.make_async_copy(
                    source.at[tile // per, :, lanes], pack.at[tile, pl.ds(low, size)], sem.at[3 * tile + i]
                )
            )
    for load in loads:
        load.start()

    held_act[...] = jnp.zeros_like(held_act)
    held_gx[...] = jnp.zeros_like(held_gx)
    sums[...] = jnp.zeros_like(sums)

    def tiles_of(x):
        return x[:, :128], x[:, 128:256], jnp.concatenate([x[:, 256:], x[:, 256:]], 1)

    def to_places(out):
        for t in range(3):
            for i in range(8):
                by_place[t, pl.ds(i, BLOCK, stride=8), :] = by_block[t, i * BLOCK : (i + 1) * BLOCK, :]

        @pl.loop(0, rows // SLAB)
        def _(w):
            out[slab(w), :] = joined(by_place, slab(w))

    def to_blocks(source):
        @pl.loop(0, rows // SLAB)
        def _(w):
            for t, value in enumerate(tiles_of(source[slab(w), :])):
                by_place[t, slab(w), :] = value

        for t in range(3):
            for i in range(8):
                by_block[t, i * BLOCK : (i + 1) * BLOCK, :] = by_place[t, pl.ds(i, BLOCK, stride=8), :]

    def joined(ref, at):
        return jnp.concatenate([ref[0, at, :], ref[1, at, :], ref[2, at, :][:, :64]], 1)

    for t in range(3):
        low, high = 128 * t, min(128 * t + 128, D)
        value = cot_t[low:high, :].T
        by_block[t] = value if high - low == 128 else jnp.concatenate([value, value], 1)
    to_places(result)

    @pl.loop(0, rows // SLAB)
    def _(w):
        for t, value in enumerate(tiles_of(after[slab(w), :])):
            by_block[t, slab(w), :] = value

    to_places(g_second)

    g_after[...] = result[...]
    dead = 180 * 8
    result[dead:, :] = (result[dead:, :].reshape(BLOCK - 180, 8, D) * k0[:, :1]).reshape(rows - dead, D)

    @pl.loop(0, rows // SLAB)
    def _(w):
        a = g_second[slab(w), :]
        for t, value in enumerate(tiles_of(a)):
            by_block[t, slab(w), :] = value
        n, _ = norm_rows(a)
        value = n * g2 + s2
        g_second[slab(w), :] = value
        second[slab(w), :] = pack_short(value)
        grad = result[slab(w), :]
        sums[2] += fold(grad)
        branch[slab(w), :] = pack_short(grad)

    for source, turned in ((g_second, second_t), (result, branch_t)):
        high, low = split(source[...].T)
        turned[...] = jnp.concatenate([high, low, high], 1)
    result[...] = jnp.zeros_like(result)
    g_second[...] = jnp.zeros_like(g_second)

    for load in loads:
        load.wait()
    for c in range(CHUNKS):
        for which, (down, lane) in enumerate(((we_s, we_l), (ws_s, ws_l))):
            value = jnp.concatenate([pack[2 * c + t, which * D : which * D + D, :] for t in range(2)], 1)
            high, low = split(value)
            down[c] = jnp.concatenate([high, low], 0)
            lane[c] = jnp.concatenate([high, low], 1)
        for t in range(2):
            for k in range(11):
                taps[c, t, k] = jnp.broadcast_to(pack[2 * c + t, 2 * D + k : 2 * D + k + 1, :], (8, 128))

    def own(h):
        return slice(h * part, (h + 1) * part)

    def left(ref, h):
        x = ref[own(h), :]
        return jnp.concatenate([x[:, :512], x[:, :256], x[:, 512:], x[:, 512:]], 1)

    def deep(ref, c):
        x = ref[c]
        return jnp.concatenate(
            [x[:256], x[:256], x[D : D + 256], x[256:D], x[256:D], x[D + 256 :], x[D + 256 :]], 0
        )

    def expand_task(c, h, outs):
        e = mm(left(second, h), deep(we_s, c))
        for t in range(2):
            outs[t][own(h), :] = e[:, 128 * t : 128 * t + 128] + taps[c, t, 9][0:1]

    def active_grad_task(c, h, outs):
        g = mm(left(branch, h), deep(ws_s, c))
        for t in range(2):
            outs[t][own(h), :] = g[:, 128 * t : 128 * t + 128]

    def out_task(c, h, source, lane, out):
        x = source[own(h), :]
        weight = lane[c]
        out[own(h), :] += mm_lane(
            jnp.concatenate([x, x[:, :256]], 1), jnp.concatenate([weight[:, :256], weight], 1)
        )

    def weight_task(c, source, turned, row):
        high, low = source[:, :256], source[:, 256:]
        value = mm(turned[...], jnp.concatenate([high, high, low], 0))
        for t in range(2):
            pack[2 * c + t, row : row + D, :] = value[:, 128 * t : 128 * t + 128]

    def early_tasks(c, x_outs, g_outs):
        return [partial(expand_task, c, h, x_outs) for h in range(2)] + [
            partial(active_grad_task, c, h, g_outs) for h in range(2)
        ]

    def late_tasks(c):
        return [
            partial(out_task, c, 0, held_act, ws_l, result),
            partial(out_task, c, 0, held_gx, we_l, g_second),
            partial(out_task, c, 1, held_act, ws_l, result),
            partial(out_task, c, 1, held_gx, we_l, g_second),
        ]

    def weight_tasks(c):
        return [
            partial(weight_task, c, held_act, branch_t, D),
            partial(weight_task, c, held_gx, second_t, 0),
        ]

    def at(r):
        return slice(8 * r, 8 * r + 8)

    def gated(value, ok):
        if ok[0] and ok[1]:
            return value
        if ok[0]:
            return value * k0
        return value * k1 if ok[1] else None

    def picked(ref, r, ok, sign):
        if ok[0] and ok[1]:
            return jnp.where(zero_kind, ref[at(r + sign * GRID), :], ref[at(r + sign * SMALL), :])
        if ok[0]:
            return ref[at(r + sign * GRID), :] * k0
        return ref[at(r + sign * SMALL), :] * k1 if ok[1] else None

    def put_split(ref, t, r, pair):
        high, low = split(jnp.concatenate(pair, 0))
        here = slice(8 * r, 8 * r + 16)
        ref[here, 128 * t : 128 * t + 128] = high
        ref[here, 256 + 128 * t : 384 + 128 * t] = low

    def item(c, t, x, g, tasks):
        tap = [taps[c, t, k] for k in range(11)]
        totals = [jnp.zeros((8, 128), f32)] * 11

        def columns(r, near):
            return [
                gated(near(r - 1), has_left(r)) if r > 0 else None,
                near(r),
                gated(near(r + 1), has_right(r)) if r + 1 < BLOCK else None,
            ]

        def mix(values, ks, more=()):
            return total_of([None if v is None else v * tap[k] for v, k in zip(values, ks)] + list(more))

        def loader():
            kept = {}

            def near(r):
                if r not in kept:
                    kept[r] = x[at(r), :]
                return kept[r]

            return near

        ahead, behind = loader(), loader()
        moved_back = {}
        every = {}
        count = (BLOCK + 30) // 2
        slots = {round((i + 0.5) * count / len(tasks)): task for i, task in enumerate(tasks)}
        for step in range(count):
            for r in (2 * step, 2 * step + 1):
                if r < BLOCK:
                    cols = columns(r, ahead)
                    yu[at(r), :] = mix(cols, (0, 1, 2))
                    y0[at(r), :] = mix(cols, (3, 4, 5), (tap[10],))
                    yd[at(r), :] = mix(cols, (6, 7, 8))
            r = 2 * step - 14
            if 0 <= r < BLOCK:
                conv = [
                    total_of([y0[at(s), :], picked(yu, s, has_up(s), -1), picked(yd, s, has_down(s), 1)])
                    for s in (r, r + 1)
                ]
                active, slope = gelu_pair(jnp.concatenate(conv, 0))
                put_split(act, t, r, [active[:8], active[8:]])
                here = slice(8 * r, 8 * r + 16)
                g[here, :] = g[here, :] * slope
            for r in (2 * step - 28, 2 * step - 27):
                if 0 <= r < BLOCK:
                    same = g[at(r), :]
                    moved = [picked(g, r, has_down(r), 1), same, picked(g, r, has_up(r), -1)]
                    cols = columns(r, behind)
                    totals[10] = totals[10] + same
                    for p in range(3):
                        for q in range(3):
                            if moved[p] is not None and cols[q] is not None:
                                totals[3 * p + q] = totals[3 * p + q] + moved[p] * cols[q]
                    moved_back[r] = [mix(moved, ks) for ks in ((0, 3, 6), (1, 4, 7), (2, 5, 8))]
            r = 2 * step - 30
            if 0 <= r < BLOCK:
                pair = []
                for s in (r, r + 1):
                    value = total_of(
                        [
                            moved_back[s][1],
                            gated(moved_back[s - 1][2], has_left(s)) if s > 0 else None,
                            gated(moved_back[s + 1][0], has_right(s)) if s + 1 < BLOCK else None,
                        ]
                    )
                    totals[9] = totals[9] + value
                    pair.append(value)
                put_split(gx, t, r, pair)
            if step in slots:
                slots[step]()
        for k in range(11):
            pack[2 * c + t, 2 * D + k : 2 * D + k + 1, :] = jnp.sum(totals[k], 0, keepdims=True)

    for task in early_tasks(0, (xs0, xs1), (ga0, ga1)):
        task()

    @pl.loop(0, CHUNKS)
    def _(c):
        before = jnp.maximum(c - 1, 0)
        item(c, 0, xs0, ga0, late_tasks(before) + weight_tasks(before)[:1])
        later = jnp.minimum(c + 1, CHUNKS - 1)
        item(c, 1, xs1, ga1, early_tasks(later, (xs0, nx1), (ga0, ng1)) + weight_tasks(before)[1:])
        xs1[...] = nx1[...]
        ga1[...] = ng1[...]
        held_act[...] = act[...]
        held_gx[...] = gx[...]

    for task in late_tasks(CHUNKS - 1) + weight_tasks(CHUNKS - 1):
        task()
    for c in range(CHUNKS):
        for t in range(2):
            pack[2 * c + t, 2 * D + 11 : 2 * D + 16, :] = jnp.zeros((5, 128), f32)

    result[dead:, :] = ((result[dead:, :] + bs).reshape(BLOCK - 180, 8, D) * k0[:, :1]).reshape(rows - dead, D) - bs

    @pl.loop(0, rows // SLAB)
    def _(w):
        a = joined(by_block, slab(w))
        result[slab(w), :] = a + (result[slab(w), :] + bs)
        n, scale = norm_rows(a)
        g = g_second[slab(w), :]
        sums[0] += fold(g * n)
        sums[1] += fold(g)
        g_second[slab(w), :] = g_after[slab(w), :] + norm_back(g * g2, n, scale)

    to_blocks(result)
    for t in range(3):
        low, high = 128 * t, min(128 * t + 128, D)
        result_t[low:high, :] = by_block[t].T[: high - low]
    to_blocks(g_second)

    @pl.loop(0, rows // SLAB)
    def _(w):
        g_after[slab(w), :] = joined(by_block, slab(w))


def feed_forward(kinds, after, cot_t, vecs, weights):
    rows = after.shape[0]
    vm = pl.BlockSpec(memory_space=pltpu.VMEM)
    tile = pltpu.VMEM((rows, 128), f32)
    half = pltpu.VMEM((rows, 2 * CHUNK), bf16)
    return pl.pallas_call(
        forward_kernel,
        out_shape=(
            jax.ShapeDtypeStruct((D, rows), f32),
            jax.ShapeDtypeStruct((rows, D), f32),
            jax.ShapeDtypeStruct((2 * CHUNKS, 2 * D + 16, 128), f32),
            jax.ShapeDtypeStruct((3, 8, D), f32),
        ),
        in_specs=[pl.BlockSpec(memory_space=pltpu.SMEM)] + [vm] * 5 + [pl.BlockSpec(memory_space=pl.ANY)] * 3,
        out_specs=(vm,) * 4,
        scratch_shapes=[
            pltpu.VMEM((CHUNKS, 2 * D, CHUNK), bf16),
            pltpu.VMEM((CHUNKS, D, 2 * CHUNK), bf16),
            pltpu.VMEM((CHUNKS, 2 * D, CHUNK), bf16),
            pltpu.VMEM((CHUNKS, D, 2 * CHUNK), bf16),
            pltpu.VMEM((rows, D), f32),
            pltpu.VMEM((rows, D), f32),
            pltpu.VMEM((3, rows, 128), f32),
            pltpu.VMEM((3, rows, 128), f32),
            pltpu.VMEM((CHUNKS, 2, 11, 8, 128), f32),
            pltpu.VMEM((rows, 640), bf16),
            pltpu.VMEM((rows, 640), bf16),
            pltpu.VMEM((D, 3 * rows), bf16),
            pltpu.VMEM((D, 3 * rows), bf16),
        ]
        + [tile] * 9
        + [half] * 4
        + [pltpu.SemaphoreType.DMA((6 * CHUNKS,))],
        compiler_params=pltpu.CompilerParams(vmem_limit_bytes=63 * MIB),
        name="feed_forward",
    )(kinds, after, cot_t, *vecs, *weights)


class Wires:
    def __init__(self, pairs, cores, send, recv):
        self.bits = pairs.bit_length() - 1
        self.cores = cores
        self.me, self.core = lax.axis_index("dp"), lax.axis_index("hidden")
        self.other = cores - 1 - self.core
        self.send, self.recv, self.used = send, recv, 0

    def groups(self):
        rest = list(range(2, self.bits))
        return [(k,) for k in range(min(2, self.bits))] + [tuple(rest[i : i + 2]) for i in range(0, len(rest), 2)]

    def bit(self, k):
        return (self.me // (1 << k)) % 2

    def peer(self, group, j):
        flips = [(1 - 2 * self.bit(k)) * (1 << k) for i, k in enumerate(group) if (j >> i) & 1]
        return (sum(flips, self.me), self.core)

    def place(self, group, j):
        bits = [(1 - self.bit(k) if (j >> i) & 1 else self.bit(k)) * (1 << i) for i, k in enumerate(group)]
        return sum(bits[1:], bits[0])

    def greet(self):
        peers = [self.peer(group, j) for group in self.groups() for j in range(1, 1 << len(group))]
        if self.cores > 1:
            peers.append((self.me, self.other))
        if not peers:
            return
        barrier = pltpu.get_barrier_semaphore()
        for target in peers:
            pl.semaphore_signal(barrier, inc=1, device_id=target, device_id_type=MESH)
        pl.semaphore_wait(barrier, len(peers))

    def copy(self, src, dst, target):
        slot = self.used
        self.used += 1
        return pltpu.make_async_remote_copy(
            src_ref=src,
            dst_ref=dst,
            send_sem=self.send.at[slot],
            recv_sem=self.recv.at[slot],
            device_id=target,
            device_id_type=MESH,
        )

    def local(self, src, dst):
        slot = self.used
        self.used += 1
        return pltpu.make_async_copy(src, dst, self.send.at[slot])

    def sibling(self, src, dst):
        return self.copy(src, dst, (self.me, self.other))


def rows_of(start, size):
    return pl.ds(pl.multiple_of(start, 8), size)


class Chain:
    def __init__(self, wires, acc, near, got, full, base, rows, order, opening, closing):
        self.stages, self.costs = [], []
        whole = pl.ds(base, rows)
        scale = 512 * wires.cores / LINK

        def meet():
            if near is not None:
                acc[whole, :] = acc[whole, :] + near[whole, :]

        start, size, spot = base + 0 * wires.me, rows, base
        pending, action = opening, meet
        self.stages.append(([], None, opening))
        self.costs.append(("core", rows * 512 / CORE_LINK))
        held = []
        for group in order:
            many = 1 << len(group)
            size //= many
            keep = start + wires.place(group, 0) * size
            copies, lands = [], []
            for j in range(1, many):
                land = pl.ds(spot, size)
                spot += size
                give = start + wires.place(group, j) * size
                copies.append(wires.copy(acc.at[rows_of(give, size)], got.at[land], wires.peer(group, j)))
                lands.append(land)
            self.stages.append((pending, action, copies))
            self.costs.append((group, scale * size * (1 if many == 2 else many)))

            def add(keep=keep, lands=lands, size=size):
                value = acc[rows_of(keep, size), :]
                for land in lands:
                    value = value + got[land, :]
                acc[rows_of(keep, size), :] = value

            pending, action = copies, add
            held.append((group, start))
            start = keep
        last, last_start, last_size = action, start, size

        def settle():
            last()
            full[rows_of(last_start, last_size), :] = acc[rows_of(last_start, last_size), :]

        action = settle
        for group, before in reversed(held):
            mine = rows_of(start, size)
            many = 1 << len(group)
            copies = [wires.copy(full.at[mine], full.at[mine], wires.peer(group, j)) for j in range(1, many)]
            self.stages.append((pending, action, copies))
            self.costs.append((group, scale * size * (1 if many == 2 else many)))
            pending, action = copies, None
            start, size = before, size * many
        if closing:
            self.stages.append((pending, action, closing))
            self.costs.append(("core", rows * 512 / CORE_LINK))
            pending, action = closing, None
        self.stages.append((pending, action, []))
        self.costs.append((None, 0.0))

    def run(self, stage):
        waits, action, starts = self.stages[stage]
        for c in waits:
            c.wait()
        if action is not None:
            action()
        for c in starts:
            c.start()


class Exchange(Chain):
    def __init__(self, wires, sums, got):
        partners = [((k,), wires.peer((k,), 1)) for k in range(wires.bits)]
        if wires.cores > 1:
            partners.insert(0, ("core", (wires.me, wires.other)))
        self.stages, self.costs = [], []
        pending, action = [], None
        for i, (name, target) in enumerate(partners):
            c = wires.copy(sums.at[i], got.at[i], target)
            self.stages.append((pending, action, [c]))
            self.costs.append((name, 0.5))

            def add(i=i):
                sums[i + 1] = sums[i] + got[i]

            pending, action = [c], add
        self.stages.append((pending, action, []))
        self.costs.append((None, 0.0))
        self.last = len(partners)


LINK = 100e3
CORE_LINK = 400e3
DELAY = 1.5
STEP_WORK = 0.1


class Plan:
    def __init__(self):
        self.now, self.free, self.going = 0.0, {}, []

    def add(self, chains):
        self.going += [[self.now, c, 0] for c in chains]

    def after(self, us):
        self.now += us
        due = []
        while True:
            ready = [g for g in self.going if g[0] <= self.now]
            if not ready:
                return due
            due.append(self.take(min(ready, key=lambda g: g[0])))

    def take(self, entry):
        done, chain, stage = entry
        self.now = max(self.now, done) + STEP_WORK
        link, us = chain.costs[stage]
        self.free[link] = max(self.free.get(link, 0.0), self.now) + us
        if stage + 1 == len(chain.stages):
            self.going.remove(entry)
        else:
            entry[0], entry[2] = self.free[link] + DELAY, stage + 1
        return chain, stage

    def rest(self):
        due = []
        while self.going:
            due.append(self.take(min(self.going, key=lambda g: g[0])))
        return due


def run_steps(steps):
    for chain, stage in steps:
        chain.run(stage)


def axis_orders(groups):
    return groups, groups[1::-1] + groups[2:], groups[2:] + groups[:2]


def cut(total, unit, parts):
    units = total // unit
    marks = sorted({0, units} | {round(units * x) for x in parts})
    return [(a * unit, b * unit) for a, b in zip(marks, marks[1:])]


def round_up(x, unit):
    return -(-x // unit) * unit


def sum_rows(pairs, cores):
    unit = 8 * pairs
    ff = round_up(2 * CHUNKS // cores * (2 * D + 16), unit)
    rest = round_up(20 * (D // cores), unit)
    return ff, rest


def backward_kernel(
    pairs,
    cores,
    kinds,
    first_n,
    g_after,
    marks,
    table,
    first_gain,
    first_bias,
    reduce_gain,
    reduce_shift,
    wq,
    wr,
    wkv,
    wo,
    query,
    attended,
    probs,
    keys,
    values,
    red_n,
    patches,
    sums,
    ff_pack,
    grad,
    ff_full,
    full,
    small,
    wq_l,
    wo_l,
    wk_l,
    wv_l,
    wr_l,
    g_att,
    g_query,
    g_keys,
    g_values,
    g_patch,
    g_scores,
    kb,
    vb,
    tmp,
    acc,
    ff_acc,
    ff_near,
    ff_got,
    big,
    near,
    got,
    small_sum,
    small_got,
    send,
    recv,
):
    blocks = probs.shape[0]
    rows = g_after.shape[0]
    slabs = rows // SLAB
    krows = blocks * KPAD
    first = own_first(blocks)
    part = D // cores
    g1, b1, gr, sr = line(first_gain), line(first_bias), line(reduce_gain), line(reduce_shift)

    wires = Wires(pairs, cores, send, recv)
    core = wires.core
    orders = axis_orders(wires.groups())
    unit = 8 * pairs
    ff_real = ff_pack.shape[0] // cores
    ff_total, total = ff_acc.shape[0], big.shape[1]
    if ff_total > ff_real:
        ff_acc[ff_real:, :] = jnp.zeros((ff_total - ff_real, 128), f32)
        ff_near[ff_real:, :] = jnp.zeros((ff_total - ff_real, 128), f32)
    if total > 20 * part:
        for h in range(cores):
            big[h, 20 * part :, :] = jnp.zeros((total - 20 * part, 128), f32)
    wires.greet()
    ff_chains = []
    for i, (low, high) in enumerate(cut(ff_total, unit, (4 / 26, 10 / 26, 16 / 26, 21 / 26))):
        size = min(high, ff_real) - low
        here = pl.ds(low, size)
        opening = [wires.local(ff_pack.at[rows_of(core * ff_real + low, size)], ff_acc.at[here])]
        if cores > 1:
            opening.append(wires.sibling(ff_pack.at[rows_of(wires.other * ff_real + low, size)], ff_near.at[here]))
        ff_chains.append(
            Chain(
                wires,
                ff_acc,
                ff_near if cores > 1 else None,
                ff_got,
                ff_full,
                low,
                high - low,
                orders[(2, 0, 1, 0, 1)[i]],
                opening,
                [],
            )
        )
    bounds = [2 * part, 12 * part, 17 * part]
    chains = []
    cuts = cut(total, unit, (2 / 25, 8 / 25, 13 / 25, 15 / 25, 18 / 25, 21 / 25, 23 / 25))
    for i, (low, high) in enumerate(cuts):
        here = pl.ds(low, high - low)
        opening, closing = [], []
        if cores > 1:
            opening = [wires.sibling(big.at[wires.other, here], near.at[here])]
            closing = [wires.sibling(full.at[core, here], full.at[core, here])]
        chain = Chain(
            wires,
            big.at[core],
            near if cores > 1 else None,
            got,
            full.at[core],
            low,
            high - low,
            orders[(0, 0, 1, 2, 0, 1, 0, 1)[i]],
            opening,
            closing,
        )
        chain.ready = sum(high > x for x in bounds)
        chains.append(chain)
    plan = Plan()
    plan.add(ff_chains)

    def tick(us, level=None):
        run_steps(plan.after(us))
        if level is not None:
            plan.add([c for c in chains if c.ready == level])
            run_steps(plan.after(0.0))

    def ticks(count, us):
        return [plan.after(us) for _ in range(count)]

    def run_at(index, planned):
        for i, steps in enumerate(planned):
            if steps:
                pl.when(index == i)(partial(run_steps, steps))

    def store(tile, value):
        for t in range(value.shape[1] // 128):
            for h in range(cores):
                big[h, (tile + t) * part : (tile + t + 1) * part, :] = value[
                    h * part : (h + 1) * part, 128 * t : 128 * t + 128
                ]

    tick(0.0)
    wo_l[...] = pack_lane(wo[...])
    wk_l[...] = pack_lane(wkv[:, :D])
    wv_l[...] = pack_lane(wkv[:, D:])
    kb[...] = jnp.zeros_like(kb)
    vb[...] = jnp.zeros_like(vb)
    acc[...] = jnp.zeros_like(acc)
    tick(2.0)
    planned_0 = ticks(slabs, 0.6)

    @pl.loop(0, slabs)
    def _(w):
        g = marks[slab(w), 0:1] * g_after[slab(w), :]
        grad[slab(w), :] = g
        acc[0] += fold(g)
        g_att[slab(w), :] = mm_lane(pack_left(g), wo_l[...])
        run_at(w, planned_0)

    d_wo = mm_rows(attended[...], grad[...])
    store(0, d_wo[:, :256])
    tick(3.5, 0)
    planned_1 = ticks(blocks, 1.8)

    @pl.loop(0, blocks)
    def _(b):
        head_block(values, b, vb)
        here = pl.ds(window(b), WIN)
        first_row = 12 * (b % 2)
        row = lax.broadcasted_iota(jnp.int32, (WIN, D), 0)
        inside = (row >= first_row) & (row < first_row + BLOCK)
        ga = jnp.where(inside, g_att[here, :], 0.0)
        p = probs[b]
        gp = mm_lane(pack_left(ga), head_lane(vb))
        below = head_of_lane(p.shape)
        gs = p * (gp - per_head(below, gp * p, 0.0, jnp.sum)) * (HEAD**-0.5)
        g_scores[b] = gs
        here_k = pl.ds(pl.multiple_of(b * KPAD, 8), KPAD)
        g_values[here_k, :] = head_unblock(tmp, mm_rows(p, ga))
        g_keys[here_k, :] = head_unblock(tmp, mm_rows(gs, query[here, :]))
        run_at(b, planned_1)


    @pl.loop(0, krows // SLAB)
    def _(w):
        gk, gv = g_keys[slab(w), :], g_values[slab(w), :]
        acc[1] += fold(gv)
        g = mm_lane(pack_left(gk), wk_l[...]) + mm_lane(pack_left(gv), wv_l[...])
        n = red_n[slab(w), :D]
        acc[2] += fold(g * n)
        acc[3] += fold(g)
        g = norm_back(g * gr, n, red_n[slab(w), D : D + 1])
        acc[4] += fold(g)
        grad[slab(w), :] = g

    tick(2.0)
    g_red = grad[0:krows, :]
    for pair in range(2):
        d_wr = jnp.concatenate([mm_rows(g_red, patches[2 * pair]), mm_rows(g_red, patches[2 * pair + 1])], 1)
        store(2 + 5 * pair, d_wr)
        tick(2.0, 1 if pair else None)
    reduced = red_n[:, :D] * gr + sr
    d_wk = mm_rows(reduced, g_keys[...])
    d_wv = mm_rows(reduced, g_values[...])
    store(12, jnp.concatenate([d_wk, d_wv], 1))
    tick(2.5, 2)
    for sub in range(4):
        wr_l[sub] = pack_down(wr[:, sub * D : sub * D + D])

    @pl.loop(0, krows // SLAB)
    def _(w):
        packed = pack_left(grad[slab(w), :])
        for sub in range(4):
            g_patch[sub, slab(w), :] = mm(packed, wr_l[sub])

    tick(2.0)
    planned_2 = ticks(blocks, 0.6)

    @pl.loop(0, blocks)
    def _(b):
        head_block(keys, b, kb)
        place_window(g_query, b, mm(triple_left(g_scores[b]), triple_down(head_rows(kb))))
        run_at(b, planned_2)

    wq_l[...] = pack_lane(wq[...])

    @pl.loop(0, slabs)
    def _(w):
        acc[5] += fold(g_query[slab(w), :])
        grad[slab(w), :] = first_n[slab(w), :D] * g1 + b1

    d_wq = mm_rows(grad[...], g_query[...])
    store(17, jnp.concatenate([d_wo[:, 256:], d_wq], 1))
    tick(4.0, 3)
    planned_3 = ticks(slabs, 0.45)

    @pl.loop(0, slabs)
    def _(w):
        g_att[slab(w), :] = mm_lane(pack_left(g_query[slab(w), :]), wq_l[...])
        run_at(w, planned_3)

    planned_4 = ticks(blocks, 0.3)

    @pl.loop(0, blocks)
    def _(b):
        which = kinds[first + b] * 2 + b % 2
        here_k = pl.ds(pl.multiple_of(b * KPAD, 8), KPAD)
        high, low = split(jnp.concatenate([g_patch[sub, here_k, :] for sub in range(4)], 0))
        pick = table[which]
        dims = (((0,), (0,)), ((), ()))
        moved = lax.dot_general(pick, high, dims, preferred_element_type=f32)
        moved = moved + lax.dot_general(pick, low, dims, preferred_element_type=f32)
        g_att[pl.ds(window(b), WIN), :] += moved
        run_at(b, planned_4)

    planned_5 = ticks(slabs, 0.3)

    @pl.loop(0, slabs)
    def _(w):
        n, scale = first_n[slab(w), :D], first_n[slab(w), D : D + 1]
        g = g_att[slab(w), :]
        acc[6] += fold(g * n)
        acc[7] += fold(g)
        grad[slab(w), :] = g_after[slab(w), :] + norm_back(g * g1, n, scale)
        run_at(w, planned_5)

    order = (acc[6], acc[7], acc[5], acc[4], acc[2], acc[3], acc[1], acc[0], sums[0], sums[1], sums[2])
    value = jnp.concatenate([jnp.sum(x, 0, keepdims=True) for x in order] + [jnp.zeros((5, D), f32)], 0)
    value = jnp.concatenate([value, value[:, 256:]], 1)
    for t in range(3):
        small_sum[0, 16 * t : 16 * t + 16, :] = value[:, 128 * t : 128 * t + 128]
    exchange = Exchange(wires, small_sum, small_got)
    plan.add([exchange])
    run_steps(plan.rest())
    for t in range(3):
        small[:, 128 * t : 128 * t + 128] = small_sum[exchange.last, 16 * t : 16 * t + 16, :]


def attention_backward(pairs, cores, kinds, g_after, marks, vecs, wq, wr, wkv, wo, saved, sums, ff_pack):
    rows = g_after.shape[0]
    blocks = rows // BLOCK
    krows = blocks * KPAD
    bits = pairs.bit_length() - 1
    ff_total, total = sum_rows(pairs, cores)
    slots = 15 * (3 + 3 * bits)
    vm = pl.BlockSpec(memory_space=pltpu.VMEM)
    first_n, *saved = saved
    return pl.pallas_call(
        partial(backward_kernel, pairs, cores),
        out_shape=(
            jax.ShapeDtypeStruct((rows, D), f32),
            jax.ShapeDtypeStruct((ff_total, 128), f32),
            jax.ShapeDtypeStruct((cores, total, 128), f32),
            jax.ShapeDtypeStruct((16, 3 * 128), f32),
        ),
        in_specs=[pl.BlockSpec(memory_space=pltpu.SMEM)] + [vm] * 20 + [pl.BlockSpec(memory_space=pl.ANY)],
        out_specs=(vm,) * 4,
        scratch_shapes=[
            pltpu.VMEM((D, 1024), bf16),
            pltpu.VMEM((D, 1024), bf16),
            pltpu.VMEM((D, 1024), bf16),
            pltpu.VMEM((D, 1024), bf16),
            pltpu.VMEM((4, 1024, D), bf16),
            pltpu.VMEM((rows, D), f32),
            pltpu.VMEM((rows, D), f32),
            pltpu.VMEM((krows, D), f32),
            pltpu.VMEM((krows, D), f32),
            pltpu.VMEM((4, krows, D), f32),
            pltpu.VMEM((blocks, WIN, 256), f32),
            pltpu.VMEM((3, 256, 128), f32),
            pltpu.VMEM((3, 256, 128), f32),
            pltpu.VMEM((3, 256, 128), f32),
            pltpu.VMEM((8, 8, D), f32),
            pltpu.VMEM((ff_total, 128), f32),
            pltpu.VMEM((ff_total, 128), f32),
            pltpu.VMEM((ff_total, 128), f32),
            pltpu.VMEM((cores, total, 128), f32),
            pltpu.VMEM((total, 128), f32),
            pltpu.VMEM((total, 128), f32),
            pltpu.VMEM((bits + cores, 48, 128), f32),
            pltpu.VMEM((bits + cores, 48, 128), f32),
            pltpu.SemaphoreType.DMA((slots,)),
            pltpu.SemaphoreType.DMA((slots,)),
        ],
        compiler_params=pltpu.CompilerParams(
            collective_id=0 if pairs * cores > 1 else None, has_side_effects=True, vmem_limit_bytes=63 * MIB
        ),
        name="attention_back",
    )(
        kinds,
        first_n,
        g_after,
        marks,
        jnp.asarray(gather_table(), bf16),
        vecs[0],
        vecs[1],
        vecs[4],
        vecs[5],
        wq,
        wr,
        wkv,
        wo,
        *saved,
        sums,
        ff_pack,
    )


def unpack_kernel(grad, ff, rest, small, grad_t, d_we, d_ws, d_dw, d_be, d_bd, d_wr, d_wkv, d_wq, d_wo, *lines):
    cores = rest.shape[0]
    part = D // cores
    grad_t[...] = grad[...].T
    span = 2 * D + 16
    for t in range(d_we.shape[1] // 128):
        lanes = slice(128 * t, 128 * t + 128)
        d_we[:, lanes] = ff[t * span : t * span + D, :]
        d_ws[:, lanes] = ff[t * span + D : t * span + 2 * D, :]
        d_dw[:, lanes] = ff[t * span + 2 * D : t * span + 2 * D + 9, :]
    for row, ref in ((9, d_be), (10, d_bd)):
        at = 2 * D + row
        parts = [ff[t * span + at : t * span + at + 1, :] for t in range(d_we.shape[1] // 128)]
        ref[...] = jnp.concatenate(parts, 1).reshape(-1)
    for i, ref in enumerate(lines):
        ref[...] = small[i : i + 1, :D].reshape(-1)

    def tile(k):
        return jnp.concatenate([rest[h, k * part : k * part + part, :] for h in range(cores)], 0)

    for t in range(10):
        d_wr[:, 128 * t : 128 * t + 128] = tile(2 + t)
    for t in range(5):
        d_wkv[:, 128 * t : 128 * t + 128] = tile(12 + t)
    mixed = jnp.concatenate([tile(17 + t) for t in range(3)], 1)
    d_wo[...] = jnp.concatenate([tile(0), tile(1), mixed[:, :64]], 1)
    d_wq[...] = mixed[:, 64:]


def unpack(grad, ff, rest, small):
    cores = rest.shape[0]
    rows = grad.shape[0]
    chans = FF // cores
    vm = pl.BlockSpec(memory_space=pltpu.VMEM)
    shapes = [(D, rows), (D, chans), (D, chans), (9, chans), (chans,), (chans,)]
    shapes += [(D, 4 * D), (D, 2 * D), (D, D), (D, D)] + [(D,)] * 11
    return pl.pallas_call(
        unpack_kernel,
        out_shape=tuple(jax.ShapeDtypeStruct(x, f32) for x in shapes),
        in_specs=[vm] * 4,
        out_specs=(vm,) * len(shapes),
        compiler_params=pltpu.CompilerParams(vmem_limit_bytes=60 * MIB),
        name="unpack",
    )(grad, ff, rest, small)


def body(
    pairs,
    cores,
    tokens,
    block_kind,
    first_gain,
    first_bias,
    query_weight,
    query_bias,
    reduce_weight,
    reduce_bias,
    reduce_gain,
    reduce_shift,
    keyval_weight,
    value_bias,
    output_weight,
    output_bias,
    second_gain,
    second_shift,
    expand_weight,
    expand_bias,
    depth_weight,
    depth_bias,
    shrink_weight,
    shrink_bias,
    cotangent,
):
    own_taps = jnp.concatenate(
        [depth_weight, expand_bias[None], depth_bias[None], jnp.zeros((5, expand_bias.shape[0]), f32)], 0
    )
    hidden = [lax.all_gather(x, "hidden", axis=0) for x in (expand_weight, shrink_weight.T, own_taps)]
    vecs = (
        first_gain,
        first_bias,
        query_bias,
        reduce_bias,
        reduce_gain,
        reduce_shift,
        value_bias,
        output_bias,
    )
    late = (second_gain, second_shift, shrink_bias)
    weights = (query_weight, reduce_weight.T, keyval_weight, output_weight)
    after, marks, *saved = attention_forward(block_kind, tokens.T, vecs, *weights)
    result_t, g_after, ff_pack, sums = feed_forward(block_kind, after, cotangent.T, late, hidden)
    grad, ff_sum, rest, small = attention_backward(
        pairs, cores, block_kind, g_after, marks, vecs, *weights, saved, sums, ff_pack.reshape(-1, 128)
    )
    outs = unpack(grad, ff_sum, rest, small)
    grad_t, d_we, d_ws, d_dw, d_be, d_bd, d_wr, d_wkv, d_wq, d_wo, *small = outs
    return (
        result_t.T,
        grad_t.T,
        small[0],
        small[1],
        d_wq,
        small[2],
        d_wr.T,
        small[3],
        small[4],
        small[5],
        d_wkv,
        small[6],
        d_wo,
        small[7],
        small[8],
        small[9],
        d_we,
        d_be,
        d_dw,
        d_bd,
        d_ws.T,
        small[10],
    )


def solution(mesh):
    both = P(("dp", "hidden"), None)
    cols = P(None, "hidden")
    chan = P("hidden")
    deep = P("hidden", None)
    whole = P()
    return jax.shard_map(
        partial(body, mesh.shape["dp"], mesh.shape["hidden"]),
        mesh=mesh,
        in_specs=(both,) + (whole,) * 15 + (cols, chan, cols, chan, deep, whole, both),
        out_specs=(both, both) + (whole,) * 14 + (cols, chan, cols, chan, deep, whole),
        check_vma=False,
    )
```

```python
from functools import partial

import jax
import jax.numpy as jnp
import numpy as np
from jax import lax
from jax.experimental import pallas as pl
from jax.experimental.pallas import tpu as pltpu
from jax.sharding import PartitionSpec as P

HEADS = 5
HEAD = 64
BLOCK = 196
GRID = 14
SMALL = 6
SMALL_IMGS = 5
KVB = 49
D = 320
FF = 1280
KPAD = 56
WIN = 208
ODD = 184
CHUNK = 256
CHUNKS = FF // CHUNK
SLAB = 224
DEEP = 1024
PAD = 16
MIB = 1024 * 1024

f32 = jnp.float32
bf16 = jnp.bfloat16
MESH = pl.DeviceIdType.MESH


def gather_table():
    out = np.zeros((2, 2, 4 * KPAD, WIN), np.float32)
    for kind in range(2):
        for parity in range(2):
            off = 12 * parity
            for a in range(2):
                for b in range(2):
                    for key in range(KVB):
                        if kind == 0:
                            i, j = divmod(key, GRID // 2)
                            spot = (2 * i + a) * GRID + 2 * j + b
                        else:
                            if key >= 45:
                                continue
                            image, rest = divmod(key, 9)
                            i, j = divmod(rest, 3)
                            spot = image * 36 + (2 * i + a) * SMALL + 2 * j + b
                        out[kind, parity, (2 * a + b) * KPAD + key, off + spot] = 1.0
    return out.reshape(4, 4 * KPAD, WIN)


def score_table():
    out = np.full((2, 2, WIN, 256), -1e30, np.float32)
    for kind in range(2):
        for parity in range(2):
            off = 12 * parity
            for row in range(WIN):
                local = row - off
                for key in range(KVB):
                    if kind == 0 or local < 0 or local >= BLOCK:
                        good = True
                    else:
                        good = key < 45 and key // 9 == min(local // 36, 4)
                    if good:
                        for head in range(HEADS):
                            out[kind, parity, row, head * KVB + key] = 0.0
    return out.reshape(4, WIN, 256)


def row_table():
    out = np.zeros((2, 2, WIN, 128), np.float32)
    for parity in range(2):
        off = 12 * parity
        for row in range(BLOCK):
            i, j = divmod(row, GRID)
            out[0, parity, off + row, :7] = (1, j > 0, j < 13, i > 0, 0, i < 13, 0)
            if row < 180:
                i, j = divmod(row % 36, SMALL)
                out[1, parity, off + row, :7] = (1, j > 0, j < 5, 0, i > 0, 0, i < 5)
    return out.reshape(4, WIN, 128)


def split(x):
    high = x.astype(bf16)
    return high, (x - high.astype(f32)).astype(bf16)


def pack_left(x):
    high = x.astype(bf16).astype(f32)
    low = x - high
    tail = jnp.concatenate([high[:, 256:], low[:, 256:]], 1).astype(bf16)
    high, low = high[:, :256].astype(bf16), low[:, :256].astype(bf16)
    return jnp.concatenate([high, low, high, tail, tail], 1)


def pack_short(x):
    high = x.astype(bf16).astype(f32)
    low = x - high
    tail = jnp.concatenate([high[:, 256:], low[:, 256:]], 1).astype(bf16)
    return jnp.concatenate([high[:, :256].astype(bf16), low[:, :256].astype(bf16), tail], 1)


def pack_lane(w):
    high = w.astype(bf16).astype(f32)
    low = w - high
    tail_high = jnp.concatenate([high[:, 256:], high[:, 256:]], 1).astype(bf16)
    tail_low = jnp.concatenate([low[:, 256:], low[:, 256:]], 1).astype(bf16)
    high, low = high[:, :256].astype(bf16), low[:, :256].astype(bf16)
    return jnp.concatenate([high, high, low, tail_high, tail_low], 1)


def pack_down(w):
    high, low = split(w)
    return jnp.concatenate(
        [high[:256], high[:256], low[:256], high[256:], high[256:], low[256:], low[256:]], 0
    )


def triple_left(x):
    high, low = split(x)
    return jnp.concatenate([high, low, high], 1)


def triple_down(w):
    high, low = split(w)
    return jnp.concatenate([high, high, low], 0)


def triple_lane(w):
    high, low = split(w)
    return jnp.concatenate([high, high, low], 1)


def mm(a, b):
    return jnp.dot(a, b, preferred_element_type=f32)


def mm_lane(a, b):
    return lax.dot_general(a, b, (((1,), (1,)), ((), ())), preferred_element_type=f32)


def mm_rows(a, b):
    left_high, left_low = split(a.T)
    high, low = split(b)
    return mm(left_high, high) + mm(left_low, high) + mm(left_high, low)


def norm_rows(x):
    center = jnp.sum(x, -1, keepdims=True) * (1.0 / D)
    centered = x - center
    spread = jnp.sum(centered * centered, -1, keepdims=True) * (1.0 / D)
    scale = lax.rsqrt(spread + 1e-06)
    return centered * scale, scale


def norm_back(h, n, scale):
    mean_h = jnp.sum(h, -1, keepdims=True) * (1.0 / D)
    mean_hn = jnp.sum(h * n, -1, keepdims=True) * (1.0 / D)
    return scale * (h - mean_h - n * mean_hn)


def fold(x):
    return jnp.sum(x.reshape(x.shape[0] // 8, 8, x.shape[1]), 0)


def window(block):
    return pl.multiple_of((block // 2) * (2 * BLOCK) + (block % 2) * ODD, 8)


def slab(w):
    return pl.ds(pl.multiple_of(w * SLAB, SLAB), SLAB)


def place_window(ref, block, value):
    start = window(block)

    @pl.when(block % 2 == 0)
    def _():
        ref[pl.ds(start, WIN), :] = value

    @pl.when(block % 2 == 1)
    def _():
        edge = ref[pl.ds(start + 8, 8), :]
        rows = lax.broadcasted_iota(jnp.int32, edge.shape, 0)
        ref[pl.ds(start + 8, 8), :] = jnp.where(rows < 4, edge, value[8:16])
        ref[pl.ds(start + 16, WIN - 16), :] = value[16:]


def head_block(rows_ref, block, out_ref):
    start = pl.multiple_of(block * KPAD, 8)
    for head in range(HEADS):
        tile = head // 2
        if tile < 2:
            value = rows_ref[pl.ds(start, KPAD), tile * 128 : tile * 128 + 128]
            lane = lax.broadcasted_iota(jnp.int32, value.shape, 1)
            value = jnp.where((lane >= 64) == (head % 2 == 1), value, 0.0)
        else:
            half = rows_ref[pl.ds(start, KPAD), 256:320]
            value = jnp.concatenate([half, half], 1)
        out_ref[tile, head * KVB : head * KVB + KVB, :] = value[:KVB]


def head_rows(ref):
    return jnp.concatenate([ref[0], ref[1], ref[2][:, :64]], 1)


def head_unblock(ref, value):
    ref[0] = value[:, :128]
    ref[1] = value[:, 128:256]
    ref[2] = jnp.concatenate([value[:, 256:], value[:, 256:]], 1)
    lane = lax.broadcasted_iota(jnp.int32, (KPAD, 128), 1)
    row = lax.broadcasted_iota(jnp.int32, (KPAD, 128), 0)
    tiles = []
    for tile in range(3):
        first = ref[tile, 2 * tile * KVB : 2 * tile * KVB + KPAD, :]
        if tile < 2:
            second = ref[tile, (2 * tile + 1) * KVB : (2 * tile + 1) * KVB + KPAD, :]
            first = jnp.where(lane < 64, first, second)
        tiles.append(jnp.where(row < KVB, first, 0.0))
    return jnp.concatenate([tiles[0], tiles[1], tiles[2][:, :64]], 1)


def head_lane(ref):
    parts = []
    for tile in range(3):
        high = ref[tile].astype(bf16)
        parts.append((high, (ref[tile] - high.astype(f32)).astype(bf16)))
    return jnp.concatenate(
        [parts[0][0], parts[1][0], parts[0][0], parts[1][0], parts[0][1], parts[1][1], parts[2][0], parts[2][1]], 1
    )


def head_of_lane(shape):
    lane = lax.broadcasted_iota(jnp.int32, shape, 1)
    return [lane < (head + 1) * KVB for head in range(HEADS - 1)]


def by_head(below, values):
    out = values[HEADS - 1]
    for head in range(HEADS - 2, -1, -1):
        out = jnp.where(below[head], values[head], out)
    return out


def per_head(below, x, empty, reduce):
    out = []
    for head in range(HEADS):
        here = x
        if head < HEADS - 1:
            here = jnp.where(below[head], here, empty)
        if head > 0:
            here = jnp.where(below[head - 1], empty, here)
        out.append(reduce(here, axis=1, keepdims=True))
    return by_head(below, [jnp.broadcast_to(v, x.shape) for v in out])


def line(ref):
    return ref[...].reshape(1, -1)


def own_first(blocks):
    return (lax.axis_index("dp") * lax.axis_size("hidden") + lax.axis_index("hidden")) * blocks


def attention_kernel(
    kinds,
    tokens_t,
    table,
    scores_mask,
    row_marks,
    first_gain,
    first_bias,
    query_bias,
    reduce_bias,
    reduce_gain,
    reduce_shift,
    value_bias,
    output_bias,
    wq,
    wr,
    wkv,
    wo,
    after,
    *refs,
):
    held, refs = refs[:9], refs[9:]
    marks, first_n, query, attended, probs, keys, values, red_n, patches = refs[:9]
    wq_s, wo_s, wk_s, wv_s, wr_s, tokens, normed, kb, vb, sem = refs[9:]
    saves = [pltpu.make_async_copy(src, dst, sem.at[i]) for i, (src, dst) in enumerate(zip(refs, held))]
    blocks = probs.shape[0]
    slabs = tokens.shape[0] // SLAB
    first = own_first(blocks)
    g1, b1, bq, br = line(first_gain), line(first_bias), line(query_bias), line(reduce_bias)
    gr, sr, bv, bo = line(reduce_gain), line(reduce_shift), line(value_bias), line(output_bias)
    wq_s[...] = pack_down(wq[...])
    wo_s[...] = pack_down(wo[...])
    wk_s[...] = pack_down(wkv[:, :D])
    wv_s[...] = pack_down(wkv[:, D:])
    for sub in range(4):
        wr_s[sub] = pack_lane(wr[:, sub * D : sub * D + D])
    kb[...] = jnp.zeros_like(kb)
    vb[...] = jnp.zeros_like(vb)
    tokens[...] = tokens_t[...].T

    @pl.loop(0, slabs)
    def _(w):
        n, scale = norm_rows(tokens[slab(w), :])
        first_n[slab(w), :] = jnp.concatenate([n, jnp.broadcast_to(scale, (SLAB, 64))], 1)
        n = n * g1 + b1
        normed[slab(w), :] = n
        query[slab(w), :] = mm(pack_left(n), wq_s[...]) + bq

    saves[1].start()
    saves[2].start()

    @pl.loop(0, blocks)
    def _(b):
        which = kinds[first + b] * 2 + b % 2
        place_window(marks, b, row_marks[which])
        part = normed[pl.ds(window(b), WIN), :]
        high, low = split(part)
        pick = table[which]
        got = mm(pick, high) + mm(pick, low)
        rows = pl.ds(pl.multiple_of(b * KPAD, 8), KPAD)
        for sub in range(4):
            patches[sub, rows, :] = got[sub * KPAD : sub * KPAD + KPAD]

    saves[0].start()
    saves[8].start()

    @pl.loop(0, blocks * KPAD // SLAB)
    def _(w):
        acc = br + mm_lane(pack_left(patches[0, slab(w), :]), wr_s[0])
        for sub in range(1, 4):
            acc = acc + mm_lane(pack_left(patches[sub, slab(w), :]), wr_s[sub])
        n, scale = norm_rows(acc)
        red_n[slab(w), :] = jnp.concatenate([n, jnp.broadcast_to(scale, (SLAB, 64))], 1)
        packed = pack_left(n * gr + sr)
        keys[slab(w), :] = mm(packed, wk_s[...])
        values[slab(w), :] = mm(packed, wv_s[...]) + bv

    for i in (5, 6, 7):
        saves[i].start()

    @pl.loop(0, blocks)
    def _(b):
        which = kinds[first + b] * 2 + b % 2
        head_block(keys, b, kb)
        head_block(values, b, vb)
        q = query[pl.ds(window(b), WIN), :]
        s = mm_lane(pack_left(q), head_lane(kb)) * (HEAD**-0.5) + scores_mask[which]
        below = head_of_lane(s.shape)
        e = jnp.exp(s - per_head(below, s, -3e38, jnp.max))
        p = e / per_head(below, e, 0.0, jnp.sum)
        probs[b] = p
        out = mm(triple_left(p), triple_down(head_rows(vb)))
        place_window(attended, b, out)

    saves[3].start()
    saves[4].start()

    @pl.loop(0, slabs)
    def _(w):
        branch = mm(pack_left(attended[slab(w), :]), wo_s[...]) + bo
        after[slab(w), :] = tokens[slab(w), :] + marks[slab(w), 0:1] * branch

    for save in saves:
        save.wait()


def attention_forward(kinds, tokens_t, vecs, wq, wr, wkv, wo):
    rows = tokens_t.shape[1]
    blocks = rows // BLOCK
    krows = blocks * KPAD
    vm = pl.BlockSpec(memory_space=pltpu.VMEM)

    def shape(*dims):
        return jax.ShapeDtypeStruct(dims, f32)

    saved = (
        shape(rows, 128),
        shape(rows, D + 64),
        shape(rows, D),
        shape(rows, D),
        shape(blocks, WIN, 256),
        shape(krows, D),
        shape(krows, D),
        shape(krows, D + 64),
        shape(4, krows, D),
    )
    return pl.pallas_call(
        attention_kernel,
        out_shape=(shape(rows, D),) + saved,
        in_specs=[pl.BlockSpec(memory_space=pltpu.SMEM)] + [vm] * 16,
        out_specs=(vm,) + (pl.BlockSpec(memory_space=pl.ANY),) * 9,
        scratch_shapes=[pltpu.VMEM(x.shape, f32) for x in saved]
        + [
            pltpu.VMEM((1024, D), bf16),
            pltpu.VMEM((1024, D), bf16),
            pltpu.VMEM((1024, D), bf16),
            pltpu.VMEM((1024, D), bf16),
            pltpu.VMEM((4, D, 1024), bf16),
            pltpu.VMEM((rows, D), f32),
            pltpu.VMEM((rows, D), f32),
            pltpu.VMEM((3, 256, 128), f32),
            pltpu.VMEM((3, 256, 128), f32),
            pltpu.SemaphoreType.DMA((9,)),
        ],
        compiler_params=pltpu.CompilerParams(vmem_limit_bytes=60 * MIB),
        name="attention",
    )(
        kinds,
        tokens_t,
        jnp.asarray(gather_table(), bf16),
        jnp.asarray(score_table()),
        jnp.asarray(row_table()),
        *vecs,
        wq,
        wr,
        wkv,
        wo,
    )


ERF_P = 0.3275911
ERF = (0.254829592, -0.284496736, 1.421413741, -1.453152027, 1.061405429)


def gelu_pair(x):
    size = jnp.abs(x)
    d = 1.0 + (ERF_P * 0.7071067811865476) * size
    t = pl.reciprocal(d, approx=True)
    t = t * (2.0 - d * t)
    e = jnp.exp(-0.5 * (x * x))
    poly = t * (ERF[0] + t * (ERF[1] + t * (ERF[2] + t * (ERF[3] + t * ERF[4]))))
    tail = 0.5 * (poly * e)
    phi = jnp.where(x < 0.0, tail, 1.0 - tail)
    return x * phi, phi + x * (0.3989422804014327 * e)


def has_left(r):
    return r % GRID > 0, r < 180 and r % SMALL > 0


def has_right(r):
    return r % GRID < GRID - 1, r < 180 and r % SMALL < SMALL - 1


def has_up(r):
    return r >= GRID, r < 180 and r % 36 >= SMALL


def has_down(r):
    return r < BLOCK - GRID, r < 180 and r % 36 < 30


def total_of(values):
    values = [v for v in values if v is not None]
    out = values[0]
    for v in values[1:]:
        out = out + v
    return out


def forward_kernel(
    kinds,
    after,
    cot_t,
    second_gain,
    second_shift,
    shrink_bias,
    own_we,
    own_ws,
    own_taps,
    result_t,
    g_after,
    pack,
    sums,
    we_s,
    we_l,
    ws_s,
    ws_l,
    result,
    g_second,
    by_block,
    by_place,
    taps,
    second,
    branch,
    second_t,
    branch_t,
    xs0,
    xs1,
    nx1,
    ga0,
    ga1,
    ng1,
    y0,
    yu,
    yd,
    act,
    gx,
    held_act,
    held_gx,
    dwe,
    dws,
    sem,
):
    rows = after.shape[0]
    pieces = rows // SLAB
    per = FF // 128 // own_we.shape[0]
    g2, s2, bs = line(second_gain), line(second_shift), line(shrink_bias)
    first = own_first(8)
    block = lax.broadcasted_iota(jnp.int32, (8, 128), 0)
    kind = jnp.zeros((8, 128), jnp.int32)
    for i in range(8):
        kind = jnp.where(block == i, kinds[first + i], kind)
    zero_kind = kind == 0
    k0 = jnp.where(zero_kind, 1.0, 0.0)
    k1 = 1.0 - k0

    loads = []
    for tile in range(FF // 128):
        lanes = pl.ds((tile % per) * 128, 128)
        for i, (source, low, size) in enumerate(((own_we, 0, D), (own_ws, D, D), (own_taps, 2 * D, 16))):
            loads.append(
                pltpu.make_async_copy(
                    source.at[tile // per, :, lanes], pack.at[tile, pl.ds(low, size)], sem.at[3 * tile + i]
                )
            )
    for load in loads:
        load.start()

    held_act[...] = jnp.zeros_like(held_act)
    held_gx[...] = jnp.zeros_like(held_gx)
    sums[...] = jnp.zeros_like(sums)

    def tiles_of(x):
        return x[:, :128], x[:, 128:256], jnp.concatenate([x[:, 256:], x[:, 256:]], 1)

    def to_places(out):
        for t in range(3):
            for i in range(8):
                by_place[t, pl.ds(i, BLOCK, stride=8), :] = by_block[t, i * BLOCK : (i + 1) * BLOCK, :]

        @pl.loop(0, rows // SLAB)
        def _(w):
            out[slab(w), :] = joined(by_place, slab(w))

    def to_blocks(source):
        @pl.loop(0, rows // SLAB)
        def _(w):
            for t, value in enumerate(tiles_of(source[slab(w), :])):
                by_place[t, slab(w), :] = value

        for t in range(3):
            for i in range(8):
                by_block[t, i * BLOCK : (i + 1) * BLOCK, :] = by_place[t, pl.ds(i, BLOCK, stride=8), :]

    def joined(ref, at):
        return jnp.concatenate([ref[0, at, :], ref[1, at, :], ref[2, at, :][:, :64]], 1)

    for t in range(3):
        low, high = 128 * t, min(128 * t + 128, D)
        value = cot_t[low:high, :].T
        by_block[t] = value if high - low == 128 else jnp.concatenate([value, value], 1)
    to_places(result)

    @pl.loop(0, rows // SLAB)
    def _(w):
        for t, value in enumerate(tiles_of(after[slab(w), :])):
            by_block[t, slab(w), :] = value

    to_places(g_second)

    g_after[...] = result[...]
    dead = 180 * 8
    result[dead:, :] = (result[dead:, :].reshape(BLOCK - 180, 8, D) * k0[:, :1]).reshape(rows - dead, D)

    @pl.loop(0, rows // SLAB)
    def _(w):
        a = g_second[slab(w), :]
        for t, value in enumerate(tiles_of(a)):
            by_block[t, slab(w), :] = value
        n, _ = norm_rows(a)
        value = n * g2 + s2
        g_second[slab(w), :] = value
        second[slab(w), :] = pack_short(value)
        grad = result[slab(w), :]
        sums[2] += fold(grad)
        branch[slab(w), :] = pack_short(grad)

    for source, turned in ((g_second, second_t), (result, branch_t)):
        high, low = split(source[...].T)
        turned[...] = jnp.concatenate([high, low, high], 1)
    result[...] = jnp.zeros_like(result)
    g_second[...] = jnp.zeros_like(g_second)

    for load in loads:
        load.wait()
    for c in range(CHUNKS):
        for which, (down, lane) in enumerate(((we_s, we_l), (ws_s, ws_l))):
            value = jnp.concatenate([pack[2 * c + t, which * D : which * D + D, :] for t in range(2)], 1)
            high, low = split(value)
            down[c] = jnp.concatenate([high, low], 0)
            lane[c] = jnp.concatenate([high, low], 1)
        for t in range(2):
            for k in range(11):
                taps[c, t, k] = jnp.broadcast_to(pack[2 * c + t, 2 * D + k : 2 * D + k + 1, :], (8, 128))

    def own(h):
        return slice(h * SLAB, (h + 1) * SLAB)

    def left(ref, h):
        x = ref[own(h), :]
        return jnp.concatenate([x[:, :512], x[:, :256], x[:, 512:], x[:, 512:]], 1)

    def deep(ref, c):
        x = ref[c]
        return jnp.concatenate(
            [x[:256], x[:256], x[D : D + 256], x[256:D], x[256:D], x[D + 256 :], x[D + 256 :]], 0
        )

    def expand_task(c, h, outs):
        e = mm(left(second, h), deep(we_s, c))
        for t in range(2):
            outs[t][own(h), :] = e[:, 128 * t : 128 * t + 128] + taps[c, t, 9][0:1]

    def active_grad_task(c, h, outs):
        g = mm(left(branch, h), deep(ws_s, c))
        for t in range(2):
            outs[t][own(h), :] = g[:, 128 * t : 128 * t + 128]

    def out_task(c, h, source, lane, out):
        x = source[own(h), :]
        weight = lane[c]
        out[own(h), :] += mm_lane(
            jnp.concatenate([x, x[:, :256]], 1), jnp.concatenate([weight[:, :256], weight], 1)
        )

    def weight_task(c, source, turned, row, total, k):
        span = slice(k * DEEP, min((k + 1) * DEEP, 3 * rows))
        parts = []
        for i, low in enumerate((0, 0, CHUNK)):
            start, stop = max(span.start, i * rows) - i * rows, min(span.stop, (i + 1) * rows) - i * rows
            if start < stop:
                parts.append(source[start:stop, low : low + CHUNK])
        value = mm(turned[:, span], jnp.concatenate(parts, 0) if len(parts) > 1 else parts[0])
        if k > 0:
            value = value + total[...]
        if span.stop < 3 * rows:
            total[...] = value
            return
        for t in range(2):
            pack[2 * c + t, row : row + D, :] = value[:, 128 * t : 128 * t + 128]

    def early_tasks(c, x_outs, g_outs):
        out = []
        for h in range(pieces):
            out += [partial(expand_task, c, h, x_outs), partial(active_grad_task, c, h, g_outs)]
        return out

    def late_tasks(c):
        out = []
        for h in range(pieces):
            out += [
                partial(out_task, c, h, held_act, ws_l, result),
                partial(out_task, c, h, held_gx, we_l, g_second),
            ]
        return out

    def weight_tasks(c):
        count = -(-3 * rows // DEEP)
        first_half = [partial(weight_task, c, held_act, branch_t, D, dws, k) for k in range(count)]
        return first_half, [partial(weight_task, c, held_gx, second_t, 0, dwe, k) for k in range(count)]

    def woven(a, b):
        out = list(a)
        for i, task in enumerate(b):
            out.insert(round((i + 1) * len(a) / (len(b) + 1)) + i, task)
        return out

    def at(r):
        return slice(8 * r, 8 * r + 8)

    def gated(value, ok):
        if ok[0] and ok[1]:
            return value
        if ok[0]:
            return value * k0
        return value * k1 if ok[1] else None

    def picked(ref, r, ok, sign):
        if ok[0] and ok[1]:
            return jnp.where(zero_kind, ref[at(r + sign * GRID), :], ref[at(r + sign * SMALL), :])
        if ok[0]:
            return ref[at(r + sign * GRID), :] * k0
        return ref[at(r + sign * SMALL), :] * k1 if ok[1] else None

    def put_split(ref, t, r, pair):
        high, low = split(jnp.concatenate(pair, 0))
        here = slice(8 * r, 8 * r + 16)
        ref[here, 128 * t : 128 * t + 128] = high
        ref[here, 256 + 128 * t : 384 + 128 * t] = low

    def item(c, t, x, g, tasks):
        tap = [taps[c, t, k] for k in range(11)]
        totals = [jnp.zeros((8, 128), f32)] * 11

        def columns(r, near):
            return [
                gated(near(r - 1), has_left(r)) if r > 0 else None,
                near(r),
                gated(near(r + 1), has_right(r)) if r + 1 < BLOCK else None,
            ]

        def mix(values, ks, more=()):
            return total_of([None if v is None else v * tap[k] for v, k in zip(values, ks)] + list(more))

        def loader():
            kept = {}

            def near(r):
                if r not in kept:
                    kept[r] = x[at(r), :]
                return kept[r]

            return near

        ahead, behind = loader(), loader()
        moved_back = {}
        every = {}
        count = (BLOCK + 30) // 2
        slots = {round((i + 0.5) * count / len(tasks)): task for i, task in enumerate(tasks)}
        for step in range(count):
            for r in (2 * step, 2 * step + 1):
                if r < BLOCK:
                    cols = columns(r, ahead)
                    yu[at(r), :] = mix(cols, (0, 1, 2))
                    y0[at(r), :] = mix(cols, (3, 4, 5), (tap[10],))
                    yd[at(r), :] = mix(cols, (6, 7, 8))
            r = 2 * step - 14
            if 0 <= r < BLOCK:
                conv = [
                    total_of([y0[at(s), :], picked(yu, s, has_up(s), -1), picked(yd, s, has_down(s), 1)])
                    for s in (r, r + 1)
                ]
                active, slope = gelu_pair(jnp.concatenate(conv, 0))
                put_split(act, t, r, [active[:8], active[8:]])
                here = slice(8 * r, 8 * r + 16)
                g[here, :] = g[here, :] * slope
            for r in (2 * step - 28, 2 * step - 27):
                if 0 <= r < BLOCK:
                    same = g[at(r), :]
                    moved = [picked(g, r, has_down(r), 1), same, picked(g, r, has_up(r), -1)]
                    cols = columns(r, behind)
                    totals[10] = totals[10] + same
                    for p in range(3):
                        for q in range(3):
                            if moved[p] is not None and cols[q] is not None:
                                totals[3 * p + q] = totals[3 * p + q] + moved[p] * cols[q]
                    moved_back[r] = [mix(moved, ks) for ks in ((0, 3, 6), (1, 4, 7), (2, 5, 8))]
            r = 2 * step - 30
            if 0 <= r < BLOCK:
                pair = []
                for s in (r, r + 1):
                    value = total_of(
                        [
                            moved_back[s][1],
                            gated(moved_back[s - 1][2], has_left(s)) if s > 0 else None,
                            gated(moved_back[s + 1][0], has_right(s)) if s + 1 < BLOCK else None,
                        ]
                    )
                    totals[9] = totals[9] + value
                    pair.append(value)
                put_split(gx, t, r, pair)
            if step in slots:
                slots[step]()
        for k in range(11):
            pack[2 * c + t, 2 * D + k : 2 * D + k + 1, :] = jnp.sum(totals[k], 0, keepdims=True)

    for task in early_tasks(0, (xs0, xs1), (ga0, ga1)):
        task()

    @pl.loop(0, CHUNKS)
    def _(c):
        before = jnp.maximum(c - 1, 0)
        item(c, 0, xs0, ga0, woven(late_tasks(before), weight_tasks(before)[0]))
        later = jnp.minimum(c + 1, CHUNKS - 1)
        item(c, 1, xs1, ga1, woven(early_tasks(later, (xs0, nx1), (ga0, ng1)), weight_tasks(before)[1]))
        xs1[...] = nx1[...]
        ga1[...] = ng1[...]
        held_act[...] = act[...]
        held_gx[...] = gx[...]

    for task in late_tasks(CHUNKS - 1) + sum(weight_tasks(CHUNKS - 1), []):
        task()
    for c in range(CHUNKS):
        for t in range(2):
            pack[2 * c + t, 2 * D + 11 : 2 * D + 16, :] = jnp.zeros((5, 128), f32)

    result[dead:, :] = ((result[dead:, :] + bs).reshape(BLOCK - 180, 8, D) * k0[:, :1]).reshape(rows - dead, D) - bs

    @pl.loop(0, rows // SLAB)
    def _(w):
        a = joined(by_block, slab(w))
        result[slab(w), :] = a + (result[slab(w), :] + bs)
        n, scale = norm_rows(a)
        g = g_second[slab(w), :]
        sums[0] += fold(g * n)
        sums[1] += fold(g)
        g_second[slab(w), :] = g_after[slab(w), :] + norm_back(g * g2, n, scale)

    to_blocks(result)
    for t in range(3):
        low, high = 128 * t, min(128 * t + 128, D)
        result_t[low:high, :] = by_block[t].T[: high - low]
    to_blocks(g_second)

    @pl.loop(0, rows // SLAB)
    def _(w):
        g_after[slab(w), :] = joined(by_block, slab(w))


def feed_forward(kinds, after, cot_t, vecs, weights):
    rows = after.shape[0]
    vm = pl.BlockSpec(memory_space=pltpu.VMEM)
    tile = pltpu.VMEM((rows, 128), f32)
    half = pltpu.VMEM((rows, 2 * CHUNK), bf16)
    return pl.pallas_call(
        forward_kernel,
        out_shape=(
            jax.ShapeDtypeStruct((D, rows), f32),
            jax.ShapeDtypeStruct((rows, D), f32),
            jax.ShapeDtypeStruct((2 * CHUNKS, 2 * D + 16, 128), f32),
            jax.ShapeDtypeStruct((3, 8, D), f32),
        ),
        in_specs=[pl.BlockSpec(memory_space=pltpu.SMEM)] + [vm] * 5 + [pl.BlockSpec(memory_space=pl.ANY)] * 3,
        out_specs=(vm,) * 4,
        scratch_shapes=[
            pltpu.VMEM((CHUNKS, 2 * D, CHUNK), bf16),
            pltpu.VMEM((CHUNKS, D, 2 * CHUNK), bf16),
            pltpu.VMEM((CHUNKS, 2 * D, CHUNK), bf16),
            pltpu.VMEM((CHUNKS, D, 2 * CHUNK), bf16),
            pltpu.VMEM((rows, D), f32),
            pltpu.VMEM((rows, D), f32),
            pltpu.VMEM((3, rows, 128), f32),
            pltpu.VMEM((3, rows, 128), f32),
            pltpu.VMEM((CHUNKS, 2, 11, 8, 128), f32),
            pltpu.VMEM((rows, 640), bf16),
            pltpu.VMEM((rows, 640), bf16),
            pltpu.VMEM((D, 3 * rows), bf16),
            pltpu.VMEM((D, 3 * rows), bf16),
        ]
        + [tile] * 9
        + [half] * 4
        + [pltpu.VMEM((D, CHUNK), f32)] * 2
        + [pltpu.SemaphoreType.DMA((6 * CHUNKS,))],
        compiler_params=pltpu.CompilerParams(vmem_limit_bytes=63 * MIB),
        name="feed_forward",
    )(kinds, after, cot_t, *vecs, *weights)


class Wires:
    def __init__(self, pairs, cores, send, recv):
        self.bits = pairs.bit_length() - 1
        self.cores = cores
        self.me, self.core = lax.axis_index("dp"), lax.axis_index("hidden")
        self.other = cores - 1 - self.core
        self.send, self.recv, self.used = send, recv, 0

    def groups(self):
        rest = list(range(2, self.bits))
        return [(k,) for k in range(min(2, self.bits))] + [tuple(rest[i : i + 2]) for i in range(0, len(rest), 2)]

    def bit(self, k):
        return (self.me // (1 << k)) % 2

    def peer(self, group, j):
        flips = [(1 - 2 * self.bit(k)) * (1 << k) for i, k in enumerate(group) if (j >> i) & 1]
        return (sum(flips, self.me), self.core)

    def place(self, group, j):
        bits = [(1 - self.bit(k) if (j >> i) & 1 else self.bit(k)) * (1 << i) for i, k in enumerate(group)]
        return sum(bits[1:], bits[0])

    def greet(self):
        peers = [self.peer(group, j) for group in self.groups() for j in range(1, 1 << len(group))]
        if self.cores > 1:
            peers.append((self.me, self.other))
        if not peers:
            return
        barrier = pltpu.get_barrier_semaphore()
        for target in peers:
            pl.semaphore_signal(barrier, inc=1, device_id=target, device_id_type=MESH)
        pl.semaphore_wait(barrier, len(peers))

    def copy(self, src, dst, target):
        slot = self.used
        self.used += 1
        return pltpu.make_async_remote_copy(
            src_ref=src,
            dst_ref=dst,
            send_sem=self.send.at[slot],
            recv_sem=self.recv.at[slot],
            device_id=target,
            device_id_type=MESH,
        )

    def local(self, src, dst):
        slot = self.used
        self.used += 1
        return pltpu.make_async_copy(src, dst, self.send.at[slot])

    def sibling(self, src, dst):
        return self.copy(src, dst, (self.me, self.other))


def rows_of(start, size):
    return pl.ds(pl.multiple_of(start, 8), size)


class Chain:
    def __init__(self, wires, acc, near, got, full, base, rows, order, opening, closing):
        self.stages, self.costs = [], []
        whole = pl.ds(base, rows)
        scale = 512 * wires.cores / LINK

        def meet():
            if near is not None:
                acc[whole, :] = acc[whole, :] + near[whole, :]

        start, size, spot = base + 0 * wires.me, rows, base
        pending, action = opening, meet
        self.stages.append(([], None, opening))
        self.costs.append(("core", rows * 512 / CORE_LINK))
        held = []
        for group in order:
            many = 1 << len(group)
            size //= many
            keep = start + wires.place(group, 0) * size
            copies, lands = [], []
            for j in range(1, many):
                land = pl.ds(spot, size)
                spot += size
                give = start + wires.place(group, j) * size
                copies.append(wires.copy(acc.at[rows_of(give, size)], got.at[land], wires.peer(group, j)))
                lands.append(land)
            self.stages.append((pending, action, copies))
            self.costs.append((group, scale * size * (1 if many == 2 else many)))

            def add(keep=keep, lands=lands, size=size):
                value = acc[rows_of(keep, size), :]
                for land in lands:
                    value = value + got[land, :]
                acc[rows_of(keep, size), :] = value

            pending, action = copies, add
            held.append((group, start))
            start = keep
        last, last_start, last_size = action, start, size

        def settle():
            last()
            full[rows_of(last_start, last_size), :] = acc[rows_of(last_start, last_size), :]

        action = settle
        for group, before in reversed(held):
            mine = rows_of(start, size)
            many = 1 << len(group)
            copies = [wires.copy(full.at[mine], full.at[mine], wires.peer(group, j)) for j in range(1, many)]
            self.stages.append((pending, action, copies))
            self.costs.append((group, scale * size * (1 if many == 2 else many)))
            pending, action = copies, None
            start, size = before, size * many
        if closing:
            self.stages.append((pending, action, closing))
            self.costs.append(("core", rows * 512 / CORE_LINK))
            pending, action = closing, None
        self.stages.append((pending, action, []))
        self.costs.append((None, 0.0))

    def run(self, stage):
        waits, action, starts = self.stages[stage]
        for c in waits:
            c.wait()
        if action is not None:
            action()
        for c in starts:
            c.start()


class Exchange(Chain):
    def __init__(self, wires, sums, got):
        partners = [((k,), wires.peer((k,), 1)) for k in range(wires.bits)]
        if wires.cores > 1:
            partners.insert(0, ("core", (wires.me, wires.other)))
        self.stages, self.costs = [], []
        pending, action = [], None
        for i, (name, target) in enumerate(partners):
            c = wires.copy(sums.at[i], got.at[i], target)
            self.stages.append((pending, action, [c]))
            self.costs.append((name, 0.5))

            def add(i=i):
                sums[i + 1] = sums[i] + got[i]

            pending, action = [c], add
        self.stages.append((pending, action, []))
        self.costs.append((None, 0.0))
        self.last = len(partners)


LINK = 100e3
CORE_LINK = 400e3
DELAY = 1.5
STEP_WORK = 0.1


class Plan:
    def __init__(self):
        self.now, self.free, self.going = 0.0, {}, []

    def add(self, chains):
        self.going += [[self.now, c, 0] for c in chains]

    def after(self, us):
        self.now += us
        due = []
        while True:
            ready = [g for g in self.going if g[0] <= self.now]
            if not ready:
                return due
            due.append(self.take(min(ready, key=lambda g: g[0])))

    def take(self, entry):
        done, chain, stage = entry
        self.now = max(self.now, done) + STEP_WORK
        link, us = chain.costs[stage]
        self.free[link] = max(self.free.get(link, 0.0), self.now) + us
        if stage + 1 == len(chain.stages):
            self.going.remove(entry)
        else:
            entry[0], entry[2] = self.free[link] + DELAY, stage + 1
        return chain, stage

    def rest(self):
        due = []
        while self.going:
            due.append(self.take(min(self.going, key=lambda g: g[0])))
        return due


def run_steps(steps):
    for chain, stage in steps:
        chain.run(stage)


def axis_orders(groups):
    return groups, groups[1::-1] + groups[2:], groups[2:] + groups[:2]


def cut(total, unit, parts):
    units = total // unit
    marks = sorted({0, units} | {round(units * x) for x in parts})
    return [(a * unit, b * unit) for a, b in zip(marks, marks[1:])]


def round_up(x, unit):
    return -(-x // unit) * unit


def sum_rows(pairs, cores):
    unit = 8 * pairs
    ff = round_up(2 * CHUNKS // cores * (2 * D + 16), unit)
    rest = round_up(20 * (D // cores), unit)
    return ff, rest


def backward_kernel(
    pairs,
    cores,
    kinds,
    first_n_from,
    g_after,
    marks,
    table,
    first_gain,
    first_bias,
    reduce_gain,
    reduce_shift,
    wq,
    wr,
    wkv,
    wo,
    query_from,
    attended_from,
    probs_from,
    keys_from,
    values_from,
    red_n_from,
    patches_from,
    sums,
    ff_pack,
    grad,
    ff_full,
    full,
    small,
    first_n,
    query,
    attended,
    probs,
    keys,
    values,
    red_n,
    patches,
    wq_l,
    wo_l,
    wk_l,
    wv_l,
    wr_l,
    g_att,
    g_query,
    g_keys,
    g_values,
    g_patch,
    g_scores,
    kb,
    vb,
    tmp,
    acc,
    ff_acc,
    ff_near,
    ff_got,
    big,
    near,
    got,
    small_sum,
    small_got,
    send,
    recv,
):
    blocks = probs.shape[0]
    rows = g_after.shape[0]
    slabs = rows // SLAB
    krows = blocks * KPAD
    first = own_first(blocks)
    part = D // cores
    g1, b1, gr, sr = line(first_gain), line(first_bias), line(reduce_gain), line(reduce_shift)

    wires = Wires(pairs, cores, send, recv)
    core = wires.core
    orders = axis_orders(wires.groups())
    unit = 8 * pairs
    ff_real = ff_pack.shape[0] // cores
    ff_total, total = ff_acc.shape[0], big.shape[1]
    if ff_total > ff_real:
        ff_acc[ff_real:, :] = jnp.zeros((ff_total - ff_real, 128), f32)
        ff_near[ff_real:, :] = jnp.zeros((ff_total - ff_real, 128), f32)
    if total > 20 * part:
        for h in range(cores):
            big[h, 20 * part :, :] = jnp.zeros((total - 20 * part, 128), f32)
    wires.greet()
    ff_chains = []
    for i, (low, high) in enumerate(cut(ff_total, unit, (4 / 26, 10 / 26, 16 / 26, 21 / 26))):
        size = min(high, ff_real) - low
        here = pl.ds(low, size)
        opening = [wires.local(ff_pack.at[rows_of(core * ff_real + low, size)], ff_acc.at[here])]
        if cores > 1:
            opening.append(wires.sibling(ff_pack.at[rows_of(wires.other * ff_real + low, size)], ff_near.at[here]))
        ff_chains.append(
            Chain(
                wires,
                ff_acc,
                ff_near if cores > 1 else None,
                ff_got,
                ff_full,
                low,
                high - low,
                orders[(2, 0, 1, 0, 1)[i]],
                opening,
                [],
            )
        )
    bounds = [2 * part, 12 * part, 17 * part]
    chains = []
    cuts = cut(total, unit, (2 / 25, 8 / 25, 13 / 25, 15 / 25, 18 / 25, 21 / 25, 23 / 25))
    for i, (low, high) in enumerate(cuts):
        here = pl.ds(low, high - low)
        opening, closing = [], []
        if cores > 1:
            opening = [wires.sibling(big.at[wires.other, here], near.at[here])]
            closing = [wires.sibling(full.at[core, here], full.at[core, here])]
        chain = Chain(
            wires,
            big.at[core],
            near if cores > 1 else None,
            got,
            full.at[core],
            low,
            high - low,
            orders[(0, 0, 1, 2, 0, 1, 0, 1)[i]],
            opening,
            closing,
        )
        chain.ready = sum(high > x for x in bounds)
        chains.append(chain)
    fetch = {
        name: wires.local(src, dst)
        for name, src, dst in (
            ("attended", attended_from, attended),
            ("values", values_from, values),
            ("probs", probs_from, probs),
            ("query", query_from, query),
            ("red_n", red_n_from, red_n),
            ("patches", patches_from, patches),
            ("keys", keys_from, keys),
            ("first_n", first_n_from, first_n),
        )
    }
    plan = Plan()
    plan.add(ff_chains)

    def tick(us, level=None):
        run_steps(plan.after(us))
        if level is not None:
            plan.add([c for c in chains if c.ready == level])
            run_steps(plan.after(0.0))

    def ticks(count, us):
        return [plan.after(us) for _ in range(count)]

    def run_at(index, planned):
        for i, steps in enumerate(planned):
            if steps:
                pl.when(index == i)(partial(run_steps, steps))

    def store(tile, value):
        for t in range(value.shape[1] // 128):
            for h in range(cores):
                big[h, (tile + t) * part : (tile + t + 1) * part, :] = value[
                    h * part : (h + 1) * part, 128 * t : 128 * t + 128
                ]

    tick(0.0)
    for c in fetch.values():
        c.start()
    wo_l[...] = pack_lane(wo[...])
    wk_l[...] = pack_lane(wkv[:, :D])
    wv_l[...] = pack_lane(wkv[:, D:])
    kb[...] = jnp.zeros_like(kb)
    vb[...] = jnp.zeros_like(vb)
    acc[...] = jnp.zeros_like(acc)
    tick(2.0)
    planned_0 = ticks(slabs, 0.6)

    @pl.loop(0, slabs)
    def _(w):
        g = marks[slab(w), 0:1] * g_after[slab(w), :]
        grad[slab(w), :] = g
        acc[0] += fold(g)
        g_att[slab(w), :] = mm_lane(pack_left(g), wo_l[...])
        run_at(w, planned_0)

    fetch["attended"].wait()
    d_wo = mm_rows(attended[...], grad[...])
    store(0, d_wo[:, :256])
    tick(3.5, 0)
    planned_1 = ticks(blocks, 1.8)
    for name in ("values", "probs", "query"):
        fetch[name].wait()

    @pl.loop(0, blocks)
    def _(b):
        head_block(values, b, vb)
        here = pl.ds(window(b), WIN)
        first_row = 12 * (b % 2)
        row = lax.broadcasted_iota(jnp.int32, (WIN, D), 0)
        inside = (row >= first_row) & (row < first_row + BLOCK)
        ga = jnp.where(inside, g_att[here, :], 0.0)
        p = probs[b]
        gp = mm_lane(pack_left(ga), head_lane(vb))
        below = head_of_lane(p.shape)
        gs = p * (gp - per_head(below, gp * p, 0.0, jnp.sum)) * (HEAD**-0.5)
        g_scores[b] = gs
        here_k = pl.ds(pl.multiple_of(b * KPAD, 8), KPAD)
        g_values[here_k, :] = head_unblock(tmp, mm_rows(p, ga))
        g_keys[here_k, :] = head_unblock(tmp, mm_rows(gs, query[here, :]))
        run_at(b, planned_1)

    fetch["red_n"].wait()
    fetch["patches"].wait()


    @pl.loop(0, krows // SLAB)
    def _(w):
        gk, gv = g_keys[slab(w), :], g_values[slab(w), :]
        acc[1] += fold(gv)
        g = mm_lane(pack_left(gk), wk_l[...]) + mm_lane(pack_left(gv), wv_l[...])
        n = red_n[slab(w), :D]
        acc[2] += fold(g * n)
        acc[3] += fold(g)
        g = norm_back(g * gr, n, red_n[slab(w), D : D + 1])
        acc[4] += fold(g)
        grad[slab(w), :] = g

    tick(2.0)
    g_red = grad[0:krows, :]
    for pair in range(2):
        d_wr = jnp.concatenate([mm_rows(g_red, patches[2 * pair]), mm_rows(g_red, patches[2 * pair + 1])], 1)
        store(2 + 5 * pair, d_wr)
        tick(2.0, 1 if pair else None)
    reduced = red_n[:, :D] * gr + sr
    d_wk = mm_rows(reduced, g_keys[...])
    d_wv = mm_rows(reduced, g_values[...])
    store(12, jnp.concatenate([d_wk, d_wv], 1))
    tick(2.5, 2)
    for sub in range(4):
        wr_l[sub] = pack_down(wr[:, sub * D : sub * D + D])

    @pl.loop(0, krows // SLAB)
    def _(w):
        packed = pack_left(grad[slab(w), :])
        for sub in range(4):
            g_patch[sub, slab(w), :] = mm(packed, wr_l[sub])

    tick(2.0)
    planned_2 = ticks(blocks, 0.6)
    fetch["keys"].wait()
    fetch["first_n"].wait()

    @pl.loop(0, blocks)
    def _(b):
        head_block(keys, b, kb)
        place_window(g_query, b, mm(triple_left(g_scores[b]), triple_down(head_rows(kb))))
        run_at(b, planned_2)

    wq_l[...] = pack_lane(wq[...])

    @pl.loop(0, slabs)
    def _(w):
        acc[5] += fold(g_query[slab(w), :])
        grad[slab(w), :] = first_n[slab(w), :D] * g1 + b1

    d_wq = mm_rows(grad[...], g_query[...])
    store(17, jnp.concatenate([d_wo[:, 256:], d_wq], 1))
    tick(4.0, 3)
    planned_3 = ticks(slabs, 0.45)

    @pl.loop(0, slabs)
    def _(w):
        g_att[slab(w), :] = mm_lane(pack_left(g_query[slab(w), :]), wq_l[...])
        run_at(w, planned_3)

    planned_4 = ticks(blocks, 0.3)

    @pl.loop(0, blocks)
    def _(b):
        which = kinds[first + b] * 2 + b % 2
        here_k = pl.ds(pl.multiple_of(b * KPAD, 8), KPAD)
        high, low = split(jnp.concatenate([g_patch[sub, here_k, :] for sub in range(4)], 0))
        pick = table[which]
        dims = (((0,), (0,)), ((), ()))
        moved = lax.dot_general(pick, high, dims, preferred_element_type=f32)
        moved = moved + lax.dot_general(pick, low, dims, preferred_element_type=f32)
        g_att[pl.ds(window(b), WIN), :] += moved
        run_at(b, planned_4)

    planned_5 = ticks(slabs, 0.3)

    @pl.loop(0, slabs)
    def _(w):
        n, scale = first_n[slab(w), :D], first_n[slab(w), D : D + 1]
        g = g_att[slab(w), :]
        acc[6] += fold(g * n)
        acc[7] += fold(g)
        grad[slab(w), :] = g_after[slab(w), :] + norm_back(g * g1, n, scale)
        run_at(w, planned_5)

    order = (acc[6], acc[7], acc[5], acc[4], acc[2], acc[3], acc[1], acc[0], sums[0], sums[1], sums[2])
    value = jnp.concatenate([jnp.sum(x, 0, keepdims=True) for x in order] + [jnp.zeros((5, D), f32)], 0)
    value = jnp.concatenate([value, value[:, 256:]], 1)
    for t in range(3):
        small_sum[0, 16 * t : 16 * t + 16, :] = value[:, 128 * t : 128 * t + 128]
    exchange = Exchange(wires, small_sum, small_got)
    plan.add([exchange])
    run_steps(plan.rest())
    for t in range(3):
        small[:, 128 * t : 128 * t + 128] = small_sum[exchange.last, 16 * t : 16 * t + 16, :]


def attention_backward(pairs, cores, kinds, g_after, marks, vecs, wq, wr, wkv, wo, saved, sums, ff_pack):
    rows = g_after.shape[0]
    blocks = rows // BLOCK
    krows = blocks * KPAD
    bits = pairs.bit_length() - 1
    ff_total, total = sum_rows(pairs, cores)
    slots = 15 * (3 + 3 * bits)
    vm, far = pl.BlockSpec(memory_space=pltpu.VMEM), pl.BlockSpec(memory_space=pl.ANY)
    first_n, *saved = saved
    return pl.pallas_call(
        partial(backward_kernel, pairs, cores),
        out_shape=(
            jax.ShapeDtypeStruct((rows, D), f32),
            jax.ShapeDtypeStruct((ff_total, 128), f32),
            jax.ShapeDtypeStruct((cores, total, 128), f32),
            jax.ShapeDtypeStruct((16, 3 * 128), f32),
        ),
        in_specs=[pl.BlockSpec(memory_space=pltpu.SMEM), far] + [vm] * 11 + [far] * 7 + [vm, far],
        out_specs=(vm,) * 4,
        scratch_shapes=[pltpu.VMEM(x.shape, f32) for x in (first_n, *saved)]
        + [
            pltpu.VMEM((D, 1024), bf16),
            pltpu.VMEM((D, 1024), bf16),
            pltpu.VMEM((D, 1024), bf16),
            pltpu.VMEM((D, 1024), bf16),
            pltpu.VMEM((4, 1024, D), bf16),
            pltpu.VMEM((rows, D), f32),
            pltpu.VMEM((rows, D), f32),
            pltpu.VMEM((krows, D), f32),
            pltpu.VMEM((krows, D), f32),
            pltpu.VMEM((4, krows, D), f32),
            pltpu.VMEM((blocks, WIN, 256), f32),
            pltpu.VMEM((3, 256, 128), f32),
            pltpu.VMEM((3, 256, 128), f32),
            pltpu.VMEM((3, 256, 128), f32),
            pltpu.VMEM((8, 8, D), f32),
            pltpu.VMEM((ff_total, 128), f32),
            pltpu.VMEM((ff_total, 128), f32),
            pltpu.VMEM((ff_total, 128), f32),
            pltpu.VMEM((cores, total, 128), f32),
            pltpu.VMEM((total, 128), f32),
            pltpu.VMEM((total, 128), f32),
            pltpu.VMEM((bits + cores, 48, 128), f32),
            pltpu.VMEM((bits + cores, 48, 128), f32),
            pltpu.SemaphoreType.DMA((slots,)),
            pltpu.SemaphoreType.DMA((slots,)),
        ],
        compiler_params=pltpu.CompilerParams(
            collective_id=0 if pairs * cores > 1 else None, has_side_effects=True, vmem_limit_bytes=63 * MIB
        ),
        name="attention_back",
    )(
        kinds,
        first_n,
        g_after,
        marks,
        jnp.asarray(gather_table(), bf16),
        vecs[0],
        vecs[1],
        vecs[4],
        vecs[5],
        wq,
        wr,
        wkv,
        wo,
        *saved,
        sums,
        ff_pack,
    )


def unpack_kernel(grad, ff, rest, small, grad_t, d_we, d_ws, d_dw, d_be, d_bd, d_wr, d_wkv, d_wq, d_wo, *lines):
    cores = rest.shape[0]
    part = D // cores
    grad_t[...] = grad[...].T
    span = 2 * D + 16
    for t in range(d_we.shape[1] // 128):
        lanes = slice(128 * t, 128 * t + 128)
        d_we[:, lanes] = ff[t * span : t * span + D, :]
        d_ws[:, lanes] = ff[t * span + D : t * span + 2 * D, :]
        d_dw[:, lanes] = ff[t * span + 2 * D : t * span + 2 * D + 9, :]
    for row, ref in ((9, d_be), (10, d_bd)):
        at = 2 * D + row
        parts = [ff[t * span + at : t * span + at + 1, :] for t in range(d_we.shape[1] // 128)]
        ref[...] = jnp.concatenate(parts, 1).reshape(-1)
    for i, ref in enumerate(lines):
        ref[...] = small[i : i + 1, :D].reshape(-1)

    def tile(k):
        return jnp.concatenate([rest[h, k * part : k * part + part, :] for h in range(cores)], 0)

    for t in range(10):
        d_wr[:, 128 * t : 128 * t + 128] = tile(2 + t)
    for t in range(5):
        d_wkv[:, 128 * t : 128 * t + 128] = tile(12 + t)
    mixed = jnp.concatenate([tile(17 + t) for t in range(3)], 1)
    d_wo[...] = jnp.concatenate([tile(0), tile(1), mixed[:, :64]], 1)
    d_wq[...] = mixed[:, 64:]


def unpack(grad, ff, rest, small):
    cores = rest.shape[0]
    rows = grad.shape[0]
    chans = FF // cores
    vm = pl.BlockSpec(memory_space=pltpu.VMEM)
    shapes = [(D, rows), (D, chans), (D, chans), (9, chans), (chans,), (chans,)]
    shapes += [(D, 4 * D), (D, 2 * D), (D, D), (D, D)] + [(D,)] * 11
    return pl.pallas_call(
        unpack_kernel,
        out_shape=tuple(jax.ShapeDtypeStruct(x, f32) for x in shapes),
        in_specs=[vm] * 4,
        out_specs=(vm,) * len(shapes),
        compiler_params=pltpu.CompilerParams(vmem_limit_bytes=60 * MIB),
        name="unpack",
    )(grad, ff, rest, small)


def body(
    pairs,
    cores,
    tokens,
    block_kind,
    first_gain,
    first_bias,
    query_weight,
    query_bias,
    reduce_weight,
    reduce_bias,
    reduce_gain,
    reduce_shift,
    keyval_weight,
    value_bias,
    output_weight,
    output_bias,
    second_gain,
    second_shift,
    expand_weight,
    expand_bias,
    depth_weight,
    depth_bias,
    shrink_weight,
    shrink_bias,
    cotangent,
):
    own_taps = jnp.concatenate(
        [depth_weight, expand_bias[None], depth_bias[None], jnp.zeros((5, expand_bias.shape[0]), f32)], 0
    )
    hidden = [lax.all_gather(x, "hidden", axis=0) for x in (expand_weight, shrink_weight.T, own_taps)]
    vecs = (
        first_gain,
        first_bias,
        query_bias,
        reduce_bias,
        reduce_gain,
        reduce_shift,
        value_bias,
        output_bias,
    )
    late = (second_gain, second_shift, shrink_bias)
    weights = (query_weight, reduce_weight.T, keyval_weight, output_weight)
    after, marks, *saved = attention_forward(block_kind, tokens.T, vecs, *weights)
    result_t, g_after, ff_pack, sums = feed_forward(block_kind, after, cotangent.T, late, hidden)
    grad, ff_sum, rest, small = attention_backward(
        pairs, cores, block_kind, g_after, marks, vecs, *weights, saved, sums, ff_pack.reshape(-1, 128)
    )
    outs = unpack(grad, ff_sum, rest, small)
    grad_t, d_we, d_ws, d_dw, d_be, d_bd, d_wr, d_wkv, d_wq, d_wo, *small = outs
    return (
        result_t.T,
        grad_t.T,
        small[0],
        small[1],
        d_wq,
        small[2],
        d_wr.T,
        small[3],
        small[4],
        small[5],
        d_wkv,
        small[6],
        d_wo,
        small[7],
        small[8],
        small[9],
        d_we,
        d_be,
        d_dw,
        d_bd,
        d_ws.T,
        small[10],
    )


def solution(mesh):
    both = P(("dp", "hidden"), None)
    cols = P(None, "hidden")
    chan = P("hidden")
    deep = P("hidden", None)
    whole = P()
    return jax.shard_map(
        partial(body, mesh.shape["dp"], mesh.shape["hidden"]),
        mesh=mesh,
        in_specs=(both,) + (whole,) * 15 + (cols, chan, cols, chan, deep, whole, both),
        out_specs=(both, both) + (whole,) * 14 + (cols, chan, cols, chan, deep, whole),
        check_vma=False,
    )
```

```python
from functools import partial

import jax
import jax.numpy as jnp
import numpy as np
from jax import lax
from jax.experimental import pallas as pl
from jax.experimental.pallas import tpu as pltpu
from jax.sharding import PartitionSpec as P

HEADS = 5
HEAD = 64
BLOCK = 196
GRID = 14
SMALL = 6
SMALL_IMGS = 5
KVB = 49
D = 320
FF = 1280
KPAD = 56
WIN = 208
ODD = 184
CHUNK = 256
CHUNKS = FF // CHUNK
SLAB = 224
DEEP = 1024
PAD = 16
MIB = 1024 * 1024

f32 = jnp.float32
bf16 = jnp.bfloat16
MESH = pl.DeviceIdType.MESH


def gather_table():
    out = np.zeros((2, 2, 4 * KPAD, WIN), np.float32)
    for kind in range(2):
        for parity in range(2):
            off = 12 * parity
            for a in range(2):
                for b in range(2):
                    for key in range(KVB):
                        if kind == 0:
                            i, j = divmod(key, GRID // 2)
                            spot = (2 * i + a) * GRID + 2 * j + b
                        else:
                            if key >= 45:
                                continue
                            image, rest = divmod(key, 9)
                            i, j = divmod(rest, 3)
                            spot = image * 36 + (2 * i + a) * SMALL + 2 * j + b
                        out[kind, parity, (2 * a + b) * KPAD + key, off + spot] = 1.0
    return out.reshape(4, 4 * KPAD, WIN)


def score_table():
    out = np.full((2, 2, WIN, 256), -1e30, np.float32)
    for kind in range(2):
        for parity in range(2):
            off = 12 * parity
            for row in range(WIN):
                local = row - off
                for key in range(KVB):
                    if kind == 0 or local < 0 or local >= BLOCK:
                        good = True
                    else:
                        good = key < 45 and key // 9 == min(local // 36, 4)
                    if good:
                        for head in range(HEADS):
                            out[kind, parity, row, head * KVB + key] = 0.0
    return out.reshape(4, WIN, 256)


def row_table():
    out = np.zeros((2, 2, WIN, 128), np.float32)
    for parity in range(2):
        off = 12 * parity
        for row in range(BLOCK):
            i, j = divmod(row, GRID)
            out[0, parity, off + row, :7] = (1, j > 0, j < 13, i > 0, 0, i < 13, 0)
            if row < 180:
                i, j = divmod(row % 36, SMALL)
                out[1, parity, off + row, :7] = (1, j > 0, j < 5, 0, i > 0, 0, i < 5)
    return out.reshape(4, WIN, 128)


def split(x):
    high = x.astype(bf16)
    return high, (x - high.astype(f32)).astype(bf16)


def pack_left(x):
    high = x.astype(bf16).astype(f32)
    low = x - high
    tail = jnp.concatenate([high[:, 256:], low[:, 256:]], 1).astype(bf16)
    high, low = high[:, :256].astype(bf16), low[:, :256].astype(bf16)
    return jnp.concatenate([high, low, high, tail, tail], 1)


def pack_short(x):
    high = x.astype(bf16).astype(f32)
    low = x - high
    tail = jnp.concatenate([high[:, 256:], low[:, 256:]], 1).astype(bf16)
    return jnp.concatenate([high[:, :256].astype(bf16), low[:, :256].astype(bf16), tail], 1)


def pack_lane(w):
    high = w.astype(bf16).astype(f32)
    low = w - high
    tail_high = jnp.concatenate([high[:, 256:], high[:, 256:]], 1).astype(bf16)
    tail_low = jnp.concatenate([low[:, 256:], low[:, 256:]], 1).astype(bf16)
    high, low = high[:, :256].astype(bf16), low[:, :256].astype(bf16)
    return jnp.concatenate([high, high, low, tail_high, tail_low], 1)


def pack_down(w):
    high, low = split(w)
    return jnp.concatenate(
        [high[:256], high[:256], low[:256], high[256:], high[256:], low[256:], low[256:]], 0
    )


def triple_left(x):
    high, low = split(x)
    return jnp.concatenate([high, low, high], 1)


def triple_down(w):
    high, low = split(w)
    return jnp.concatenate([high, high, low], 0)


def triple_lane(w):
    high, low = split(w)
    return jnp.concatenate([high, high, low], 1)


def mm(a, b):
    return jnp.dot(a, b, preferred_element_type=f32)


def mm_lane(a, b):
    return lax.dot_general(a, b, (((1,), (1,)), ((), ())), preferred_element_type=f32)


def mm_rows(a, b):
    left_high, left_low = split(a.T)
    high, low = split(b)
    return mm(left_high, high) + mm(left_low, high) + mm(left_high, low)


def norm_rows(x):
    center = jnp.sum(x, -1, keepdims=True) * (1.0 / D)
    centered = x - center
    spread = jnp.sum(centered * centered, -1, keepdims=True) * (1.0 / D)
    scale = lax.rsqrt(spread + 1e-06)
    return centered * scale, scale


def norm_back(h, n, scale):
    mean_h = jnp.sum(h, -1, keepdims=True) * (1.0 / D)
    mean_hn = jnp.sum(h * n, -1, keepdims=True) * (1.0 / D)
    return scale * (h - mean_h - n * mean_hn)


def fold(x):
    return jnp.sum(x.reshape(x.shape[0] // 8, 8, x.shape[1]), 0)


def window(block):
    return pl.multiple_of((block // 2) * (2 * BLOCK) + (block % 2) * ODD, 8)


def slab(w):
    return pl.ds(pl.multiple_of(w * SLAB, SLAB), SLAB)


def place_window(ref, block, value):
    start = window(block)

    @pl.when(block % 2 == 0)
    def _():
        ref[pl.ds(start, WIN), :] = value

    @pl.when(block % 2 == 1)
    def _():
        edge = ref[pl.ds(start + 8, 8), :]
        rows = lax.broadcasted_iota(jnp.int32, edge.shape, 0)
        ref[pl.ds(start + 8, 8), :] = jnp.where(rows < 4, edge, value[8:16])
        ref[pl.ds(start + 16, WIN - 16), :] = value[16:]


def head_block(rows_ref, block, out_ref):
    start = pl.multiple_of(block * KPAD, 8)
    for head in range(HEADS):
        tile = head // 2
        if tile < 2:
            value = rows_ref[pl.ds(start, KPAD), tile * 128 : tile * 128 + 128]
            lane = lax.broadcasted_iota(jnp.int32, value.shape, 1)
            value = jnp.where((lane >= 64) == (head % 2 == 1), value, 0.0)
        else:
            half = rows_ref[pl.ds(start, KPAD), 256:320]
            value = jnp.concatenate([half, half], 1)
        out_ref[tile, head * KVB : head * KVB + KVB, :] = value[:KVB]


def head_rows(ref):
    return jnp.concatenate([ref[0], ref[1], ref[2][:, :64]], 1)


def head_unblock(ref, value):
    ref[0] = value[:, :128]
    ref[1] = value[:, 128:256]
    ref[2] = jnp.concatenate([value[:, 256:], value[:, 256:]], 1)
    lane = lax.broadcasted_iota(jnp.int32, (KPAD, 128), 1)
    row = lax.broadcasted_iota(jnp.int32, (KPAD, 128), 0)
    tiles = []
    for tile in range(3):
        first = ref[tile, 2 * tile * KVB : 2 * tile * KVB + KPAD, :]
        if tile < 2:
            second = ref[tile, (2 * tile + 1) * KVB : (2 * tile + 1) * KVB + KPAD, :]
            first = jnp.where(lane < 64, first, second)
        tiles.append(jnp.where(row < KVB, first, 0.0))
    return jnp.concatenate([tiles[0], tiles[1], tiles[2][:, :64]], 1)


def head_lane(ref):
    parts = []
    for tile in range(3):
        high = ref[tile].astype(bf16)
        parts.append((high, (ref[tile] - high.astype(f32)).astype(bf16)))
    return jnp.concatenate(
        [parts[0][0], parts[1][0], parts[0][0], parts[1][0], parts[0][1], parts[1][1], parts[2][0], parts[2][1]], 1
    )


def head_of_lane(shape):
    lane = lax.broadcasted_iota(jnp.int32, shape, 1)
    return [lane < (head + 1) * KVB for head in range(HEADS - 1)]


def by_head(below, values):
    out = values[HEADS - 1]
    for head in range(HEADS - 2, -1, -1):
        out = jnp.where(below[head], values[head], out)
    return out


def per_head(below, x, empty, reduce):
    out = []
    for head in range(HEADS):
        here = x
        if head < HEADS - 1:
            here = jnp.where(below[head], here, empty)
        if head > 0:
            here = jnp.where(below[head - 1], empty, here)
        out.append(reduce(here, axis=1, keepdims=True))
    return by_head(below, [jnp.broadcast_to(v, x.shape) for v in out])


def line(ref):
    return ref[...].reshape(1, -1)


def own_first(blocks):
    return (lax.axis_index("dp") * lax.axis_size("hidden") + lax.axis_index("hidden")) * blocks


def attention_kernel(
    kinds,
    tokens_t,
    table,
    scores_mask,
    row_marks,
    first_gain,
    first_bias,
    query_bias,
    reduce_bias,
    reduce_gain,
    reduce_shift,
    value_bias,
    output_bias,
    wq,
    wr,
    wkv,
    wo,
    after,
    *refs,
):
    held, refs = refs[:9], refs[9:]
    marks, first_n, query, attended, probs, keys, values, red_n, patches = refs[:9]
    wq_s, wo_s, wk_s, wv_s, wr_s, tokens, normed, kb, vb, sem = refs[9:]
    saves = [pltpu.make_async_copy(src, dst, sem.at[i]) for i, (src, dst) in enumerate(zip(refs, held))]
    blocks = probs.shape[0]
    slabs = tokens.shape[0] // SLAB
    first = own_first(blocks)
    g1, b1, bq, br = line(first_gain), line(first_bias), line(query_bias), line(reduce_bias)
    gr, sr, bv, bo = line(reduce_gain), line(reduce_shift), line(value_bias), line(output_bias)
    wq_s[...] = pack_down(wq[...])
    wo_s[...] = pack_down(wo[...])
    wk_s[...] = pack_down(wkv[:, :D])
    wv_s[...] = pack_down(wkv[:, D:])
    for sub in range(4):
        wr_s[sub] = pack_lane(wr[:, sub * D : sub * D + D])
    kb[...] = jnp.zeros_like(kb)
    vb[...] = jnp.zeros_like(vb)
    tokens[...] = tokens_t[...].T

    @pl.loop(0, slabs)
    def _(w):
        n, scale = norm_rows(tokens[slab(w), :])
        first_n[slab(w), :] = jnp.concatenate([n, jnp.broadcast_to(scale, (SLAB, 64))], 1)
        n = n * g1 + b1
        normed[slab(w), :] = n
        query[slab(w), :] = mm(pack_left(n), wq_s[...]) + bq

    saves[1].start()
    saves[2].start()

    @pl.loop(0, blocks)
    def _(b):
        which = kinds[first + b] * 2 + b % 2
        place_window(marks, b, row_marks[which])
        part = normed[pl.ds(window(b), WIN), :]
        high, low = split(part)
        pick = table[which]
        got = mm(pick, high) + mm(pick, low)
        rows = pl.ds(pl.multiple_of(b * KPAD, 8), KPAD)
        for sub in range(4):
            patches[sub, rows, :] = got[sub * KPAD : sub * KPAD + KPAD]

    saves[0].start()
    saves[8].start()

    @pl.loop(0, blocks * KPAD // SLAB)
    def _(w):
        acc = br + mm_lane(pack_left(patches[0, slab(w), :]), wr_s[0])
        for sub in range(1, 4):
            acc = acc + mm_lane(pack_left(patches[sub, slab(w), :]), wr_s[sub])
        n, scale = norm_rows(acc)
        red_n[slab(w), :] = jnp.concatenate([n, jnp.broadcast_to(scale, (SLAB, 64))], 1)
        packed = pack_left(n * gr + sr)
        keys[slab(w), :] = mm(packed, wk_s[...])
        values[slab(w), :] = mm(packed, wv_s[...]) + bv

    for i in (5, 6, 7):
        saves[i].start()

    @pl.loop(0, blocks)
    def _(b):
        which = kinds[first + b] * 2 + b % 2
        head_block(keys, b, kb)
        head_block(values, b, vb)
        q = query[pl.ds(window(b), WIN), :]
        s = mm_lane(pack_left(q), head_lane(kb)) * (HEAD**-0.5) + scores_mask[which]
        below = head_of_lane(s.shape)
        e = jnp.exp(s - per_head(below, s, -3e38, jnp.max))
        p = e / per_head(below, e, 0.0, jnp.sum)
        probs[b] = p
        out = mm(triple_left(p), triple_down(head_rows(vb)))
        place_window(attended, b, out)

    saves[3].start()
    saves[4].start()

    @pl.loop(0, slabs)
    def _(w):
        branch = mm(pack_left(attended[slab(w), :]), wo_s[...]) + bo
        after[slab(w), :] = tokens[slab(w), :] + marks[slab(w), 0:1] * branch

    for save in saves:
        save.wait()


def attention_forward(kinds, tokens_t, vecs, wq, wr, wkv, wo):
    rows = tokens_t.shape[1]
    blocks = rows // BLOCK
    krows = blocks * KPAD
    vm = pl.BlockSpec(memory_space=pltpu.VMEM)

    def shape(*dims):
        return jax.ShapeDtypeStruct(dims, f32)

    saved = (
        shape(rows, 128),
        shape(rows, D + 64),
        shape(rows, D),
        shape(rows, D),
        shape(blocks, WIN, 256),
        shape(krows, D),
        shape(krows, D),
        shape(krows, D + 64),
        shape(4, krows, D),
    )
    return pl.pallas_call(
        attention_kernel,
        out_shape=(shape(rows, D),) + saved,
        in_specs=[pl.BlockSpec(memory_space=pltpu.SMEM)] + [vm] * 16,
        out_specs=(vm,) + (pl.BlockSpec(memory_space=pl.ANY),) * 9,
        scratch_shapes=[pltpu.VMEM(x.shape, f32) for x in saved]
        + [
            pltpu.VMEM((1024, D), bf16),
            pltpu.VMEM((1024, D), bf16),
            pltpu.VMEM((1024, D), bf16),
            pltpu.VMEM((1024, D), bf16),
            pltpu.VMEM((4, D, 1024), bf16),
            pltpu.VMEM((rows, D), f32),
            pltpu.VMEM((rows, D), f32),
            pltpu.VMEM((3, 256, 128), f32),
            pltpu.VMEM((3, 256, 128), f32),
            pltpu.SemaphoreType.DMA((9,)),
        ],
        compiler_params=pltpu.CompilerParams(vmem_limit_bytes=60 * MIB),
        name="attention",
    )(
        kinds,
        tokens_t,
        jnp.asarray(gather_table(), bf16),
        jnp.asarray(score_table()),
        jnp.asarray(row_table()),
        *vecs,
        wq,
        wr,
        wkv,
        wo,
    )


ERF_P = 0.3275911
ERF = (0.254829592, -0.284496736, 1.421413741, -1.453152027, 1.061405429)


def gelu_pair(x):
    size = jnp.abs(x)
    d = 1.0 + (ERF_P * 0.7071067811865476) * size
    t = pl.reciprocal(d, approx=True)
    t = t * (2.0 - d * t)
    e = jnp.exp(-0.5 * (x * x))
    poly = t * (ERF[0] + t * (ERF[1] + t * (ERF[2] + t * (ERF[3] + t * ERF[4]))))
    tail = 0.5 * (poly * e)
    phi = jnp.where(x < 0.0, tail, 1.0 - tail)
    return x * phi, phi + x * (0.3989422804014327 * e)


def has_left(r):
    return r % GRID > 0, r < 180 and r % SMALL > 0


def has_right(r):
    return r % GRID < GRID - 1, r < 180 and r % SMALL < SMALL - 1


def has_up(r):
    return r >= GRID, r < 180 and r % 36 >= SMALL


def has_down(r):
    return r < BLOCK - GRID, r < 180 and r % 36 < 30


def total_of(values):
    values = [v for v in values if v is not None]
    out = values[0]
    for v in values[1:]:
        out = out + v
    return out


def forward_kernel(
    kinds,
    after,
    cot_t,
    second_gain,
    second_shift,
    shrink_bias,
    own_we,
    own_ws,
    own_taps,
    result_t,
    g_after,
    pack,
    sums,
    we_s,
    we_l,
    ws_s,
    ws_l,
    result,
    g_second,
    by_block,
    by_place,
    taps,
    second,
    branch,
    second_t,
    branch_t,
    xs0,
    xs1,
    nx1,
    ga0,
    ga1,
    ng1,
    y0,
    yu,
    yd,
    act,
    gx,
    held_act,
    held_gx,
    dwe,
    dws,
    sem,
):
    rows = after.shape[0]
    pieces = rows // SLAB
    per = FF // 128 // own_we.shape[0]
    g2, s2, bs = line(second_gain), line(second_shift), line(shrink_bias)
    first = own_first(8)
    block = lax.broadcasted_iota(jnp.int32, (8, 128), 0)
    kind = jnp.zeros((8, 128), jnp.int32)
    for i in range(8):
        kind = jnp.where(block == i, kinds[first + i], kind)
    zero_kind = kind == 0
    k0 = jnp.where(zero_kind, 1.0, 0.0)
    k1 = 1.0 - k0

    loads = []
    for tile in range(FF // 128):
        lanes = pl.ds((tile % per) * 128, 128)
        for i, (source, low, size) in enumerate(((own_we, 0, D), (own_ws, D, D), (own_taps, 2 * D, 16))):
            loads.append(
                pltpu.make_async_copy(
                    source.at[tile // per, :, lanes], pack.at[tile, pl.ds(low, size)], sem.at[3 * tile + i]
                )
            )
    for load in loads:
        load.start()

    held_act[...] = jnp.zeros_like(held_act)
    held_gx[...] = jnp.zeros_like(held_gx)
    sums[...] = jnp.zeros_like(sums)

    def tiles_of(x):
        return x[:, :128], x[:, 128:256], jnp.concatenate([x[:, 256:], x[:, 256:]], 1)

    def to_places(out):
        for t in range(3):
            for i in range(8):
                by_place[t, pl.ds(i, BLOCK, stride=8), :] = by_block[t, i * BLOCK : (i + 1) * BLOCK, :]

        @pl.loop(0, rows // SLAB)
        def _(w):
            out[slab(w), :] = joined(by_place, slab(w))

    def to_blocks(source):
        @pl.loop(0, rows // SLAB)
        def _(w):
            for t, value in enumerate(tiles_of(source[slab(w), :])):
                by_place[t, slab(w), :] = value

        for t in range(3):
            for i in range(8):
                by_block[t, i * BLOCK : (i + 1) * BLOCK, :] = by_place[t, pl.ds(i, BLOCK, stride=8), :]

    def joined(ref, at):
        return jnp.concatenate([ref[0, at, :], ref[1, at, :], ref[2, at, :][:, :64]], 1)

    for t in range(3):
        low, high = 128 * t, min(128 * t + 128, D)
        value = cot_t[low:high, :].T
        by_block[t] = value if high - low == 128 else jnp.concatenate([value, value], 1)
    to_places(result)

    @pl.loop(0, rows // SLAB)
    def _(w):
        for t, value in enumerate(tiles_of(after[slab(w), :])):
            by_block[t, slab(w), :] = value

    to_places(g_second)

    g_after[...] = result[...]
    dead = 180 * 8
    result[dead:, :] = (result[dead:, :].reshape(BLOCK - 180, 8, D) * k0[:, :1]).reshape(rows - dead, D)

    @pl.loop(0, rows // SLAB)
    def _(w):
        a = g_second[slab(w), :]
        for t, value in enumerate(tiles_of(a)):
            by_block[t, slab(w), :] = value
        n, _ = norm_rows(a)
        value = n * g2 + s2
        g_second[slab(w), :] = value
        second[slab(w), :] = pack_short(value)
        grad = result[slab(w), :]
        sums[2] += fold(grad)
        branch[slab(w), :] = pack_short(grad)

    for source, turned in ((g_second, second_t), (result, branch_t)):
        high, low = split(source[...].T)
        turned[...] = jnp.concatenate([high, low, high], 1)
    result[...] = jnp.zeros_like(result)
    g_second[...] = jnp.zeros_like(g_second)

    for load in loads:
        load.wait()
    for c in range(CHUNKS):
        for which, (down, lane) in enumerate(((we_s, we_l), (ws_s, ws_l))):
            value = jnp.concatenate([pack[2 * c + t, which * D : which * D + D, :] for t in range(2)], 1)
            high, low = split(value)
            down[c] = jnp.concatenate([high, low], 0)
            lane[c] = jnp.concatenate([high, low], 1)
        for t in range(2):
            for k in range(11):
                taps[c, t, k] = jnp.broadcast_to(pack[2 * c + t, 2 * D + k : 2 * D + k + 1, :], (8, 128))

    def own(h):
        return slice(h * SLAB, (h + 1) * SLAB)

    def left(ref, h):
        x = ref[own(h), :]
        return jnp.concatenate([x[:, :512], x[:, :256], x[:, 512:], x[:, 512:]], 1)

    def deep(ref, c):
        x = ref[c]
        return jnp.concatenate(
            [x[:256], x[:256], x[D : D + 256], x[256:D], x[256:D], x[D + 256 :], x[D + 256 :]], 0
        )

    def expand_task(c, h, outs):
        e = mm(left(second, h), deep(we_s, c))
        for t in range(2):
            outs[t][own(h), :] = e[:, 128 * t : 128 * t + 128] + taps[c, t, 9][0:1]

    def active_grad_task(c, h, outs):
        g = mm(left(branch, h), deep(ws_s, c))
        for t in range(2):
            outs[t][own(h), :] = g[:, 128 * t : 128 * t + 128]

    def out_task(c, h, source, lane, out):
        x = source[own(h), :]
        weight = lane[c]
        out[own(h), :] += mm_lane(
            jnp.concatenate([x, x[:, :256]], 1), jnp.concatenate([weight[:, :256], weight], 1)
        )

    def weight_task(c, source, turned, row, total, k):
        span = slice(k * DEEP, min((k + 1) * DEEP, 3 * rows))
        parts = []
        for i, low in enumerate((0, 0, CHUNK)):
            start, stop = max(span.start, i * rows) - i * rows, min(span.stop, (i + 1) * rows) - i * rows
            if start < stop:
                parts.append(source[start:stop, low : low + CHUNK])
        value = mm(turned[:, span], jnp.concatenate(parts, 0) if len(parts) > 1 else parts[0])
        if k > 0:
            value = value + total[...]
        if span.stop < 3 * rows:
            total[...] = value
            return
        for t in range(2):
            pack[2 * c + t, row : row + D, :] = value[:, 128 * t : 128 * t + 128]

    def early_tasks(c, x_outs, g_outs):
        out = []
        for h in range(pieces):
            out += [partial(expand_task, c, h, x_outs), partial(active_grad_task, c, h, g_outs)]
        return out

    def late_tasks(c):
        out = []
        for h in range(pieces):
            out += [
                partial(out_task, c, h, held_act, ws_l, result),
                partial(out_task, c, h, held_gx, we_l, g_second),
            ]
        return out

    def weight_tasks(c):
        count = -(-3 * rows // DEEP)
        first_half = [partial(weight_task, c, held_act, branch_t, D, dws, k) for k in range(count)]
        return first_half, [partial(weight_task, c, held_gx, second_t, 0, dwe, k) for k in range(count)]

    def woven(a, b):
        out = list(a)
        for i, task in enumerate(b):
            out.insert(round((i + 1) * len(a) / (len(b) + 1)) + i, task)
        return out

    def at(r):
        return slice(8 * r, 8 * r + 8)

    def gated(value, ok):
        if ok[0] and ok[1]:
            return value
        if ok[0]:
            return value * k0
        return value * k1 if ok[1] else None

    def picked(ref, r, ok, sign):
        if ok[0] and ok[1]:
            return jnp.where(zero_kind, ref[at(r + sign * GRID), :], ref[at(r + sign * SMALL), :])
        if ok[0]:
            return ref[at(r + sign * GRID), :] * k0
        return ref[at(r + sign * SMALL), :] * k1 if ok[1] else None

    def put_split(ref, t, r, pair):
        high, low = split(jnp.concatenate(pair, 0))
        here = slice(8 * r, 8 * r + 16)
        ref[here, 128 * t : 128 * t + 128] = high
        ref[here, 256 + 128 * t : 384 + 128 * t] = low

    def item(c, t, x, g, tasks):
        tap = [taps[c, t, k] for k in range(11)]
        totals = [jnp.zeros((8, 128), f32)] * 11

        def columns(r, near):
            return [
                gated(near(r - 1), has_left(r)) if r > 0 else None,
                near(r),
                gated(near(r + 1), has_right(r)) if r + 1 < BLOCK else None,
            ]

        def mix(values, ks, more=()):
            return total_of([None if v is None else v * tap[k] for v, k in zip(values, ks)] + list(more))

        def loader():
            kept = {}

            def near(r):
                if r not in kept:
                    kept[r] = x[at(r), :]
                return kept[r]

            return near

        ahead, behind = loader(), loader()
        moved_back = {}
        every = {}
        count = (BLOCK + 30) // 2
        slots = {round((i + 0.5) * count / len(tasks)): task for i, task in enumerate(tasks)}
        for step in range(count):
            for r in (2 * step, 2 * step + 1):
                if r < BLOCK:
                    cols = columns(r, ahead)
                    yu[at(r), :] = mix(cols, (0, 1, 2))
                    y0[at(r), :] = mix(cols, (3, 4, 5), (tap[10],))
                    yd[at(r), :] = mix(cols, (6, 7, 8))
            r = 2 * step - 14
            if 0 <= r < BLOCK:
                conv = [
                    total_of([y0[at(s), :], picked(yu, s, has_up(s), -1), picked(yd, s, has_down(s), 1)])
                    for s in (r, r + 1)
                ]
                active, slope = gelu_pair(jnp.concatenate(conv, 0))
                put_split(act, t, r, [active[:8], active[8:]])
                here = slice(8 * r, 8 * r + 16)
                g[here, :] = g[here, :] * slope
            for r in (2 * step - 28, 2 * step - 27):
                if 0 <= r < BLOCK:
                    same = g[at(r), :]
                    moved = [picked(g, r, has_down(r), 1), same, picked(g, r, has_up(r), -1)]
                    cols = columns(r, behind)
                    totals[10] = totals[10] + same
                    for p in range(3):
                        for q in range(3):
                            if moved[p] is not None and cols[q] is not None:
                                totals[3 * p + q] = totals[3 * p + q] + moved[p] * cols[q]
                    moved_back[r] = [mix(moved, ks) for ks in ((0, 3, 6), (1, 4, 7), (2, 5, 8))]
            r = 2 * step - 30
            if 0 <= r < BLOCK:
                pair = []
                for s in (r, r + 1):
                    value = total_of(
                        [
                            moved_back[s][1],
                            gated(moved_back[s - 1][2], has_left(s)) if s > 0 else None,
                            gated(moved_back[s + 1][0], has_right(s)) if s + 1 < BLOCK else None,
                        ]
                    )
                    totals[9] = totals[9] + value
                    pair.append(value)
                put_split(gx, t, r, pair)
            if step in slots:
                slots[step]()
        for k in range(11):
            pack[2 * c + t, 2 * D + k : 2 * D + k + 1, :] = jnp.sum(totals[k], 0, keepdims=True)

    for task in early_tasks(0, (xs0, xs1), (ga0, ga1)):
        task()

    @pl.loop(0, CHUNKS)
    def _(c):
        before = jnp.maximum(c - 1, 0)
        item(c, 0, xs0, ga0, woven(late_tasks(before), weight_tasks(before)[0]))
        later = jnp.minimum(c + 1, CHUNKS - 1)
        item(c, 1, xs1, ga1, woven(early_tasks(later, (xs0, nx1), (ga0, ng1)), weight_tasks(before)[1]))
        xs1[...] = nx1[...]
        ga1[...] = ng1[...]
        held_act[...] = act[...]
        held_gx[...] = gx[...]

    for task in late_tasks(CHUNKS - 1) + sum(weight_tasks(CHUNKS - 1), []):
        task()
    for c in range(CHUNKS):
        for t in range(2):
            pack[2 * c + t, 2 * D + 11 : 2 * D + 16, :] = jnp.zeros((5, 128), f32)

    result[dead:, :] = ((result[dead:, :] + bs).reshape(BLOCK - 180, 8, D) * k0[:, :1]).reshape(rows - dead, D) - bs

    @pl.loop(0, rows // SLAB)
    def _(w):
        a = joined(by_block, slab(w))
        result[slab(w), :] = a + (result[slab(w), :] + bs)
        n, scale = norm_rows(a)
        g = g_second[slab(w), :]
        sums[0] += fold(g * n)
        sums[1] += fold(g)
        g_second[slab(w), :] = g_after[slab(w), :] + norm_back(g * g2, n, scale)

    to_blocks(result)
    for t in range(3):
        low, high = 128 * t, min(128 * t + 128, D)
        result_t[low:high, :] = by_block[t].T[: high - low]
    to_blocks(g_second)

    @pl.loop(0, rows // SLAB)
    def _(w):
        g_after[slab(w), :] = joined(by_block, slab(w))


def feed_forward(kinds, after, cot_t, vecs, weights):
    rows = after.shape[0]
    vm = pl.BlockSpec(memory_space=pltpu.VMEM)
    tile = pltpu.VMEM((rows, 128), f32)
    half = pltpu.VMEM((rows, 2 * CHUNK), bf16)
    return pl.pallas_call(
        forward_kernel,
        out_shape=(
            jax.ShapeDtypeStruct((D, rows), f32),
            jax.ShapeDtypeStruct((rows, D), f32),
            jax.ShapeDtypeStruct((2 * CHUNKS, 2 * D + 16, 128), f32),
            jax.ShapeDtypeStruct((3, 8, D), f32),
        ),
        in_specs=[pl.BlockSpec(memory_space=pltpu.SMEM)] + [vm] * 5 + [pl.BlockSpec(memory_space=pl.ANY)] * 3,
        out_specs=(vm,) * 4,
        scratch_shapes=[
            pltpu.VMEM((CHUNKS, 2 * D, CHUNK), bf16),
            pltpu.VMEM((CHUNKS, D, 2 * CHUNK), bf16),
            pltpu.VMEM((CHUNKS, 2 * D, CHUNK), bf16),
            pltpu.VMEM((CHUNKS, D, 2 * CHUNK), bf16),
            pltpu.VMEM((rows, D), f32),
            pltpu.VMEM((rows, D), f32),
            pltpu.VMEM((3, rows, 128), f32),
            pltpu.VMEM((3, rows, 128), f32),
            pltpu.VMEM((CHUNKS, 2, 11, 8, 128), f32),
            pltpu.VMEM((rows, 640), bf16),
            pltpu.VMEM((rows, 640), bf16),
            pltpu.VMEM((D, 3 * rows), bf16),
            pltpu.VMEM((D, 3 * rows), bf16),
        ]
        + [tile] * 9
        + [half] * 4
        + [pltpu.VMEM((D, CHUNK), f32)] * 2
        + [pltpu.SemaphoreType.DMA((6 * CHUNKS,))],
        compiler_params=pltpu.CompilerParams(vmem_limit_bytes=63 * MIB),
        name="feed_forward",
    )(kinds, after, cot_t, *vecs, *weights)


class Wires:
    def __init__(self, pairs, cores, send, recv):
        self.bits = pairs.bit_length() - 1
        self.cores = cores
        self.me, self.core = lax.axis_index("dp"), lax.axis_index("hidden")
        self.other = cores - 1 - self.core
        self.send, self.recv, self.used = send, recv, 0

    def groups(self):
        rest = list(range(2, self.bits))
        return [(k,) for k in range(min(2, self.bits))] + [tuple(rest[i : i + 2]) for i in range(0, len(rest), 2)]

    def bit(self, k):
        return (self.me // (1 << k)) % 2

    def peer(self, group, j):
        flips = [(1 - 2 * self.bit(k)) * (1 << k) for i, k in enumerate(group) if (j >> i) & 1]
        return (sum(flips, self.me), self.core)

    def place(self, group, j):
        bits = [(1 - self.bit(k) if (j >> i) & 1 else self.bit(k)) * (1 << i) for i, k in enumerate(group)]
        return sum(bits[1:], bits[0])

    def greet(self):
        peers = [self.peer(group, j) for group in self.groups() for j in range(1, 1 << len(group))]
        if self.cores > 1:
            peers.append((self.me, self.other))
        if not peers:
            return
        barrier = pltpu.get_barrier_semaphore()
        for target in peers:
            pl.semaphore_signal(barrier, inc=1, device_id=target, device_id_type=MESH)
        pl.semaphore_wait(barrier, len(peers))

    def copy(self, src, dst, target):
        slot = self.used
        self.used += 1
        return pltpu.make_async_remote_copy(
            src_ref=src,
            dst_ref=dst,
            send_sem=self.send.at[slot],
            recv_sem=self.recv.at[slot],
            device_id=target,
            device_id_type=MESH,
        )

    def local(self, src, dst):
        slot = self.used
        self.used += 1
        return pltpu.make_async_copy(src, dst, self.send.at[slot])

    def sibling(self, src, dst):
        return self.copy(src, dst, (self.me, self.other))


def rows_of(start, size):
    return pl.ds(pl.multiple_of(start, 8), size)


class Chain:
    def __init__(self, wires, acc, near, got, full, base, rows, order, opening, closing):
        self.stages, self.costs = [], []
        whole = pl.ds(base, rows)
        scale = 512 * wires.cores / LINK

        def meet():
            if near is not None:
                acc[whole, :] = acc[whole, :] + near[whole, :]

        start, size, spot = base + 0 * wires.me, rows, base
        pending, action = opening, meet
        self.stages.append(([], None, opening))
        self.costs.append(("core", rows * 512 / CORE_LINK))
        held = []
        for group in order:
            many = 1 << len(group)
            size //= many
            keep = start + wires.place(group, 0) * size
            copies, lands = [], []
            for j in range(1, many):
                land = pl.ds(spot, size)
                spot += size
                give = start + wires.place(group, j) * size
                copies.append(wires.copy(acc.at[rows_of(give, size)], got.at[land], wires.peer(group, j)))
                lands.append(land)
            self.stages.append((pending, action, copies))
            self.costs.append((group, scale * size * (1 if many == 2 else many)))

            def add(keep=keep, lands=lands, size=size):
                value = acc[rows_of(keep, size), :]
                for land in lands:
                    value = value + got[land, :]
                acc[rows_of(keep, size), :] = value

            pending, action = copies, add
            held.append((group, start))
            start = keep
        last, last_start, last_size = action, start, size

        def settle():
            last()
            full[rows_of(last_start, last_size), :] = acc[rows_of(last_start, last_size), :]

        action = settle
        for group, before in reversed(held):
            mine = rows_of(start, size)
            many = 1 << len(group)
            copies = [wires.copy(full.at[mine], full.at[mine], wires.peer(group, j)) for j in range(1, many)]
            self.stages.append((pending, action, copies))
            self.costs.append((group, scale * size * (1 if many == 2 else many)))
            pending, action = copies, None
            start, size = before, size * many
        if closing:
            self.stages.append((pending, action, closing))
            self.costs.append(("core", rows * 512 / CORE_LINK))
            pending, action = closing, None
        self.stages.append((pending, action, []))
        self.costs.append((None, 0.0))

    def run(self, stage):
        waits, action, starts = self.stages[stage]
        for c in waits:
            c.wait()
        if action is not None:
            action()
        for c in starts:
            c.start()


class Exchange(Chain):
    def __init__(self, wires, sums, got):
        partners = [((k,), wires.peer((k,), 1)) for k in range(wires.bits)]
        if wires.cores > 1:
            partners.insert(0, ("core", (wires.me, wires.other)))
        self.stages, self.costs = [], []
        pending, action = [], None
        for i, (name, target) in enumerate(partners):
            c = wires.copy(sums.at[i], got.at[i], target)
            self.stages.append((pending, action, [c]))
            self.costs.append((name, 0.5))

            def add(i=i):
                sums[i + 1] = sums[i] + got[i]

            pending, action = [c], add
        self.stages.append((pending, action, []))
        self.costs.append((None, 0.0))
        self.last = len(partners)


LINK = 100e3
CORE_LINK = 400e3
DELAY = 2.5
STEP_WORK = 0.1


class Plan:
    def __init__(self):
        self.now, self.free, self.going = 0.0, {}, []

    def add(self, chains):
        self.going += [[self.now, c, 0] for c in chains]

    def after(self, us):
        self.now += us
        due = []
        while True:
            ready = [g for g in self.going if g[0] <= self.now]
            if not ready:
                return due
            due.append(self.take(min(ready, key=lambda g: g[0])))

    def take(self, entry):
        done, chain, stage = entry
        self.now = max(self.now, done) + STEP_WORK
        link, us = chain.costs[stage]
        self.free[link] = max(self.free.get(link, 0.0), self.now) + us
        if stage + 1 == len(chain.stages):
            self.going.remove(entry)
        else:
            entry[0], entry[2] = self.free[link] + DELAY, stage + 1
        return chain, stage

    def rest(self):
        due = []
        while self.going:
            due.append(self.take(min(self.going, key=lambda g: g[0])))
        return due


def run_steps(steps):
    for chain, stage in steps:
        chain.run(stage)


def axis_orders(groups):
    return groups, groups[1::-1] + groups[2:], groups[2:] + groups[:2]


def cut(total, unit, parts):
    units = total // unit
    marks = sorted({0, units} | {round(units * x) for x in parts})
    return [(a * unit, b * unit) for a, b in zip(marks, marks[1:])]


def round_up(x, unit):
    return -(-x // unit) * unit


def sum_rows(pairs, cores):
    unit = 8 * pairs
    ff = round_up(2 * CHUNKS // cores * (2 * D + 16), unit)
    rest = round_up(20 * (D // cores), unit)
    return ff, rest


def backward_kernel(
    pairs,
    cores,
    kinds,
    first_n_from,
    g_after,
    marks,
    table,
    first_gain,
    first_bias,
    reduce_gain,
    reduce_shift,
    wq,
    wr,
    wkv,
    wo,
    query_from,
    attended_from,
    probs_from,
    keys_from,
    values_from,
    red_n_from,
    patches_from,
    sums,
    ff_pack,
    grad,
    ff_full,
    full,
    small,
    first_n,
    query,
    attended,
    probs,
    keys,
    values,
    red_n,
    patches,
    wq_l,
    wo_l,
    wk_l,
    wv_l,
    wr_l,
    g_att,
    g_query,
    g_keys,
    g_values,
    g_patch,
    g_scores,
    kb,
    vb,
    tmp,
    acc,
    ff_acc,
    ff_near,
    ff_got,
    big,
    near,
    got,
    small_sum,
    small_got,
    send,
    recv,
):
    blocks = probs.shape[0]
    rows = g_after.shape[0]
    slabs = rows // SLAB
    krows = blocks * KPAD
    first = own_first(blocks)
    part = D // cores
    g1, b1, gr, sr = line(first_gain), line(first_bias), line(reduce_gain), line(reduce_shift)

    wires = Wires(pairs, cores, send, recv)
    core = wires.core
    orders = axis_orders(wires.groups())
    unit = 8 * pairs
    ff_real = ff_pack.shape[0] // cores
    ff_total, total = ff_acc.shape[0], big.shape[1]
    if ff_total > ff_real:
        ff_acc[ff_real:, :] = jnp.zeros((ff_total - ff_real, 128), f32)
        ff_near[ff_real:, :] = jnp.zeros((ff_total - ff_real, 128), f32)
    if total > 20 * part:
        for h in range(cores):
            big[h, 20 * part :, :] = jnp.zeros((total - 20 * part, 128), f32)
    wires.greet()
    ff_chains = []
    for i, (low, high) in enumerate(cut(ff_total, unit, (11 / 26, 22 / 26))):
        size = min(high, ff_real) - low
        here = pl.ds(low, size)
        opening = [wires.local(ff_pack.at[rows_of(core * ff_real + low, size)], ff_acc.at[here])]
        if cores > 1:
            opening.append(wires.sibling(ff_pack.at[rows_of(wires.other * ff_real + low, size)], ff_near.at[here]))
        ff_chains.append(
            Chain(
                wires,
                ff_acc,
                ff_near if cores > 1 else None,
                ff_got,
                ff_full,
                low,
                high - low,
                orders[i],
                opening,
                [],
            )
        )
    bounds = [10 * part, 15 * part, 17 * part]
    chains = []
    cuts = cut(total, unit, (6 / 25, 12 / 25, 15 / 25, 18 / 25, 19 / 25, 22 / 25))
    for i, (low, high) in enumerate(cuts):
        here = pl.ds(low, high - low)
        opening, closing = [], []
        if cores > 1:
            opening = [wires.sibling(big.at[wires.other, here], near.at[here])]
            closing = [wires.sibling(full.at[core, here], full.at[core, here])]
        chain = Chain(
            wires,
            big.at[core],
            near if cores > 1 else None,
            got,
            full.at[core],
            low,
            high - low,
            orders[(0, 1, 0, 1, 2, 0, 1)[i]],
            opening,
            closing,
        )
        chain.ready = sum(high > x for x in bounds)
        chains.append(chain)
    fetch = {
        name: wires.local(src, dst)
        for name, src, dst in (
            ("values", values_from, values),
            ("probs", probs_from, probs),
            ("query", query_from, query),
            ("red_n", red_n_from, red_n),
            ("patches", patches_from, patches),
            ("attended", attended_from, attended),
            ("keys", keys_from, keys),
            ("first_n", first_n_from, first_n),
        )
    }
    plan = Plan()
    plan.add(ff_chains)

    def tick(us, level=None):
        run_steps(plan.after(us))
        if level is not None:
            plan.add([c for c in chains if c.ready == level])
            run_steps(plan.after(0.0))

    def ticks(count, us):
        return [plan.after(us) for _ in range(count)]

    def run_at(index, planned):
        for i, steps in enumerate(planned):
            if steps:
                pl.when(index == i)(partial(run_steps, steps))

    def store(tile, value):
        for t in range(value.shape[1] // 128):
            for h in range(cores):
                big[h, (tile + t) * part : (tile + t + 1) * part, :] = value[
                    h * part : (h + 1) * part, 128 * t : 128 * t + 128
                ]

    tick(0.0)
    for c in fetch.values():
        c.start()
    wo_l[...] = pack_lane(wo[...])
    wk_l[...] = pack_lane(wkv[:, :D])
    wv_l[...] = pack_lane(wkv[:, D:])
    kb[...] = jnp.zeros_like(kb)
    vb[...] = jnp.zeros_like(vb)
    acc[...] = jnp.zeros_like(acc)
    tick(2.0)
    planned_0 = ticks(slabs, 0.6)

    @pl.loop(0, slabs)
    def _(w):
        g = marks[slab(w), 0:1] * g_after[slab(w), :]
        grad[slab(w), :] = g
        acc[0] += fold(g)
        g_att[slab(w), :] = mm_lane(pack_left(g), wo_l[...])
        run_at(w, planned_0)

    planned_1 = ticks(blocks, 1.8)
    for name in ("values", "probs", "query"):
        fetch[name].wait()

    @pl.loop(0, blocks)
    def _(b):
        head_block(values, b, vb)
        here = pl.ds(window(b), WIN)
        first_row = 12 * (b % 2)
        row = lax.broadcasted_iota(jnp.int32, (WIN, D), 0)
        inside = (row >= first_row) & (row < first_row + BLOCK)
        ga = jnp.where(inside, g_att[here, :], 0.0)
        p = probs[b]
        gp = mm_lane(pack_left(ga), head_lane(vb))
        below = head_of_lane(p.shape)
        gs = p * (gp - per_head(below, gp * p, 0.0, jnp.sum)) * (HEAD**-0.5)
        g_scores[b] = gs
        here_k = pl.ds(pl.multiple_of(b * KPAD, 8), KPAD)
        g_values[here_k, :] = head_unblock(tmp, mm_rows(p, ga))
        g_keys[here_k, :] = head_unblock(tmp, mm_rows(gs, query[here, :]))
        run_at(b, planned_1)

    fetch["red_n"].wait()
    fetch["patches"].wait()


    @pl.loop(0, krows // SLAB)
    def _(w):
        gk, gv = g_keys[slab(w), :], g_values[slab(w), :]
        acc[1] += fold(gv)
        g = mm_lane(pack_left(gk), wk_l[...]) + mm_lane(pack_left(gv), wv_l[...])
        n = red_n[slab(w), :D]
        acc[2] += fold(g * n)
        acc[3] += fold(g)
        g = norm_back(g * gr, n, red_n[slab(w), D : D + 1])
        acc[4] += fold(g)
        g_query[slab(w), :] = g

    tick(2.0)
    g_red = g_query[0:krows, :]
    for pair in range(2):
        d_wr = jnp.concatenate([mm_rows(g_red, patches[2 * pair]), mm_rows(g_red, patches[2 * pair + 1])], 1)
        store(5 * pair, d_wr)
        tick(2.0, 0 if pair else None)
    reduced = red_n[:, :D] * gr + sr
    d_wk = mm_rows(reduced, g_keys[...])
    d_wv = mm_rows(reduced, g_values[...])
    store(10, jnp.concatenate([d_wk, d_wv], 1))
    tick(2.5, 1)
    fetch["attended"].wait()
    d_wo = mm_rows(attended[...], grad[...])
    store(15, d_wo[:, :256])
    tick(3.5, 2)
    for sub in range(4):
        wr_l[sub] = pack_down(wr[:, sub * D : sub * D + D])

    @pl.loop(0, krows // SLAB)
    def _(w):
        packed = pack_left(g_query[slab(w), :])
        for sub in range(4):
            g_patch[sub, slab(w), :] = mm(packed, wr_l[sub])

    tick(2.0)
    planned_2 = ticks(blocks, 0.6)
    fetch["keys"].wait()
    fetch["first_n"].wait()

    @pl.loop(0, blocks)
    def _(b):
        head_block(keys, b, kb)
        place_window(g_query, b, mm(triple_left(g_scores[b]), triple_down(head_rows(kb))))
        run_at(b, planned_2)

    wq_l[...] = pack_lane(wq[...])

    @pl.loop(0, slabs)
    def _(w):
        acc[5] += fold(g_query[slab(w), :])
        grad[slab(w), :] = first_n[slab(w), :D] * g1 + b1

    d_wq = mm_rows(grad[...], g_query[...])
    store(17, jnp.concatenate([d_wo[:, 256:], d_wq], 1))
    tick(4.0, 3)
    planned_3 = ticks(slabs, 0.45)

    @pl.loop(0, slabs)
    def _(w):
        g_att[slab(w), :] = mm_lane(pack_left(g_query[slab(w), :]), wq_l[...])
        run_at(w, planned_3)

    planned_4 = ticks(blocks, 0.3)

    @pl.loop(0, blocks)
    def _(b):
        which = kinds[first + b] * 2 + b % 2
        here_k = pl.ds(pl.multiple_of(b * KPAD, 8), KPAD)
        high, low = split(jnp.concatenate([g_patch[sub, here_k, :] for sub in range(4)], 0))
        pick = table[which]
        dims = (((0,), (0,)), ((), ()))
        moved = lax.dot_general(pick, high, dims, preferred_element_type=f32)
        moved = moved + lax.dot_general(pick, low, dims, preferred_element_type=f32)
        g_att[pl.ds(window(b), WIN), :] += moved
        run_at(b, planned_4)

    planned_5 = ticks(slabs, 0.3)

    @pl.loop(0, slabs)
    def _(w):
        n, scale = first_n[slab(w), :D], first_n[slab(w), D : D + 1]
        g = g_att[slab(w), :]
        acc[6] += fold(g * n)
        acc[7] += fold(g)
        grad[slab(w), :] = g_after[slab(w), :] + norm_back(g * g1, n, scale)
        run_at(w, planned_5)

    order = (acc[6], acc[7], acc[5], acc[4], acc[2], acc[3], acc[1], acc[0], sums[0], sums[1], sums[2])
    value = jnp.concatenate([jnp.sum(x, 0, keepdims=True) for x in order] + [jnp.zeros((5, D), f32)], 0)
    value = jnp.concatenate([value, value[:, 256:]], 1)
    for t in range(3):
        small_sum[0, 16 * t : 16 * t + 16, :] = value[:, 128 * t : 128 * t + 128]
    exchange = Exchange(wires, small_sum, small_got)
    plan.add([exchange])
    run_steps(plan.rest())
    for t in range(3):
        small[:, 128 * t : 128 * t + 128] = small_sum[exchange.last, 16 * t : 16 * t + 16, :]


def attention_backward(pairs, cores, kinds, g_after, marks, vecs, wq, wr, wkv, wo, saved, sums, ff_pack):
    rows = g_after.shape[0]
    blocks = rows // BLOCK
    krows = blocks * KPAD
    bits = pairs.bit_length() - 1
    ff_total, total = sum_rows(pairs, cores)
    slots = 15 * (3 + 3 * bits)
    vm, far = pl.BlockSpec(memory_space=pltpu.VMEM), pl.BlockSpec(memory_space=pl.ANY)
    first_n, *saved = saved
    return pl.pallas_call(
        partial(backward_kernel, pairs, cores),
        out_shape=(
            jax.ShapeDtypeStruct((rows, D), f32),
            jax.ShapeDtypeStruct((ff_total, 128), f32),
            jax.ShapeDtypeStruct((cores, total, 128), f32),
            jax.ShapeDtypeStruct((16, 3 * 128), f32),
        ),
        in_specs=[pl.BlockSpec(memory_space=pltpu.SMEM), far] + [vm] * 11 + [far] * 7 + [vm, far],
        out_specs=(vm,) * 4,
        scratch_shapes=[pltpu.VMEM(x.shape, f32) for x in (first_n, *saved)]
        + [
            pltpu.VMEM((D, 1024), bf16),
            pltpu.VMEM((D, 1024), bf16),
            pltpu.VMEM((D, 1024), bf16),
            pltpu.VMEM((D, 1024), bf16),
            pltpu.VMEM((4, 1024, D), bf16),
            pltpu.VMEM((rows, D), f32),
            pltpu.VMEM((rows, D), f32),
            pltpu.VMEM((krows, D), f32),
            pltpu.VMEM((krows, D), f32),
            pltpu.VMEM((4, krows, D), f32),
            pltpu.VMEM((blocks, WIN, 256), f32),
            pltpu.VMEM((3, 256, 128), f32),
            pltpu.VMEM((3, 256, 128), f32),
            pltpu.VMEM((3, 256, 128), f32),
            pltpu.VMEM((8, 8, D), f32),
            pltpu.VMEM((ff_total, 128), f32),
            pltpu.VMEM((ff_total, 128), f32),
            pltpu.VMEM((ff_total, 128), f32),
            pltpu.VMEM((cores, total, 128), f32),
            pltpu.VMEM((total, 128), f32),
            pltpu.VMEM((total, 128), f32),
            pltpu.VMEM((bits + cores, 48, 128), f32),
            pltpu.VMEM((bits + cores, 48, 128), f32),
            pltpu.SemaphoreType.DMA((slots,)),
            pltpu.SemaphoreType.DMA((slots,)),
        ],
        compiler_params=pltpu.CompilerParams(
            collective_id=0 if pairs * cores > 1 else None, has_side_effects=True, vmem_limit_bytes=63 * MIB
        ),
        name="attention_back",
    )(
        kinds,
        first_n,
        g_after,
        marks,
        jnp.asarray(gather_table(), bf16),
        vecs[0],
        vecs[1],
        vecs[4],
        vecs[5],
        wq,
        wr,
        wkv,
        wo,
        *saved,
        sums,
        ff_pack,
    )


def unpack_kernel(grad_from, ff_from, rest_from, small, *refs):
    outs, (d_dw, d_be, d_bd, *lines), refs = refs[:7], refs[7:21], refs[21:]
    grad, ff, rest = refs[:3]
    grad_t, d_we, d_ws, d_wr, d_wkv, d_wq, d_wo = refs[3:10]
    sem = refs[10]
    loads = [
        pltpu.make_async_copy(src, dst, sem.at[i])
        for i, (src, dst) in enumerate(((grad_from, grad), (ff_from, ff), (rest_from, rest)))
    ]
    saves = [pltpu.make_async_copy(src, dst, sem.at[3 + i]) for i, (src, dst) in enumerate(zip(refs[3:10], outs))]
    for load in loads:
        load.start()
    for i, ref in enumerate(lines):
        ref[...] = small[i : i + 1, :D].reshape(-1)
    cores = rest.shape[0]
    part = D // cores
    loads[0].wait()
    grad_t[...] = grad[...].T
    saves[0].start()
    loads[1].wait()
    span = 2 * D + 16
    for t in range(d_we.shape[1] // 128):
        lanes = slice(128 * t, 128 * t + 128)
        d_we[:, lanes] = ff[t * span : t * span + D, :]
        d_ws[:, lanes] = ff[t * span + D : t * span + 2 * D, :]
        d_dw[:, lanes] = ff[t * span + 2 * D : t * span + 2 * D + 9, :]
    saves[1].start()
    saves[2].start()
    for row, ref in ((9, d_be), (10, d_bd)):
        at = 2 * D + row
        parts = [ff[t * span + at : t * span + at + 1, :] for t in range(d_we.shape[1] // 128)]
        ref[...] = jnp.concatenate(parts, 1).reshape(-1)
    loads[2].wait()

    def tile(k):
        return jnp.concatenate([rest[h, k * part : k * part + part, :] for h in range(cores)], 0)

    for t in range(10):
        d_wr[:, 128 * t : 128 * t + 128] = tile(t)
    saves[3].start()
    for t in range(5):
        d_wkv[:, 128 * t : 128 * t + 128] = tile(10 + t)
    saves[4].start()
    mixed = jnp.concatenate([tile(17 + t) for t in range(3)], 1)
    d_wo[...] = jnp.concatenate([tile(15), tile(16), mixed[:, :64]], 1)
    d_wq[...] = mixed[:, 64:]
    saves[5].start()
    saves[6].start()
    for save in saves:
        save.wait()


def unpack(grad, ff, rest, small):
    cores = rest.shape[0]
    rows = grad.shape[0]
    chans = FF // cores
    vm, far = pl.BlockSpec(memory_space=pltpu.VMEM), pl.BlockSpec(memory_space=pl.ANY)
    large = [(D, rows), (D, chans), (D, chans), (D, 4 * D), (D, 2 * D), (D, D), (D, D)]
    shapes = large + [(9, chans), (chans,), (chans,)] + [(D,)] * 11
    held = [x.shape for x in (grad, ff, rest)] + large
    return pl.pallas_call(
        unpack_kernel,
        out_shape=tuple(jax.ShapeDtypeStruct(x, f32) for x in shapes),
        in_specs=[far] * 3 + [vm],
        out_specs=(far,) * 7 + (vm,) * 14,
        scratch_shapes=[pltpu.VMEM(x, f32) for x in held] + [pltpu.SemaphoreType.DMA((10,))],
        compiler_params=pltpu.CompilerParams(vmem_limit_bytes=60 * MIB),
        name="unpack",
    )(grad, ff, rest, small)


def body(
    pairs,
    cores,
    tokens,
    block_kind,
    first_gain,
    first_bias,
    query_weight,
    query_bias,
    reduce_weight,
    reduce_bias,
    reduce_gain,
    reduce_shift,
    keyval_weight,
    value_bias,
    output_weight,
    output_bias,
    second_gain,
    second_shift,
    expand_weight,
    expand_bias,
    depth_weight,
    depth_bias,
    shrink_weight,
    shrink_bias,
    cotangent,
):
    own_taps = jnp.concatenate(
        [depth_weight, expand_bias[None], depth_bias[None], jnp.zeros((5, expand_bias.shape[0]), f32)], 0
    )
    hidden = [lax.all_gather(x, "hidden", axis=0) for x in (expand_weight, shrink_weight.T, own_taps)]
    vecs = (
        first_gain,
        first_bias,
        query_bias,
        reduce_bias,
        reduce_gain,
        reduce_shift,
        value_bias,
        output_bias,
    )
    late = (second_gain, second_shift, shrink_bias)
    weights = (query_weight, reduce_weight.T, keyval_weight, output_weight)
    after, marks, *saved = attention_forward(block_kind, tokens.T, vecs, *weights)
    result_t, g_after, ff_pack, sums = feed_forward(block_kind, after, cotangent.T, late, hidden)
    grad, ff_sum, rest, small = attention_backward(
        pairs, cores, block_kind, g_after, marks, vecs, *weights, saved, sums, ff_pack.reshape(-1, 128)
    )
    outs = unpack(grad, ff_sum, rest, small)
    grad_t, d_we, d_ws, d_wr, d_wkv, d_wq, d_wo, d_dw, d_be, d_bd, *small = outs
    return (
        result_t.T,
        grad_t.T,
        small[0],
        small[1],
        d_wq,
        small[2],
        d_wr.T,
        small[3],
        small[4],
        small[5],
        d_wkv,
        small[6],
        d_wo,
        small[7],
        small[8],
        small[9],
        d_we,
        d_be,
        d_dw,
        d_bd,
        d_ws.T,
        small[10],
    )


def solution(mesh):
    both = P(("dp", "hidden"), None)
    cols = P(None, "hidden")
    chan = P("hidden")
    deep = P("hidden", None)
    whole = P()
    return jax.shard_map(
        partial(body, mesh.shape["dp"], mesh.shape["hidden"]),
        mesh=mesh,
        in_specs=(both,) + (whole,) * 15 + (cols, chan, cols, chan, deep, whole, both),
        out_specs=(both, both) + (whole,) * 14 + (cols, chan, cols, chan, deep, whole),
        check_vma=False,
    )
```

```python
from functools import partial

import jax
import jax.numpy as jnp
import numpy as np
from jax import lax
from jax.experimental import pallas as pl
from jax.experimental.pallas import tpu as pltpu
from jax.sharding import PartitionSpec as P

HEADS = 5
HEAD = 64
BLOCK = 196
GRID = 14
SMALL = 6
SMALL_IMGS = 5
KVB = 49
D = 320
FF = 1280
KPAD = 56
WIN = 208
ODD = 184
CHUNK = 256
CHUNKS = FF // CHUNK
SLAB = 224
DEEP = 1024
PAD = 16
MIB = 1024 * 1024

f32 = jnp.float32
bf16 = jnp.bfloat16
MESH = pl.DeviceIdType.MESH


def gather_table():
    out = np.zeros((2, 2, 4 * KPAD, WIN), np.float32)
    for kind in range(2):
        for parity in range(2):
            off = 12 * parity
            for a in range(2):
                for b in range(2):
                    for key in range(KVB):
                        if kind == 0:
                            i, j = divmod(key, GRID // 2)
                            spot = (2 * i + a) * GRID + 2 * j + b
                        else:
                            if key >= 45:
                                continue
                            image, rest = divmod(key, 9)
                            i, j = divmod(rest, 3)
                            spot = image * 36 + (2 * i + a) * SMALL + 2 * j + b
                        out[kind, parity, (2 * a + b) * KPAD + key, off + spot] = 1.0
    return out.reshape(4, 4 * KPAD, WIN)


def score_table():
    out = np.full((2, 2, WIN, 256), -1e30, np.float32)
    for kind in range(2):
        for parity in range(2):
            off = 12 * parity
            for row in range(WIN):
                local = row - off
                for key in range(KVB):
                    if kind == 0 or local < 0 or local >= BLOCK:
                        good = True
                    else:
                        good = key < 45 and key // 9 == min(local // 36, 4)
                    if good:
                        for head in range(HEADS):
                            out[kind, parity, row, head * KVB + key] = 0.0
    return out.reshape(4, WIN, 256)


def row_table():
    out = np.zeros((2, 2, WIN, 128), np.float32)
    for parity in range(2):
        off = 12 * parity
        for row in range(BLOCK):
            i, j = divmod(row, GRID)
            out[0, parity, off + row, :7] = (1, j > 0, j < 13, i > 0, 0, i < 13, 0)
            if row < 180:
                i, j = divmod(row % 36, SMALL)
                out[1, parity, off + row, :7] = (1, j > 0, j < 5, 0, i > 0, 0, i < 5)
    return out.reshape(4, WIN, 128)


def split(x):
    high = x.astype(bf16)
    return high, (x - high.astype(f32)).astype(bf16)


def pack_left(x):
    high = x.astype(bf16).astype(f32)
    low = x - high
    tail = jnp.concatenate([high[:, 256:], low[:, 256:]], 1).astype(bf16)
    high, low = high[:, :256].astype(bf16), low[:, :256].astype(bf16)
    return jnp.concatenate([high, low, high, tail, tail], 1)


def pack_short(x):
    high = x.astype(bf16).astype(f32)
    low = x - high
    tail = jnp.concatenate([high[:, 256:], low[:, 256:]], 1).astype(bf16)
    return jnp.concatenate([high[:, :256].astype(bf16), low[:, :256].astype(bf16), tail], 1)


def pack_lane(w):
    high = w.astype(bf16).astype(f32)
    low = w - high
    tail_high = jnp.concatenate([high[:, 256:], high[:, 256:]], 1).astype(bf16)
    tail_low = jnp.concatenate([low[:, 256:], low[:, 256:]], 1).astype(bf16)
    high, low = high[:, :256].astype(bf16), low[:, :256].astype(bf16)
    return jnp.concatenate([high, high, low, tail_high, tail_low], 1)


def pack_down(w):
    high, low = split(w)
    return jnp.concatenate(
        [high[:256], high[:256], low[:256], high[256:], high[256:], low[256:], low[256:]], 0
    )


def triple_left(x):
    high, low = split(x)
    return jnp.concatenate([high, low, high], 1)


def triple_down(w):
    high, low = split(w)
    return jnp.concatenate([high, high, low], 0)


def triple_lane(w):
    high, low = split(w)
    return jnp.concatenate([high, high, low], 1)


def mm(a, b):
    return jnp.dot(a, b, preferred_element_type=f32)


def mm_lane(a, b):
    return lax.dot_general(a, b, (((1,), (1,)), ((), ())), preferred_element_type=f32)


def mm_rows(a, b):
    left_high, left_low = split(a.T)
    high, low = split(b)
    return mm(left_high, high) + mm(left_low, high) + mm(left_high, low)


def norm_rows(x):
    center = jnp.sum(x, -1, keepdims=True) * (1.0 / D)
    centered = x - center
    spread = jnp.sum(centered * centered, -1, keepdims=True) * (1.0 / D)
    scale = lax.rsqrt(spread + 1e-06)
    return centered * scale, scale


def norm_back(h, n, scale):
    mean_h = jnp.sum(h, -1, keepdims=True) * (1.0 / D)
    mean_hn = jnp.sum(h * n, -1, keepdims=True) * (1.0 / D)
    return scale * (h - mean_h - n * mean_hn)


def fold(x):
    return jnp.sum(x.reshape(x.shape[0] // 8, 8, x.shape[1]), 0)


def window(block):
    return pl.multiple_of((block // 2) * (2 * BLOCK) + (block % 2) * ODD, 8)


def slab(w):
    return pl.ds(pl.multiple_of(w * SLAB, SLAB), SLAB)


def place_window(ref, block, value):
    start = window(block)

    @pl.when(block % 2 == 0)
    def _():
        ref[pl.ds(start, WIN), :] = value

    @pl.when(block % 2 == 1)
    def _():
        edge = ref[pl.ds(start + 8, 8), :]
        rows = lax.broadcasted_iota(jnp.int32, edge.shape, 0)
        ref[pl.ds(start + 8, 8), :] = jnp.where(rows < 4, edge, value[8:16])
        ref[pl.ds(start + 16, WIN - 16), :] = value[16:]


def head_block(rows_ref, block, out_ref):
    start = pl.multiple_of(block * KPAD, 8)
    for head in range(HEADS):
        tile = head // 2
        if tile < 2:
            value = rows_ref[pl.ds(start, KPAD), tile * 128 : tile * 128 + 128]
            lane = lax.broadcasted_iota(jnp.int32, value.shape, 1)
            value = jnp.where((lane >= 64) == (head % 2 == 1), value, 0.0)
        else:
            half = rows_ref[pl.ds(start, KPAD), 256:320]
            value = jnp.concatenate([half, half], 1)
        out_ref[tile, head * KVB : head * KVB + KVB, :] = value[:KVB]


def head_rows(ref):
    return jnp.concatenate([ref[0], ref[1], ref[2][:, :64]], 1)


def head_unblock(ref, value):
    ref[0] = value[:, :128]
    ref[1] = value[:, 128:256]
    ref[2] = jnp.concatenate([value[:, 256:], value[:, 256:]], 1)
    lane = lax.broadcasted_iota(jnp.int32, (KPAD, 128), 1)
    row = lax.broadcasted_iota(jnp.int32, (KPAD, 128), 0)
    tiles = []
    for tile in range(3):
        first = ref[tile, 2 * tile * KVB : 2 * tile * KVB + KPAD, :]
        if tile < 2:
            second = ref[tile, (2 * tile + 1) * KVB : (2 * tile + 1) * KVB + KPAD, :]
            first = jnp.where(lane < 64, first, second)
        tiles.append(jnp.where(row < KVB, first, 0.0))
    return jnp.concatenate([tiles[0], tiles[1], tiles[2][:, :64]], 1)


def head_lane(ref):
    parts = []
    for tile in range(3):
        high = ref[tile].astype(bf16)
        parts.append((high, (ref[tile] - high.astype(f32)).astype(bf16)))
    return jnp.concatenate(
        [parts[0][0], parts[1][0], parts[0][0], parts[1][0], parts[0][1], parts[1][1], parts[2][0], parts[2][1]], 1
    )


def head_of_lane(shape):
    lane = lax.broadcasted_iota(jnp.int32, shape, 1)
    return [lane < (head + 1) * KVB for head in range(HEADS - 1)]


def by_head(below, values):
    out = values[HEADS - 1]
    for head in range(HEADS - 2, -1, -1):
        out = jnp.where(below[head], values[head], out)
    return out


def per_head(below, x, empty, reduce):
    out = []
    for head in range(HEADS):
        here = x
        if head < HEADS - 1:
            here = jnp.where(below[head], here, empty)
        if head > 0:
            here = jnp.where(below[head - 1], empty, here)
        out.append(reduce(here, axis=1, keepdims=True))
    return by_head(below, [jnp.broadcast_to(v, x.shape) for v in out])


def line(ref):
    return ref[...].reshape(1, -1)


def own_first(blocks):
    return (lax.axis_index("dp") * lax.axis_size("hidden") + lax.axis_index("hidden")) * blocks


def attention_kernel(
    kinds,
    tokens_t,
    table,
    scores_mask,
    row_marks,
    first_gain,
    first_bias,
    query_bias,
    reduce_bias,
    reduce_gain,
    reduce_shift,
    value_bias,
    output_bias,
    wq,
    wr,
    wkv,
    wo,
    after,
    *refs,
):
    held, refs = refs[:9], refs[9:]
    marks, first_n, query, attended, probs, keys, values, red_n, patches = refs[:9]
    wq_s, wo_s, wk_s, wv_s, wr_s, tokens, normed, kb, vb, sem = refs[9:]
    saves = [pltpu.make_async_copy(src, dst, sem.at[i]) for i, (src, dst) in enumerate(zip(refs, held))]
    blocks = probs.shape[0]
    slabs = tokens.shape[0] // SLAB
    first = own_first(blocks)
    g1, b1, bq, br = line(first_gain), line(first_bias), line(query_bias), line(reduce_bias)
    gr, sr, bv, bo = line(reduce_gain), line(reduce_shift), line(value_bias), line(output_bias)
    wq_s[...] = pack_down(wq[...])
    wo_s[...] = pack_down(wo[...])
    wk_s[...] = pack_down(wkv[:, :D])
    wv_s[...] = pack_down(wkv[:, D:])
    for sub in range(4):
        wr_s[sub] = pack_lane(wr[:, sub * D : sub * D + D])
    kb[...] = jnp.zeros_like(kb)
    vb[...] = jnp.zeros_like(vb)
    tokens[...] = tokens_t[...].T

    @pl.loop(0, slabs)
    def _(w):
        n, scale = norm_rows(tokens[slab(w), :])
        first_n[slab(w), :] = jnp.concatenate([n, jnp.broadcast_to(scale, (SLAB, 64))], 1)
        n = n * g1 + b1
        normed[slab(w), :] = n
        query[slab(w), :] = mm(pack_left(n), wq_s[...]) + bq

    saves[1].start()
    saves[2].start()

    @pl.loop(0, blocks)
    def _(b):
        which = kinds[first + b] * 2 + b % 2
        place_window(marks, b, row_marks[which])
        part = normed[pl.ds(window(b), WIN), :]
        high, low = split(part)
        pick = table[which]
        got = mm(pick, high) + mm(pick, low)
        rows = pl.ds(pl.multiple_of(b * KPAD, 8), KPAD)
        for sub in range(4):
            patches[sub, rows, :] = got[sub * KPAD : sub * KPAD + KPAD]

    saves[0].start()
    saves[8].start()

    @pl.loop(0, blocks * KPAD // SLAB)
    def _(w):
        acc = br + mm_lane(pack_left(patches[0, slab(w), :]), wr_s[0])
        for sub in range(1, 4):
            acc = acc + mm_lane(pack_left(patches[sub, slab(w), :]), wr_s[sub])
        n, scale = norm_rows(acc)
        red_n[slab(w), :] = jnp.concatenate([n, jnp.broadcast_to(scale, (SLAB, 64))], 1)
        packed = pack_left(n * gr + sr)
        keys[slab(w), :] = mm(packed, wk_s[...])
        values[slab(w), :] = mm(packed, wv_s[...]) + bv

    for i in (5, 6, 7):
        saves[i].start()

    @pl.loop(0, blocks)
    def _(b):
        which = kinds[first + b] * 2 + b % 2
        head_block(keys, b, kb)
        head_block(values, b, vb)
        q = query[pl.ds(window(b), WIN), :]
        s = mm_lane(pack_left(q), head_lane(kb)) * (HEAD**-0.5) + scores_mask[which]
        below = head_of_lane(s.shape)
        e = jnp.exp(s - per_head(below, s, -3e38, jnp.max))
        p = e / per_head(below, e, 0.0, jnp.sum)
        probs[b] = p
        out = mm(triple_left(p), triple_down(head_rows(vb)))
        place_window(attended, b, out)

    saves[3].start()
    saves[4].start()

    @pl.loop(0, slabs)
    def _(w):
        branch = mm(pack_left(attended[slab(w), :]), wo_s[...]) + bo
        after[slab(w), :] = tokens[slab(w), :] + marks[slab(w), 0:1] * branch

    for save in saves:
        save.wait()


def attention_forward(kinds, tokens_t, vecs, wq, wr, wkv, wo):
    rows = tokens_t.shape[1]
    blocks = rows // BLOCK
    krows = blocks * KPAD
    vm = pl.BlockSpec(memory_space=pltpu.VMEM)

    def shape(*dims):
        return jax.ShapeDtypeStruct(dims, f32)

    saved = (
        shape(rows, 128),
        shape(rows, D + 64),
        shape(rows, D),
        shape(rows, D),
        shape(blocks, WIN, 256),
        shape(krows, D),
        shape(krows, D),
        shape(krows, D + 64),
        shape(4, krows, D),
    )
    return pl.pallas_call(
        attention_kernel,
        out_shape=(shape(rows, D),) + saved,
        in_specs=[pl.BlockSpec(memory_space=pltpu.SMEM)] + [vm] * 16,
        out_specs=(vm,) + (pl.BlockSpec(memory_space=pl.ANY),) * 9,
        scratch_shapes=[pltpu.VMEM(x.shape, f32) for x in saved]
        + [
            pltpu.VMEM((1024, D), bf16),
            pltpu.VMEM((1024, D), bf16),
            pltpu.VMEM((1024, D), bf16),
            pltpu.VMEM((1024, D), bf16),
            pltpu.VMEM((4, D, 1024), bf16),
            pltpu.VMEM((rows, D), f32),
            pltpu.VMEM((rows, D), f32),
            pltpu.VMEM((3, 256, 128), f32),
            pltpu.VMEM((3, 256, 128), f32),
            pltpu.SemaphoreType.DMA((9,)),
        ],
        compiler_params=pltpu.CompilerParams(vmem_limit_bytes=60 * MIB),
        name="attention",
    )(
        kinds,
        tokens_t,
        jnp.asarray(gather_table(), bf16),
        jnp.asarray(score_table()),
        jnp.asarray(row_table()),
        *vecs,
        wq,
        wr,
        wkv,
        wo,
    )


ERF_P = 0.3275911
ERF = (0.254829592, -0.284496736, 1.421413741, -1.453152027, 1.061405429)


def gelu_pair(x):
    size = jnp.abs(x)
    d = 1.0 + (ERF_P * 0.7071067811865476) * size
    t = pl.reciprocal(d, approx=True)
    t = t * (2.0 - d * t)
    e = jnp.exp(-0.5 * (x * x))
    poly = t * (ERF[0] + t * (ERF[1] + t * (ERF[2] + t * (ERF[3] + t * ERF[4]))))
    tail = 0.5 * (poly * e)
    phi = jnp.where(x < 0.0, tail, 1.0 - tail)
    return x * phi, phi + x * (0.3989422804014327 * e)


def has_left(r):
    return r % GRID > 0, r < 180 and r % SMALL > 0


def has_right(r):
    return r % GRID < GRID - 1, r < 180 and r % SMALL < SMALL - 1


def has_up(r):
    return r >= GRID, r < 180 and r % 36 >= SMALL


def has_down(r):
    return r < BLOCK - GRID, r < 180 and r % 36 < 30


def total_of(values):
    values = [v for v in values if v is not None]
    out = values[0]
    for v in values[1:]:
        out = out + v
    return out


def forward_kernel(
    kinds,
    after,
    cot_t,
    second_gain,
    second_shift,
    shrink_bias,
    own_we,
    own_ws,
    own_taps,
    result_t,
    g_after,
    pack,
    sums,
    we_s,
    we_l,
    ws_s,
    ws_l,
    result,
    g_second,
    by_block,
    by_place,
    taps,
    second,
    branch,
    second_t,
    branch_t,
    xs0,
    xs1,
    nx1,
    ga0,
    ga1,
    ng1,
    y0,
    yu,
    yd,
    act,
    gx,
    held_act,
    held_gx,
    dwe,
    dws,
    sem,
):
    rows = after.shape[0]
    pieces = rows // SLAB
    per = FF // 128 // own_we.shape[0]
    g2, s2, bs = line(second_gain), line(second_shift), line(shrink_bias)
    first = own_first(8)
    block = lax.broadcasted_iota(jnp.int32, (8, 128), 0)
    kind = jnp.zeros((8, 128), jnp.int32)
    for i in range(8):
        kind = jnp.where(block == i, kinds[first + i], kind)
    zero_kind = kind == 0
    k0 = jnp.where(zero_kind, 1.0, 0.0)
    k1 = 1.0 - k0

    loads = []
    for tile in range(FF // 128):
        lanes = pl.ds((tile % per) * 128, 128)
        for i, (source, low, size) in enumerate(((own_we, 0, D), (own_ws, D, D), (own_taps, 2 * D, 16))):
            loads.append(
                pltpu.make_async_copy(
                    source.at[tile // per, :, lanes], pack.at[tile, pl.ds(low, size)], sem.at[3 * tile + i]
                )
            )
    for load in loads:
        load.start()

    held_act[...] = jnp.zeros_like(held_act)
    held_gx[...] = jnp.zeros_like(held_gx)
    sums[...] = jnp.zeros_like(sums)

    def tiles_of(x):
        return x[:, :128], x[:, 128:256], jnp.concatenate([x[:, 256:], x[:, 256:]], 1)

    def to_places(out):
        for t in range(3):
            for i in range(8):
                by_place[t, pl.ds(i, BLOCK, stride=8), :] = by_block[t, i * BLOCK : (i + 1) * BLOCK, :]

        @pl.loop(0, rows // SLAB)
        def _(w):
            out[slab(w), :] = joined(by_place, slab(w))

    def to_blocks(source):
        @pl.loop(0, rows // SLAB)
        def _(w):
            for t, value in enumerate(tiles_of(source[slab(w), :])):
                by_place[t, slab(w), :] = value

        for t in range(3):
            for i in range(8):
                by_block[t, i * BLOCK : (i + 1) * BLOCK, :] = by_place[t, pl.ds(i, BLOCK, stride=8), :]

    def joined(ref, at):
        return jnp.concatenate([ref[0, at, :], ref[1, at, :], ref[2, at, :][:, :64]], 1)

    for t in range(3):
        low, high = 128 * t, min(128 * t + 128, D)
        value = cot_t[low:high, :].T
        by_block[t, 0:rows, :] = value if high - low == 128 else jnp.concatenate([value, value], 1)
    to_places(result)

    @pl.loop(0, rows // SLAB)
    def _(w):
        for t, value in enumerate(tiles_of(after[slab(w), :])):
            by_block[t, slab(w), :] = value

    to_places(g_second)

    g_after[...] = result[...]
    dead = 180 * 8
    result[dead:, :] = (result[dead:, :].reshape(BLOCK - 180, 8, D) * k0[:, :1]).reshape(rows - dead, D)

    @pl.loop(0, rows // SLAB)
    def _(w):
        a = g_second[slab(w), :]
        for t, value in enumerate(tiles_of(a)):
            by_block[t, slab(w), :] = value
        n, _ = norm_rows(a)
        value = n * g2 + s2
        g_second[slab(w), :] = value
        second[slab(w), :] = pack_short(value)
        grad = result[slab(w), :]
        sums[2] += fold(grad)
        branch[slab(w), :] = pack_short(grad)

    for source, turned in ((g_second, second_t), (result, branch_t)):
        high, low = split(source[...].T)
        turned[...] = jnp.concatenate([high, low, high], 1)
    result[...] = jnp.zeros_like(result)
    g_second[...] = jnp.zeros_like(g_second)

    for load in loads:
        load.wait()
    for c in range(CHUNKS):
        for which, (down, lane) in enumerate(((we_s, we_l), (ws_s, ws_l))):
            value = jnp.concatenate([pack[2 * c + t, which * D : which * D + D, :] for t in range(2)], 1)
            high, low = split(value)
            down[c] = jnp.concatenate([high, low], 0)
            lane[c] = jnp.concatenate([high, low], 1)
        for t in range(2):
            for k in range(11):
                taps[c, t, k] = jnp.broadcast_to(pack[2 * c + t, 2 * D + k : 2 * D + k + 1, :], (8, 128))

    def own(h):
        return slice(h * SLAB, (h + 1) * SLAB)

    def left(ref, h):
        x = ref[own(h), :]
        return jnp.concatenate([x[:, :512], x[:, :256], x[:, 512:], x[:, 512:]], 1)

    def deep(ref, c):
        x = ref[c]
        return jnp.concatenate(
            [x[:256], x[:256], x[D : D + 256], x[256:D], x[256:D], x[D + 256 :], x[D + 256 :]], 0
        )

    def expand_task(c, h, outs):
        e = mm(left(second, h), deep(we_s, c))
        for t in range(2):
            outs[t][own(h), :] = e[:, 128 * t : 128 * t + 128] + taps[c, t, 9][0:1]

    def active_grad_task(c, h, outs):
        g = mm(left(branch, h), deep(ws_s, c))
        for t in range(2):
            outs[t][own(h), :] = g[:, 128 * t : 128 * t + 128]

    def out_task(c, h, source, lane, out):
        x = source[own(h), :]
        weight = lane[c]
        out[own(h), :] += mm_lane(
            jnp.concatenate([x, x[:, :256]], 1), jnp.concatenate([weight[:, :256], weight], 1)
        )

    def weight_task(c, source, turned, row, total, k):
        span = slice(k * DEEP, min((k + 1) * DEEP, 3 * rows))
        parts = []
        for i, low in enumerate((0, 0, CHUNK)):
            start, stop = max(span.start, i * rows) - i * rows, min(span.stop, (i + 1) * rows) - i * rows
            if start < stop:
                parts.append(source[start:stop, low : low + CHUNK])
        value = mm(turned[:, span], jnp.concatenate(parts, 0) if len(parts) > 1 else parts[0])
        if k > 0:
            value = value + total[...]
        if span.stop < 3 * rows:
            total[...] = value
            return
        for t in range(2):
            pack[2 * c + t, row : row + D, :] = value[:, 128 * t : 128 * t + 128]

    def early_tasks(c, x_outs, g_outs):
        out = []
        for h in range(pieces):
            out += [partial(expand_task, c, h, x_outs), partial(active_grad_task, c, h, g_outs)]
        return out

    def late_tasks(c):
        out = []
        for h in range(pieces):
            out += [
                partial(out_task, c, h, held_act, ws_l, result),
                partial(out_task, c, h, held_gx, we_l, g_second),
            ]
        return out

    def weight_tasks(c):
        count = -(-3 * rows // DEEP)
        first_half = [partial(weight_task, c, held_act, branch_t, D, dws, k) for k in range(count)]
        return first_half, [partial(weight_task, c, held_gx, second_t, 0, dwe, k) for k in range(count)]

    def woven(a, b):
        out = list(a)
        for i, task in enumerate(b):
            out.insert(round((i + 1) * len(a) / (len(b) + 1)) + i, task)
        return out

    def at(r):
        return slice(8 * r, 8 * r + 8)

    def gated(value, ok):
        if ok[0] and ok[1]:
            return value
        if ok[0]:
            return value * k0
        return value * k1 if ok[1] else None

    def picked(ref, r, ok, sign):
        if ok[0] and ok[1]:
            return jnp.where(zero_kind, ref[at(r + sign * GRID), :], ref[at(r + sign * SMALL), :])
        if ok[0]:
            return ref[at(r + sign * GRID), :] * k0
        return ref[at(r + sign * SMALL), :] * k1 if ok[1] else None

    def put_split(ref, t, r, pair):
        high, low = split(jnp.concatenate(pair, 0))
        here = slice(8 * r, 8 * r + 16)
        ref[here, 128 * t : 128 * t + 128] = high
        ref[here, 256 + 128 * t : 384 + 128 * t] = low

    def item(c, t, x, g, tasks):
        tap = [taps[c, t, k] for k in range(11)]
        totals = [jnp.zeros((8, 128), f32)] * 11

        def columns(r, near):
            return [
                gated(near(r - 1), has_left(r)) if r > 0 else None,
                near(r),
                gated(near(r + 1), has_right(r)) if r + 1 < BLOCK else None,
            ]

        def mix(values, ks, more=()):
            return total_of([None if v is None else v * tap[k] for v, k in zip(values, ks)] + list(more))

        def loader():
            kept = {}

            def near(r):
                if r not in kept:
                    kept[r] = x[at(r), :]
                return kept[r]

            return near

        ahead, behind = loader(), loader()
        moved_back = {}
        every = {}
        count = (BLOCK + 30) // 2
        slots = {round((i + 0.5) * count / len(tasks)): task for i, task in enumerate(tasks)}
        for step in range(count):
            for r in (2 * step, 2 * step + 1):
                if r < BLOCK:
                    cols = columns(r, ahead)
                    yu[at(r), :] = mix(cols, (0, 1, 2))
                    y0[at(r), :] = mix(cols, (3, 4, 5), (tap[10],))
                    yd[at(r), :] = mix(cols, (6, 7, 8))
            r = 2 * step - 14
            if 0 <= r < BLOCK:
                conv = [
                    total_of([y0[at(s), :], picked(yu, s, has_up(s), -1), picked(yd, s, has_down(s), 1)])
                    for s in (r, r + 1)
                ]
                active, slope = gelu_pair(jnp.concatenate(conv, 0))
                put_split(act, t, r, [active[:8], active[8:]])
                here = slice(8 * r, 8 * r + 16)
                g[here, :] = g[here, :] * slope
            for r in (2 * step - 28, 2 * step - 27):
                if 0 <= r < BLOCK:
                    same = g[at(r), :]
                    moved = [picked(g, r, has_down(r), 1), same, picked(g, r, has_up(r), -1)]
                    cols = columns(r, behind)
                    totals[10] = totals[10] + same
                    for p in range(3):
                        for q in range(3):
                            if moved[p] is not None and cols[q] is not None:
                                totals[3 * p + q] = totals[3 * p + q] + moved[p] * cols[q]
                    moved_back[r] = [mix(moved, ks) for ks in ((0, 3, 6), (1, 4, 7), (2, 5, 8))]
            r = 2 * step - 30
            if 0 <= r < BLOCK:
                pair = []
                for s in (r, r + 1):
                    value = total_of(
                        [
                            moved_back[s][1],
                            gated(moved_back[s - 1][2], has_left(s)) if s > 0 else None,
                            gated(moved_back[s + 1][0], has_right(s)) if s + 1 < BLOCK else None,
                        ]
                    )
                    totals[9] = totals[9] + value
                    pair.append(value)
                put_split(gx, t, r, pair)
            if step in slots:
                slots[step]()
        for k in range(11):
            pack[2 * c + t, 2 * D + k : 2 * D + k + 1, :] = jnp.sum(totals[k], 0, keepdims=True)

    for task in early_tasks(0, (xs0, xs1), (ga0, ga1)):
        task()

    @pl.loop(0, CHUNKS)
    def _(c):
        before = jnp.maximum(c - 1, 0)
        item(c, 0, xs0, ga0, woven(late_tasks(before), weight_tasks(before)[0]))
        later = jnp.minimum(c + 1, CHUNKS - 1)
        item(c, 1, xs1, ga1, woven(early_tasks(later, (xs0, nx1), (ga0, ng1)), weight_tasks(before)[1]))
        xs1[...] = nx1[...]
        ga1[...] = ng1[...]
        held_act[...] = act[...]
        held_gx[...] = gx[...]

    for task in late_tasks(CHUNKS - 1) + sum(weight_tasks(CHUNKS - 1), []):
        task()
    for c in range(CHUNKS):
        for t in range(2):
            pack[2 * c + t, 2 * D + 11 : 2 * D + 16, :] = jnp.zeros((5, 128), f32)

    result[dead:, :] = ((result[dead:, :] + bs).reshape(BLOCK - 180, 8, D) * k0[:, :1]).reshape(rows - dead, D) - bs

    @pl.loop(0, rows // SLAB)
    def _(w):
        a = joined(by_block, slab(w))
        result[slab(w), :] = a + (result[slab(w), :] + bs)
        n, scale = norm_rows(a)
        g = g_second[slab(w), :]
        sums[0] += fold(g * n)
        sums[1] += fold(g)
        g_second[slab(w), :] = g_after[slab(w), :] + norm_back(g * g2, n, scale)

    to_blocks(result)
    for t in range(3):
        low, high = 128 * t, min(128 * t + 128, D)
        result_t[low:high, :] = by_block[t, 0:rows, :].T[: high - low]
    to_blocks(g_second)

    @pl.loop(0, rows // SLAB)
    def _(w):
        g_after[slab(w), :] = joined(by_block, slab(w))


def feed_forward(kinds, after, cot_t, vecs, weights):
    rows = after.shape[0]
    vm = pl.BlockSpec(memory_space=pltpu.VMEM)
    tile = pltpu.VMEM((rows, 128), f32)
    half = pltpu.VMEM((rows, 2 * CHUNK), bf16)
    return pl.pallas_call(
        forward_kernel,
        out_shape=(
            jax.ShapeDtypeStruct((D, rows), f32),
            jax.ShapeDtypeStruct((rows, D), f32),
            jax.ShapeDtypeStruct((2 * CHUNKS, 2 * D + 16, 128), f32),
            jax.ShapeDtypeStruct((3, 8, D), f32),
        ),
        in_specs=[pl.BlockSpec(memory_space=pltpu.SMEM)] + [vm] * 5 + [pl.BlockSpec(memory_space=pl.ANY)] * 3,
        out_specs=(vm,) * 4,
        scratch_shapes=[
            pltpu.VMEM((CHUNKS, 2 * D, CHUNK), bf16),
            pltpu.VMEM((CHUNKS, D, 2 * CHUNK), bf16),
            pltpu.VMEM((CHUNKS, 2 * D, CHUNK), bf16),
            pltpu.VMEM((CHUNKS, D, 2 * CHUNK), bf16),
            pltpu.VMEM((rows, D), f32),
            pltpu.VMEM((rows, D), f32),
            pltpu.VMEM((3, rows + 64, 128), f32),
            pltpu.VMEM((3, rows + 64, 128), f32),
            pltpu.VMEM((CHUNKS, 2, 11, 8, 128), f32),
            pltpu.VMEM((rows, 640), bf16),
            pltpu.VMEM((rows, 640), bf16),
            pltpu.VMEM((D, 3 * rows), bf16),
            pltpu.VMEM((D, 3 * rows), bf16),
        ]
        + [tile] * 9
        + [half] * 4
        + [pltpu.VMEM((D, CHUNK), f32)] * 2
        + [pltpu.SemaphoreType.DMA((6 * CHUNKS,))],
        compiler_params=pltpu.CompilerParams(vmem_limit_bytes=63 * MIB),
        name="feed_forward",
    )(kinds, after, cot_t, *vecs, *weights)


class Wires:
    def __init__(self, pairs, cores, send, recv):
        self.bits = pairs.bit_length() - 1
        self.cores = cores
        self.me, self.core = lax.axis_index("dp"), lax.axis_index("hidden")
        self.other = cores - 1 - self.core
        self.send, self.recv, self.used = send, recv, 0

    def groups(self):
        rest = list(range(2, self.bits))
        return [(k,) for k in range(min(2, self.bits))] + [tuple(rest[i : i + 2]) for i in range(0, len(rest), 2)]

    def bit(self, k):
        return (self.me // (1 << k)) % 2

    def peer(self, group, j):
        flips = [(1 - 2 * self.bit(k)) * (1 << k) for i, k in enumerate(group) if (j >> i) & 1]
        return (sum(flips, self.me), self.core)

    def place(self, group, j):
        bits = [(1 - self.bit(k) if (j >> i) & 1 else self.bit(k)) * (1 << i) for i, k in enumerate(group)]
        return sum(bits[1:], bits[0])

    def greet(self):
        peers = [self.peer(group, j) for group in self.groups() for j in range(1, 1 << len(group))]
        if self.cores > 1:
            peers.append((self.me, self.other))
        if not peers:
            return
        barrier = pltpu.get_barrier_semaphore()
        for target in peers:
            pl.semaphore_signal(barrier, inc=1, device_id=target, device_id_type=MESH)
        pl.semaphore_wait(barrier, len(peers))

    def copy(self, src, dst, target):
        slot = self.used
        self.used += 1
        return pltpu.make_async_remote_copy(
            src_ref=src,
            dst_ref=dst,
            send_sem=self.send.at[slot],
            recv_sem=self.recv.at[slot],
            device_id=target,
            device_id_type=MESH,
        )

    def local(self, src, dst):
        slot = self.used
        self.used += 1
        return pltpu.make_async_copy(src, dst, self.send.at[slot])

    def sibling(self, src, dst):
        return self.copy(src, dst, (self.me, self.other))


def rows_of(start, size):
    return pl.ds(pl.multiple_of(start, 8), size)


class Chain:
    def __init__(self, wires, acc, near, got, full, base, rows, order, opening, closing):
        self.stages, self.costs = [], []
        whole = pl.ds(base, rows)
        scale = 512 * wires.cores / LINK

        def meet():
            if near is not None:
                acc[whole, :] = acc[whole, :] + near[whole, :]

        start, size, spot = base + 0 * wires.me, rows, base
        pending, action = opening, meet
        self.stages.append(([], None, opening))
        self.costs.append(("core", rows * 512 / CORE_LINK))
        held = []
        for group in order:
            many = 1 << len(group)
            size //= many
            keep = start + wires.place(group, 0) * size
            copies, lands = [], []
            for j in range(1, many):
                land = pl.ds(spot, size)
                spot += size
                give = start + wires.place(group, j) * size
                copies.append(wires.copy(acc.at[rows_of(give, size)], got.at[land], wires.peer(group, j)))
                lands.append(land)
            self.stages.append((pending, action, copies))
            self.costs.append((group, scale * size * (1 if many == 2 else many)))

            def add(keep=keep, lands=lands, size=size):
                value = acc[rows_of(keep, size), :]
                for land in lands:
                    value = value + got[land, :]
                acc[rows_of(keep, size), :] = value

            pending, action = copies, add
            held.append((group, start))
            start = keep
        last, last_start, last_size = action, start, size

        def settle():
            last()
            full[rows_of(last_start, last_size), :] = acc[rows_of(last_start, last_size), :]

        action = settle
        for group, before in reversed(held):
            mine = rows_of(start, size)
            many = 1 << len(group)
            copies = [wires.copy(full.at[mine], full.at[mine], wires.peer(group, j)) for j in range(1, many)]
            self.stages.append((pending, action, copies))
            self.costs.append((group, scale * size * (1 if many == 2 else many)))
            pending, action = copies, None
            start, size = before, size * many
        if closing:
            self.stages.append((pending, action, closing))
            self.costs.append(("core", rows * 512 / CORE_LINK))
            pending, action = closing, None
        self.stages.append((pending, action, []))
        self.costs.append((None, 0.0))

    def run(self, stage):
        waits, action, starts = self.stages[stage]
        for c in waits:
            c.wait()
        if action is not None:
            action()
        for c in starts:
            c.start()


class Exchange(Chain):
    def __init__(self, wires, sums, got):
        partners = [((k,), wires.peer((k,), 1)) for k in range(wires.bits)]
        if wires.cores > 1:
            partners.insert(0, ("core", (wires.me, wires.other)))
        self.stages, self.costs = [], []
        pending, action = [], None
        for i, (name, target) in enumerate(partners):
            c = wires.copy(sums.at[i], got.at[i], target)
            self.stages.append((pending, action, [c]))
            self.costs.append((name, 0.5))

            def add(i=i):
                sums[i + 1] = sums[i] + got[i]

            pending, action = [c], add
        self.stages.append((pending, action, []))
        self.costs.append((None, 0.0))
        self.last = len(partners)


LINK = 100e3
CORE_LINK = 400e3
DELAY = 2.5
STEP_WORK = 0.1


class Plan:
    def __init__(self):
        self.now, self.free, self.going = 0.0, {}, []

    def add(self, chains):
        self.going += [[self.now, c, 0] for c in chains]

    def after(self, us):
        self.now += us
        due = []
        while True:
            ready = [g for g in self.going if g[0] <= self.now]
            if not ready:
                return due
            due.append(self.take(min(ready, key=lambda g: g[0])))

    def take(self, entry):
        done, chain, stage = entry
        self.now = max(self.now, done) + STEP_WORK
        link, us = chain.costs[stage]
        self.free[link] = max(self.free.get(link, 0.0), self.now) + us
        if stage + 1 == len(chain.stages):
            self.going.remove(entry)
        else:
            entry[0], entry[2] = self.free[link] + DELAY, stage + 1
        return chain, stage

    def rest(self):
        due = []
        while self.going:
            due.append(self.take(min(self.going, key=lambda g: g[0])))
        return due


def run_steps(steps):
    for chain, stage in steps:
        chain.run(stage)


def axis_orders(groups):
    return groups, groups[1::-1] + groups[2:], groups[2:] + groups[:2]


def cut(total, unit, parts):
    units = total // unit
    marks = sorted({0, units} | {round(units * x) for x in parts})
    return [(a * unit, b * unit) for a, b in zip(marks, marks[1:])]


def round_up(x, unit):
    return -(-x // unit) * unit


def sum_rows(pairs, cores):
    unit = 8 * pairs
    ff = round_up(2 * CHUNKS // cores * (2 * D + 16), unit)
    rest = round_up(20 * (D // cores), unit)
    return ff, rest


def backward_kernel(
    pairs,
    cores,
    kinds,
    first_n_from,
    g_after,
    marks,
    table,
    first_gain,
    first_bias,
    reduce_gain,
    reduce_shift,
    wq,
    wr,
    wkv,
    wo,
    query_from,
    attended_from,
    probs_from,
    keys_from,
    values_from,
    red_n_from,
    patches_from,
    sums,
    ff_pack,
    grad,
    ff_full,
    full,
    small,
    first_n,
    query,
    attended,
    probs,
    keys,
    values,
    red_n,
    patches,
    wq_l,
    wo_l,
    wk_l,
    wv_l,
    wr_l,
    g_att,
    g_query,
    g_keys,
    g_values,
    g_patch,
    g_scores,
    kb,
    vb,
    tmp,
    acc,
    ff_acc,
    ff_near,
    ff_got,
    big,
    near,
    got,
    small_sum,
    small_got,
    send,
    recv,
):
    blocks = probs.shape[0]
    rows = g_after.shape[0]
    slabs = rows // SLAB
    krows = blocks * KPAD
    first = own_first(blocks)
    part = D // cores
    g1, b1, gr, sr = line(first_gain), line(first_bias), line(reduce_gain), line(reduce_shift)

    wires = Wires(pairs, cores, send, recv)
    core = wires.core
    orders = axis_orders(wires.groups())
    unit = 8 * pairs
    ff_real = ff_pack.shape[0] // cores
    ff_total, total = ff_acc.shape[0], big.shape[1]
    if ff_total > ff_real:
        ff_acc[ff_real:, :] = jnp.zeros((ff_total - ff_real, 128), f32)
        ff_near[ff_real:, :] = jnp.zeros((ff_total - ff_real, 128), f32)
    if total > 20 * part:
        for h in range(cores):
            big[h, 20 * part :, :] = jnp.zeros((total - 20 * part, 128), f32)
    wires.greet()
    ff_chains = []
    for i, (low, high) in enumerate(cut(ff_total, unit, (11 / 26, 22 / 26))):
        size = min(high, ff_real) - low
        here = pl.ds(low, size)
        opening = [wires.local(ff_pack.at[rows_of(core * ff_real + low, size)], ff_acc.at[here])]
        if cores > 1:
            opening.append(wires.sibling(ff_pack.at[rows_of(wires.other * ff_real + low, size)], ff_near.at[here]))
        ff_chains.append(
            Chain(
                wires,
                ff_acc,
                ff_near if cores > 1 else None,
                ff_got,
                ff_full,
                low,
                high - low,
                orders[i],
                opening,
                [],
            )
        )
    bounds = [10 * part, 15 * part, 17 * part]
    chains = []
    cuts = cut(total, unit, (6 / 25, 12 / 25, 15 / 25, 18 / 25, 19 / 25, 22 / 25))
    for i, (low, high) in enumerate(cuts):
        here = pl.ds(low, high - low)
        opening, closing = [], []
        if cores > 1:
            opening = [wires.sibling(big.at[wires.other, here], near.at[here])]
            closing = [wires.sibling(full.at[core, here], full.at[core, here])]
        chain = Chain(
            wires,
            big.at[core],
            near if cores > 1 else None,
            got,
            full.at[core],
            low,
            high - low,
            orders[(0, 1, 0, 1, 2, 0, 1)[i]],
            opening,
            closing,
        )
        chain.ready = sum(high > x for x in bounds)
        chains.append(chain)
    fetch = {
        name: wires.local(src, dst)
        for name, src, dst in (
            ("values", values_from, values),
            ("probs", probs_from, probs),
            ("query", query_from, query),
            ("red_n", red_n_from, red_n),
            ("patches", patches_from, patches),
            ("attended", attended_from, attended),
            ("keys", keys_from, keys),
            ("first_n", first_n_from, first_n),
        )
    }
    plan = Plan()
    plan.add(ff_chains)

    def tick(us, level=None):
        run_steps(plan.after(us))
        if level is not None:
            plan.add([c for c in chains if c.ready == level])
            run_steps(plan.after(0.0))

    def ticks(count, us):
        return [plan.after(us) for _ in range(count)]

    def run_at(index, planned):
        for i, steps in enumerate(planned):
            if steps:
                pl.when(index == i)(partial(run_steps, steps))

    def store(tile, value):
        for t in range(value.shape[1] // 128):
            for h in range(cores):
                big[h, (tile + t) * part : (tile + t + 1) * part, :] = value[
                    h * part : (h + 1) * part, 128 * t : 128 * t + 128
                ]

    tick(0.0)
    for c in fetch.values():
        c.start()
    wo_l[...] = pack_lane(wo[...])
    wk_l[...] = pack_lane(wkv[:, :D])
    wv_l[...] = pack_lane(wkv[:, D:])
    kb[...] = jnp.zeros_like(kb)
    vb[...] = jnp.zeros_like(vb)
    acc[...] = jnp.zeros_like(acc)
    tick(2.0)
    planned_0 = ticks(slabs, 0.6)

    @pl.loop(0, slabs)
    def _(w):
        g = marks[slab(w), 0:1] * g_after[slab(w), :]
        grad[slab(w), :] = g
        acc[0] += fold(g)
        g_att[slab(w), :] = mm_lane(pack_left(g), wo_l[...])
        run_at(w, planned_0)

    planned_1 = ticks(blocks, 1.8)
    for name in ("values", "probs", "query"):
        fetch[name].wait()

    @pl.loop(0, blocks)
    def _(b):
        head_block(values, b, vb)
        here = pl.ds(window(b), WIN)
        first_row = 12 * (b % 2)
        row = lax.broadcasted_iota(jnp.int32, (WIN, D), 0)
        inside = (row >= first_row) & (row < first_row + BLOCK)
        ga = jnp.where(inside, g_att[here, :], 0.0)
        p = probs[b]
        gp = mm_lane(pack_left(ga), head_lane(vb))
        below = head_of_lane(p.shape)
        gs = p * (gp - per_head(below, gp * p, 0.0, jnp.sum)) * (HEAD**-0.5)
        g_scores[b] = gs
        here_k = pl.ds(pl.multiple_of(b * KPAD, 8), KPAD)
        g_values[here_k, :] = head_unblock(tmp, mm_rows(p, ga))
        g_keys[here_k, :] = head_unblock(tmp, mm_rows(gs, query[here, :]))
        run_at(b, planned_1)

    fetch["red_n"].wait()
    fetch["patches"].wait()


    @pl.loop(0, krows // SLAB)
    def _(w):
        gk, gv = g_keys[slab(w), :], g_values[slab(w), :]
        acc[1] += fold(gv)
        g = mm_lane(pack_left(gk), wk_l[...]) + mm_lane(pack_left(gv), wv_l[...])
        n = red_n[slab(w), :D]
        acc[2] += fold(g * n)
        acc[3] += fold(g)
        g = norm_back(g * gr, n, red_n[slab(w), D : D + 1])
        acc[4] += fold(g)
        g_query[slab(w), :] = g

    tick(2.0)
    g_red = g_query[0:krows, :]
    for pair in range(2):
        d_wr = jnp.concatenate([mm_rows(g_red, patches[2 * pair]), mm_rows(g_red, patches[2 * pair + 1])], 1)
        store(5 * pair, d_wr)
        tick(2.0, 0 if pair else None)
    reduced = red_n[:, :D] * gr + sr
    d_wk = mm_rows(reduced, g_keys[...])
    d_wv = mm_rows(reduced, g_values[...])
    store(10, jnp.concatenate([d_wk, d_wv], 1))
    tick(2.5, 1)
    fetch["attended"].wait()
    d_wo = mm_rows(attended[...], grad[...])
    store(15, d_wo[:, :256])
    tick(3.5, 2)
    for sub in range(4):
        wr_l[sub] = pack_down(wr[:, sub * D : sub * D + D])

    @pl.loop(0, krows // SLAB)
    def _(w):
        packed = pack_left(g_query[slab(w), :])
        for sub in range(4):
            g_patch[sub, slab(w), :] = mm(packed, wr_l[sub])

    tick(2.0)
    planned_2 = ticks(blocks, 0.6)
    fetch["keys"].wait()
    fetch["first_n"].wait()

    @pl.loop(0, blocks)
    def _(b):
        head_block(keys, b, kb)
        place_window(g_query, b, mm(triple_left(g_scores[b]), triple_down(head_rows(kb))))
        run_at(b, planned_2)

    wq_l[...] = pack_lane(wq[...])

    @pl.loop(0, slabs)
    def _(w):
        acc[5] += fold(g_query[slab(w), :])
        grad[slab(w), :] = first_n[slab(w), :D] * g1 + b1

    d_wq = mm_rows(grad[...], g_query[...])
    store(17, jnp.concatenate([d_wo[:, 256:], d_wq], 1))
    tick(4.0, 3)
    planned_3 = ticks(slabs, 0.45)

    @pl.loop(0, slabs)
    def _(w):
        g_att[slab(w), :] = mm_lane(pack_left(g_query[slab(w), :]), wq_l[...])
        run_at(w, planned_3)

    planned_4 = ticks(blocks, 0.3)

    @pl.loop(0, blocks)
    def _(b):
        which = kinds[first + b] * 2 + b % 2
        here_k = pl.ds(pl.multiple_of(b * KPAD, 8), KPAD)
        high, low = split(jnp.concatenate([g_patch[sub, here_k, :] for sub in range(4)], 0))
        pick = table[which]
        dims = (((0,), (0,)), ((), ()))
        moved = lax.dot_general(pick, high, dims, preferred_element_type=f32)
        moved = moved + lax.dot_general(pick, low, dims, preferred_element_type=f32)
        g_att[pl.ds(window(b), WIN), :] += moved
        run_at(b, planned_4)

    planned_5 = ticks(slabs, 0.3)

    @pl.loop(0, slabs)
    def _(w):
        n, scale = first_n[slab(w), :D], first_n[slab(w), D : D + 1]
        g = g_att[slab(w), :]
        acc[6] += fold(g * n)
        acc[7] += fold(g)
        grad[slab(w), :] = g_after[slab(w), :] + norm_back(g * g1, n, scale)
        run_at(w, planned_5)

    order = (acc[6], acc[7], acc[5], acc[4], acc[2], acc[3], acc[1], acc[0], sums[0], sums[1], sums[2])
    value = jnp.concatenate([jnp.sum(x, 0, keepdims=True) for x in order] + [jnp.zeros((5, D), f32)], 0)
    value = jnp.concatenate([value, value[:, 256:]], 1)
    for t in range(3):
        small_sum[0, 16 * t : 16 * t + 16, :] = value[:, 128 * t : 128 * t + 128]
    exchange = Exchange(wires, small_sum, small_got)
    plan.add([exchange])
    run_steps(plan.rest())
    for t in range(3):
        small[:, 128 * t : 128 * t + 128] = small_sum[exchange.last, 16 * t : 16 * t + 16, :]


def attention_backward(pairs, cores, kinds, g_after, marks, vecs, wq, wr, wkv, wo, saved, sums, ff_pack):
    rows = g_after.shape[0]
    blocks = rows // BLOCK
    krows = blocks * KPAD
    bits = pairs.bit_length() - 1
    ff_total, total = sum_rows(pairs, cores)
    slots = 15 * (3 + 3 * bits)
    vm, far = pl.BlockSpec(memory_space=pltpu.VMEM), pl.BlockSpec(memory_space=pl.ANY)
    first_n, *saved = saved
    return pl.pallas_call(
        partial(backward_kernel, pairs, cores),
        out_shape=(
            jax.ShapeDtypeStruct((rows, D), f32),
            jax.ShapeDtypeStruct((ff_total, 128), f32),
            jax.ShapeDtypeStruct((cores, total, 128), f32),
            jax.ShapeDtypeStruct((16, 3 * 128), f32),
        ),
        in_specs=[pl.BlockSpec(memory_space=pltpu.SMEM), far] + [vm] * 11 + [far] * 7 + [vm, far],
        out_specs=(vm,) * 4,
        scratch_shapes=[pltpu.VMEM(x.shape, f32) for x in (first_n, *saved)]
        + [
            pltpu.VMEM((D, 1024), bf16),
            pltpu.VMEM((D, 1024), bf16),
            pltpu.VMEM((D, 1024), bf16),
            pltpu.VMEM((D, 1024), bf16),
            pltpu.VMEM((4, 1024, D), bf16),
            pltpu.VMEM((rows, D), f32),
            pltpu.VMEM((rows, D), f32),
            pltpu.VMEM((krows, D), f32),
            pltpu.VMEM((krows, D), f32),
            pltpu.VMEM((4, krows, D), f32),
            pltpu.VMEM((blocks, WIN, 256), f32),
            pltpu.VMEM((3, 256, 128), f32),
            pltpu.VMEM((3, 256, 128), f32),
            pltpu.VMEM((3, 256, 128), f32),
            pltpu.VMEM((8, 8, D), f32),
            pltpu.VMEM((ff_total, 128), f32),
            pltpu.VMEM((ff_total, 128), f32),
            pltpu.VMEM((ff_total, 128), f32),
            pltpu.VMEM((cores, total, 128), f32),
            pltpu.VMEM((total, 128), f32),
            pltpu.VMEM((total, 128), f32),
            pltpu.VMEM((bits + cores, 48, 128), f32),
            pltpu.VMEM((bits + cores, 48, 128), f32),
            pltpu.SemaphoreType.DMA((slots,)),
            pltpu.SemaphoreType.DMA((slots,)),
        ],
        compiler_params=pltpu.CompilerParams(
            collective_id=0 if pairs * cores > 1 else None, has_side_effects=True, vmem_limit_bytes=63 * MIB
        ),
        name="attention_back",
    )(
        kinds,
        first_n,
        g_after,
        marks,
        jnp.asarray(gather_table(), bf16),
        vecs[0],
        vecs[1],
        vecs[4],
        vecs[5],
        wq,
        wr,
        wkv,
        wo,
        *saved,
        sums,
        ff_pack,
    )


def unpack_kernel(grad_from, ff_from, rest_from, small, *refs):
    outs, (d_dw, d_be, d_bd, *lines), refs = refs[:7], refs[7:21], refs[21:]
    grad, ff, rest = refs[:3]
    grad_t, d_we, d_ws, d_wr, d_wkv, d_wq, d_wo = refs[3:10]
    sem = refs[10]
    loads = [
        pltpu.make_async_copy(src, dst, sem.at[i])
        for i, (src, dst) in enumerate(((grad_from, grad), (ff_from, ff), (rest_from, rest)))
    ]
    saves = [pltpu.make_async_copy(src, dst, sem.at[3 + i]) for i, (src, dst) in enumerate(zip(refs[3:10], outs))]
    for load in loads:
        load.start()
    for i, ref in enumerate(lines):
        ref[...] = small[i : i + 1, :D].reshape(-1)
    cores = rest.shape[0]
    part = D // cores
    loads[0].wait()
    grad_t[...] = grad[...].T
    saves[0].start()
    loads[1].wait()
    span = 2 * D + 16
    for t in range(d_we.shape[1] // 128):
        lanes = slice(128 * t, 128 * t + 128)
        d_we[:, lanes] = ff[t * span : t * span + D, :]
        d_ws[:, lanes] = ff[t * span + D : t * span + 2 * D, :]
        d_dw[:, lanes] = ff[t * span + 2 * D : t * span + 2 * D + 9, :]
    saves[1].start()
    saves[2].start()
    for row, ref in ((9, d_be), (10, d_bd)):
        at = 2 * D + row
        parts = [ff[t * span + at : t * span + at + 1, :] for t in range(d_we.shape[1] // 128)]
        ref[...] = jnp.concatenate(parts, 1).reshape(-1)
    loads[2].wait()

    def tile(k):
        return jnp.concatenate([rest[h, k * part : k * part + part, :] for h in range(cores)], 0)

    for t in range(10):
        d_wr[:, 128 * t : 128 * t + 128] = tile(t)
    saves[3].start()
    for t in range(5):
        d_wkv[:, 128 * t : 128 * t + 128] = tile(10 + t)
    saves[4].start()
    mixed = jnp.concatenate([tile(17 + t) for t in range(3)], 1)
    d_wo[...] = jnp.concatenate([tile(15), tile(16), mixed[:, :64]], 1)
    d_wq[...] = mixed[:, 64:]
    saves[5].start()
    saves[6].start()
    for save in saves:
        save.wait()


def unpack(grad, ff, rest, small):
    cores = rest.shape[0]
    rows = grad.shape[0]
    chans = FF // cores
    vm, far = pl.BlockSpec(memory_space=pltpu.VMEM), pl.BlockSpec(memory_space=pl.ANY)
    large = [(D, rows), (D, chans), (D, chans), (D, 4 * D), (D, 2 * D), (D, D), (D, D)]
    shapes = large + [(9, chans), (chans,), (chans,)] + [(D,)] * 11
    held = [x.shape for x in (grad, ff, rest)] + large
    return pl.pallas_call(
        unpack_kernel,
        out_shape=tuple(jax.ShapeDtypeStruct(x, f32) for x in shapes),
        in_specs=[far] * 3 + [vm],
        out_specs=(far,) * 7 + (vm,) * 14,
        scratch_shapes=[pltpu.VMEM(x, f32) for x in held] + [pltpu.SemaphoreType.DMA((10,))],
        compiler_params=pltpu.CompilerParams(vmem_limit_bytes=60 * MIB),
        name="unpack",
    )(grad, ff, rest, small)


def body(
    pairs,
    cores,
    tokens,
    block_kind,
    first_gain,
    first_bias,
    query_weight,
    query_bias,
    reduce_weight,
    reduce_bias,
    reduce_gain,
    reduce_shift,
    keyval_weight,
    value_bias,
    output_weight,
    output_bias,
    second_gain,
    second_shift,
    expand_weight,
    expand_bias,
    depth_weight,
    depth_bias,
    shrink_weight,
    shrink_bias,
    cotangent,
):
    own_taps = jnp.concatenate(
        [depth_weight, expand_bias[None], depth_bias[None], jnp.zeros((5, expand_bias.shape[0]), f32)], 0
    )
    hidden = [lax.all_gather(x, "hidden", axis=0) for x in (expand_weight, shrink_weight.T, own_taps)]
    vecs = (
        first_gain,
        first_bias,
        query_bias,
        reduce_bias,
        reduce_gain,
        reduce_shift,
        value_bias,
        output_bias,
    )
    late = (second_gain, second_shift, shrink_bias)
    weights = (query_weight, reduce_weight.T, keyval_weight, output_weight)
    after, marks, *saved = attention_forward(block_kind, tokens.T, vecs, *weights)
    result_t, g_after, ff_pack, sums = feed_forward(block_kind, after, cotangent.T, late, hidden)
    grad, ff_sum, rest, small = attention_backward(
        pairs, cores, block_kind, g_after, marks, vecs, *weights, saved, sums, ff_pack.reshape(-1, 128)
    )
    outs = unpack(grad, ff_sum, rest, small)
    grad_t, d_we, d_ws, d_wr, d_wkv, d_wq, d_wo, d_dw, d_be, d_bd, *small = outs
    return (
        result_t.T,
        grad_t.T,
        small[0],
        small[1],
        d_wq,
        small[2],
        d_wr.T,
        small[3],
        small[4],
        small[5],
        d_wkv,
        small[6],
        d_wo,
        small[7],
        small[8],
        small[9],
        d_we,
        d_be,
        d_dw,
        d_bd,
        d_ws.T,
        small[10],
    )


def solution(mesh):
    both = P(("dp", "hidden"), None)
    cols = P(None, "hidden")
    chan = P("hidden")
    deep = P("hidden", None)
    whole = P()
    return jax.shard_map(
        partial(body, mesh.shape["dp"], mesh.shape["hidden"]),
        mesh=mesh,
        in_specs=(both,) + (whole,) * 15 + (cols, chan, cols, chan, deep, whole, both),
        out_specs=(both, both) + (whole,) * 14 + (cols, chan, cols, chan, deep, whole),
        check_vma=False,
    )
```
